32 devices in a mesh: grp: 4 (over y, x), col: 8 (over z, core).
Axes of the slice: x: 2, y: 2, z: 4, core: 2. Of those that a mesh axis runs over, the one named last changes fastest.
Arguments:
- state_now: float32 [6, 512, 2048], P(None, 'col', 'grp'), may hold values from -6 to 6
- force_now: float32 [6, 512, 2048], P(None, 'col', 'grp'), may hold values from -6 to 6
- force_old: float32 [6, 512, 2048], P(None, 'col', 'grp'), may hold values from -6 to 6
- velocity: float32 [6, 512, 2048], P(None, 'col', 'grp'), may hold values from -0.125 to 0.125
- second_deriv: float32 [512, 512], replicated, may hold values from -0.25 to 0.25
- eig_basis: float32 [512, 512], replicated, may hold values from -0.25 to 0.25
- eig_inverse: float32 [512, 512], replicated, may hold values from -0.25 to 0.25
- eig_values: float32 [512], replicated, may hold values from 0.1 to 10
- kept_modes: int32 [2, 2048], P(None, 'grp'), may hold values from 0 to 2047
- col_owner: int32 [2048, 1], P('grp'), may hold values from 0 to 7; in each aligned block of 512 rows (0 to 511, 512 to 1023, ...) at most 128 rows name the same one
Outputs:
- state_next: float32 [6, 512, 2048], P(None, 'col', 'grp')
- owned_columns: float32 [6, 512, 4096], P(None, None, ('grp', 'col'))
- mean_emf: float32 [3, 512], P(None, 'col')
The draws below stay inside these ranges and needn't reach their ends.
Inputs may be any that keep to these rules, and one draw needn't show every extreme that they name: `col_owner`: in each group of 512 consecutive columns no owner gets more than 128 columns, and some owner gets exactly 128.
All inputs are finite; a program needn't handle non-finite values.
Results may differ from the reference program's by a relative error of at most 0.000073.
Values sent between devices are 32-bit elements; how exact they have to be, the bound alone decides.
No kernel may reach another device: no remote copies, remote signals or barrier semaphores. Data moves between devices by JAX's collectives and lax.ppermute only.
A program may use at most 128 MiB of HBM per device.

```python
import math
import jax
import jax.numpy as jnp
import numpy as np
from jax import lax

NY = 512
KMAX = 2048
TESTS = 1
COMPS = 6
CAP = 128
M = 512
MTOT = 2048
N_GRP = 4
N_COL = 8


def set_ends(values, rng, least, high):
    longest = values.shape.index(max(values.shape))
    spots = []
    for shift in (0, 1):
        where = [jax.random.randint(jax.random.fold_in(rng, axis), (), 0, length) for axis, length in enumerate(values.shape)]
        where[longest] = (where[longest] + shift) % values.shape[longest]
        spots.append(tuple(where))
    return values.at[spots[0]].set(least).at[spots[1]].set(high)


def block_levels(own_key, extent, cuts, least, top_value):
    level, own = 1.0, jax.random.fold_in(own_key, 6)
    for axis_at, blocks in cuts:
        heights = jnp.exp(jax.random.uniform(jax.random.fold_in(own, axis_at), (blocks,), jnp.float32, least / len(cuts), top_value / len(cuts)))
        level = level * jnp.repeat(heights, extent[axis_at] // blocks).reshape([-1 if axis == axis_at else 1 for axis in range(len(extent))])
    return level


def assign_block(key, own, number, rows, number_of, top, most, skew):
    order = jax.random.permutation(key, number_of)
    crowded, common = load_shares(number_of, rows * top, most, skew, True), load_shares(number_of, rows * top, most, skew, False)
    places = jnp.arange(number_of)

    def named(sizes, offset_by):
        used = int((sizes > 0).sum())
        fixed = max(1, used // 4)
        passed = fixed + (places - fixed + offset_by * (used - fixed)) % max(1, number_of - fixed)
        return jnp.zeros((number_of,), jnp.int32).at[order[jnp.where(places < fixed, places, passed)]].set(jnp.asarray(sizes, jnp.int32))

    sizes = jnp.where(number % 4 == 0, named(crowded, number // 4), named(common, number - number // 4 - 1))
    mixed = jax.random.permutation(jax.random.fold_in(own, 3), number_of)
    donor, sink = mixed[0:number_of // 2 * 2:2], mixed[1:number_of // 2 * 2:2]
    margin = jnp.minimum(sizes[donor] - 1, most - sizes[sink]) // 2
    margin = jnp.where((donor == order[0]) | (sink == order[0]) | (sizes[sink] == 0), 0, jnp.maximum(margin, 0))
    passed = jax.random.randint(jax.random.fold_in(own, 4), (number_of // 2,), 0, 1 << 20) % (margin + 1)
    sizes = sizes.at[donor].add(-passed).at[sink].add(passed)
    members = jnp.searchsorted(jnp.cumsum(sizes), jnp.arange(rows * top), side="right").astype(jnp.int32)
    grid = members.reshape(top, rows).T
    grid = grid[jax.random.permutation(jax.random.fold_in(own, 1), rows)]
    offset_by = jax.random.randint(jax.random.fold_in(own, 2), (rows, 1), 0, top)
    return jnp.take_along_axis(grid, (jnp.arange(top)[None, :] + offset_by) % top, axis=1)


def load_shares(count, total, bound, lean, full):
    loads = [(1 << 20) // math.isqrt(standing ** lean) + 1 for standing in range(1, count + 1)]
    largest = bound if full else min(bound, max(-(-total // count), total * loads[0] // sum(loads)))
    least = 1 if total - largest >= count - 1 else 0
    holding, rest = [largest] + [least] * (count - 1), total - largest - least * (count - 1)
    while rest > 0:
        candidates = [i for i in range(1, count) if holding[i] < largest] or [i for i in range(1, count) if holding[i] < bound]
        mass, remaining = sum([loads[i] for i in candidates]), rest
        for i in candidates:
            more = min(bound - holding[i], max(1, remaining * loads[i] // mass), rest)
            holding[i] = holding[i] + more
            rest = rest - more
    return np.array(holding)


def scatter_about(own_key, shape, spread, most, split=(), kind=jnp.bfloat16):
    values = jax.random.normal(own_key, shape, jnp.float32) * spread
    if len(split) > 0:
        values = block_levels(own_key, shape, split, -0.22, 0.18) * values
    return jnp.clip(values, min=-most, max=most).astype(kind)


def setup_inputs(seed: int = 0) -> dict:
    streams_of = jax.random.split(jax.random.key(seed), 11)
    state_now = scatter_about(streams_of[0], (COMPS, NY, MTOT), 1.0, 6.0, ((1, 8), (2, 4)), jnp.float32)
    force_now = scatter_about(streams_of[1], (COMPS, NY, MTOT), 1.0, 6.0, ((1, 8), (2, 4)), jnp.float32)
    force_old = scatter_about(streams_of[2], (COMPS, NY, MTOT), 1.0, 6.0, ((1, 8), (2, 4)), jnp.float32)
    velocity = scatter_about(streams_of[3], (6, NY, MTOT), ((8 * MTOT) ** -0.5), 0.125, ((1, 8), (2, 4)), jnp.float32)
    second_deriv = scatter_about(streams_of[4], (NY, NY), NY ** -0.5, 0.25, (), jnp.float32)
    eig_basis = scatter_about(streams_of[5], (NY, NY), NY ** -0.5, 0.25, (), jnp.float32)
    eig_inverse = scatter_about(streams_of[6], (NY, NY), NY ** -0.5, 0.25, (), jnp.float32)
    eig_values = jnp.clip(jnp.exp(jax.random.uniform(streams_of[7], (NY,), jnp.float32, math.log(0.1), math.log(10.0))), 0.1, 10.0)
    kept_modes = set_ends(jax.random.randint(streams_of[8], (2, MTOT), 0, KMAX), jax.random.fold_in(streams_of[8], 1), 0, KMAX - 1).astype(jnp.int32)
    col_owner_keys = jax.random.split(jax.random.fold_in(streams_of[9], 1), MTOT // M)
    col_owner_turns = jax.random.permutation(jax.random.fold_in(streams_of[9], 3), MTOT // M)
    col_owner = jax.vmap(lambda own, number: assign_block(jax.random.fold_in(streams_of[9], 2), own, number, M, N_COL, 1, CAP, 2))(col_owner_keys, col_owner_turns).reshape((MTOT, 1))
    return dict(state_now=state_now, force_now=force_now, force_old=force_old, velocity=velocity, second_deriv=second_deriv, eig_basis=eig_basis, eig_inverse=eig_inverse, eig_values=eig_values, kept_modes=kept_modes, col_owner=col_owner)


TIME_STEP = 2.0
RK_ALPHA = -3.0 / 40.0
RK_BETA = 5.0 / 24.0
RK_GAMMA = 5.0 / 12.0
RK_ZETA = -17.0 / 60.0
WAVE_SCALE = 8.0


def wave_squares(kept_modes):
    wave_x = kept_modes[0].astype(jnp.float32)
    wave_z = kept_modes[1].astype(jnp.float32)
    return (wave_x * wave_x + wave_z * wave_z) * (WAVE_SCALE / (KMAX * KMAX))


def emf_of(velocity, state, kept_modes):
    weight = jnp.where(kept_modes[0] > 0, 2.0, 1.0).astype(jnp.float32)
    speed = velocity.reshape(3, 2, velocity.shape[1], velocity.shape[2])
    parts = state.reshape(TESTS, 3, 2, state.shape[1], state.shape[2])
    pairs = jnp.einsum("jrym,fkrym,m->fjky", speed, parts, weight, precision=lax.Precision.HIGHEST)
    result = jnp.stack([pairs[:, 1, 2] - pairs[:, 2, 1], pairs[:, 2, 0] - pairs[:, 0, 2], pairs[:, 0, 1] - pairs[:, 1, 0]], axis=1)
    return result.reshape(3 * TESTS, state.shape[1])


def reference(state_now, force_now, force_old, velocity, second_deriv, eig_basis, eig_inverse, eig_values, kept_modes, col_owner):
    ksq = wave_squares(kept_modes)

    def grouped(array):
        return jnp.moveaxis(array.reshape(array.shape[0], NY, N_GRP, M), 2, 0)

    def per_group(items):
        state, f_now, f_old, wave = items
        forcing = RK_GAMMA * f_now + RK_ZETA * f_old
        lap_term = jnp.einsum("yz,czm->cym", second_deriv, state, precision=lax.Precision.HIGHEST) - wave[None, None, :] * state
        rhs_term = state + TIME_STEP * (RK_ALPHA * lap_term + forcing)
        project = jnp.einsum("yz,czm->cym", eig_inverse, rhs_term, precision=lax.Precision.HIGHEST)
        project = project / (1.0 + TIME_STEP * RK_BETA * (eig_values[:, None] + wave[None, :]))
        return jnp.einsum("yz,czm->cym", eig_basis, project, precision=lax.Precision.HIGHEST)

    solved = lax.map(per_group, (grouped(state_now), grouped(force_now), grouped(force_old), ksq.reshape(N_GRP, M)))
    state_next = jnp.moveaxis(solved, 0, 2).reshape(COMPS, NY, MTOT)
    owners = col_owner[:, 0].reshape(N_GRP, M)
    onehot = (owners[:, :, None] == jnp.arange(N_COL, dtype=jnp.int32)[None, None, :]).astype(jnp.int32)
    ranks = jnp.sum(jnp.cumsum(onehot, axis=1) * onehot, axis=2) - 1
    group_base = (jnp.arange(N_GRP, dtype=jnp.int32) * (N_COL * CAP))[:, None]
    slots = (group_base + owners * CAP + ranks).reshape(MTOT).astype(jnp.int32)
    owned_columns = jnp.zeros((COMPS, NY, N_GRP * N_COL * CAP), jnp.float32).at[:, :, slots].set(state_next)
    mean_emf = emf_of(velocity, state_next, kept_modes)
    return state_next, owned_columns, mean_emf
```

```python
import functools

import jax
import jax.numpy as jnp
from jax import lax
from jax.experimental import pallas as pl
from jax.experimental.pallas import tpu as pltpu
from jax.sharding import PartitionSpec as P

KMAX = 2048
TIME_STEP = 2.0
RK_ALPHA = -3.0 / 40.0
RK_BETA = 5.0 / 24.0
RK_GAMMA = 5.0 / 12.0
RK_ZETA = -17.0 / 60.0
WAVE_SCALE = 8.0
VMEM_LIMIT = 56 * 1024 * 1024
GROUPS = 3
LANES = 128

F32 = jnp.float32
BF16 = jnp.bfloat16


def call(body, out_shape, in_specs, out_specs, flops, nbytes, scratch=(), aliases=None):
    return pl.pallas_call(
        body,
        grid=(1,),
        out_shape=out_shape,
        in_specs=in_specs,
        out_specs=out_specs,
        scratch_shapes=list(scratch),
        input_output_aliases=aliases or {},
        cost_estimate=pl.CostEstimate(flops=flops, bytes_accessed=nbytes, transcendentals=0),
        compiler_params=pltpu.CompilerParams(vmem_limit_bytes=VMEM_LIMIT),
    )


def whole(shape):
    return pl.BlockSpec(shape, lambda i: (0,) * len(shape))


def part(shape, at):
    return pl.BlockSpec(shape, lambda i: (at,) + (0,) * (len(shape) - 1))


def scalar():
    return pl.BlockSpec(memory_space=pltpu.SMEM)


def untouched():
    return pl.BlockSpec(memory_space=pl.ANY)


def shaped(shape, dtype=F32):
    return jax.ShapeDtypeStruct(shape, dtype)


def three_parts(x):
    high = x.astype(BF16)
    rest = x - high.astype(F32)
    middle = rest.astype(BF16)
    low = (rest - middle.astype(F32)).astype(BF16)
    return jnp.concatenate([high, middle, low], axis=0)


def sum_parts(x):
    rows = x.shape[0] // 3
    return x[:rows] + x[rows : 2 * rows] + x[2 * rows :]


def two_parts(x):
    high = x.astype(BF16)
    low = (x - high.astype(F32)).astype(BF16)
    return high, low


def selector(places, rows):
    columns = places.shape[1]
    return (lax.broadcasted_iota(jnp.int32, (rows, columns), 0) == places).astype(F32).astype(BF16)


def wave_row(modes):
    wave_x = modes[0:1, :].astype(F32)
    wave_z = modes[1:2, :].astype(F32)
    return (wave_x * wave_x + wave_z * wave_z) * (WAVE_SCALE / (KMAX * KMAX))


NT = (((1,), (1,)), ((), ()))


def plan_kernel(devices, me_ref, owner_ref, modes_ref, info_ref, wave_ref):
    columns = owner_ref.shape[1]
    share = columns // devices
    rows = -(-devices // 8) * 8
    me = me_ref[0]
    owner = owner_ref[...]
    owned = (lax.broadcasted_iota(jnp.int32, (rows, columns), 0) == owner).astype(F32)
    before = (
        lax.broadcasted_iota(jnp.int32, (LANES, LANES), 0) < lax.broadcasted_iota(jnp.int32, (LANES, LANES), 1)
    ).astype(F32)
    carry = jnp.zeros((rows, 1), F32)
    earlier = []
    for at in range(columns // LANES):
        block = owned[:, at * LANES : (at + 1) * LANES]
        earlier.append(jnp.dot(block, before, preferred_element_type=F32) + carry)
        carry = carry + jnp.sum(block, axis=1, keepdims=True)
    counts = carry
    rank = jnp.sum(owned * jnp.concatenate(earlier, axis=1), axis=0, keepdims=True)
    surplus = jnp.maximum(counts - share, 0.0)
    lower = (lax.broadcasted_iota(jnp.int32, (rows, columns), 0) < owner).astype(F32)
    number = jnp.sum(lower * surplus, axis=0, keepdims=True) + (rank - share)
    free = share - jnp.minimum(counts, share)
    start = jnp.zeros((1, 1), F32)
    solver = owner
    slot = rank
    beyond = rank >= share
    for device in range(devices):
        here = free[device : device + 1, :]
        inside = beyond & (number >= start) & (number < start + here)
        solver = jnp.where(inside, device, solver)
        slot = jnp.where(inside, share - here + number - start, slot)
        start = start + here
    place = (solver ^ me) * share + slot.astype(jnp.int32)
    extra = jnp.where(beyond, (owner ^ me) * share + rank.astype(jnp.int32) - share, -1)
    mine = jnp.sum((owner == me).astype(F32), axis=1, keepdims=True).astype(jnp.int32)
    info_ref[...] = jnp.concatenate(
        [place, extra, jnp.broadcast_to(mine, (1, columns)), jnp.zeros((5, columns), jnp.int32)], axis=0
    )
    wave = jnp.broadcast_to(wave_row(modes_ref[...]), (16, columns))
    picked = sum_parts(
        lax.dot_general(three_parts(wave), selector(place, share), NT, preferred_element_type=F32)
    )
    wave_ref[...] = jnp.concatenate([picked, picked], axis=1)[:8]


def pack_kernel(devices, info_ref, modes_ref, state_ref, now_ref, old_ref, *out_refs):
    comps, points, columns = state_ref.shape
    share = columns // devices
    wave = wave_row(modes_ref[...]).reshape(1, 1, columns)
    state = state_ref[...]
    forcing = RK_GAMMA * now_ref[...] + RK_ZETA * old_ref[...]
    local = state + TIME_STEP * (forcing - RK_ALPHA * (wave * state))
    rows = comps * points
    both = jnp.concatenate([state.reshape(rows, columns), local.reshape(rows, columns)], axis=0)
    placed = sum_parts(
        lax.dot_general(
            three_parts(both), selector(info_ref[0:1, :], columns), NT, preferred_element_type=F32
        )
    )
    for step, out in enumerate(out_refs):
        taken = placed[:, step * share : (step + 1) * share]
        for kind in range(2):
            for pair in range(comps // 2):
                real = (kind * comps + 2 * pair) * points
                imag = real + points
                out[kind, pair] = jnp.concatenate(
                    [taken[real : real + points], taken[imag : imag + points]], axis=1
                )


def operators_kernel(deriv_ref, inverse_ref, basis_ref, values_ref, deriv_out, inverse_out, basis_out, values_out):
    for source, target in ((deriv_ref, deriv_out), (inverse_ref, inverse_out), (basis_ref, basis_out)):
        high, low = two_parts(source[...])
        target[...] = jnp.concatenate([high, high, low], axis=1)
    lanes = values_out.shape[1]
    values_out[...] = jnp.transpose(jnp.broadcast_to(values_ref[...], (lanes, values_ref.shape[1])))


def apply(operator, x):
    high, low = two_parts(x)
    return jnp.dot(operator, jnp.concatenate([high, low, high], axis=0), preferred_element_type=F32)


def solve_kernel(devices, me_ref, wave_ref, values_ref, deriv_ref, inverse_ref, basis_ref, *refs):
    in_refs, refs = refs[:devices], refs[devices:]
    out_refs, (solved_ref, state, local, after) = refs[:devices], refs[devices:]
    me = me_ref[0]
    _, pairs, points, lanes = in_refs[0].shape
    for step, block in enumerate(in_refs):
        rows = pl.ds(pl.multiple_of((me ^ step) * points, points), points)
        for pair in range(pairs):
            state[rows, pair * lanes : (pair + 1) * lanes] = block[0, pair]
            local[rows, pair * lanes : (pair + 1) * lanes] = block[1, pair]
    rhs = local[...] + (TIME_STEP * RK_ALPHA) * apply(deriv_ref[...], state[...])
    project = apply(inverse_ref[...], rhs)
    damping = 1.0 + TIME_STEP * RK_BETA * (values_ref[...] + wave_ref[0:1, :])
    project = project / jnp.concatenate([damping] * pairs, axis=1)
    after[...] = apply(basis_ref[...], project)
    for pair in range(pairs):
        solved_ref[pair] = after[:, pair * lanes : (pair + 1) * lanes]
    for step, block in enumerate(out_refs):
        rows = pl.ds(pl.multiple_of((me ^ step) * points, points), points)
        for pair in range(pairs):
            block[pair] = after[rows, pair * lanes : (pair + 1) * lanes]


def unpack_kernel(devices, chunk, first, info_ref, modes_ref, velocity_ref, *refs):
    in_refs, refs = refs[:devices], refs[devices:]
    if not first:
        (_, emf_in), refs = refs[:2], refs[2:]
    (state_ref, emf_ref), out_refs = refs[:2], refs[2:]
    pairs, points, lanes = in_refs[0].shape
    share = lanes // 2
    columns = devices * share
    got = []
    for pair in range(pairs):
        for half in range(2):
            got.append(
                jnp.concatenate(
                    [block[pair][:, half * share : (half + 1) * share] for block in in_refs], axis=1
                )
            )
    got = jnp.concatenate(got, axis=0)
    state = sum_parts(
        jnp.dot(three_parts(got), selector(info_ref[0:1, :], columns), preferred_element_type=F32)
    )
    state_ref[...] = state.reshape(2 * pairs, points, columns)
    extra = sum_parts(
        lax.dot_general(
            three_parts(state), selector(info_ref[1:2, :], columns), NT, preferred_element_type=F32
        )
    )
    for step, out in enumerate(out_refs):
        taken = extra[:, step * share : (step + 1) * share]
        for pair in range(pairs):
            real = 2 * pair * points
            imag = real + points
            out[pair] = jnp.concatenate([taken[real : real + points], taken[imag : imag + points]], axis=1)
    weight = jnp.where(modes_ref[0:1, :] > 0, 2.0, 1.0).astype(F32)
    totals = [jnp.zeros((points, columns), F32)] * 3
    for pair in range(pairs):
        field = chunk * pairs + pair
        real = weight * state[2 * pair * points : (2 * pair + 1) * points]
        imag = weight * state[(2 * pair + 1) * points : (2 * pair + 2) * points]
        for sign, i, j in ((1.0, (field + 1) % 3, (field + 2) % 3), (-1.0, (field + 2) % 3, (field + 1) % 3)):
            totals[i] = totals[i] + sign * (velocity_ref[2 * j] * real + velocity_ref[2 * j + 1] * imag)
    rows = []
    for total in totals:
        folded = total[:, :LANES]
        for at in range(1, columns // LANES):
            folded = folded + total[:, at * LANES : (at + 1) * LANES]
        rows.append(jnp.sum(jnp.transpose(folded), axis=0, keepdims=True))
    rows = jnp.concatenate(rows, axis=0)
    emf_ref[...] = rows if first else rows + emf_in[...]


def assemble_kernel(devices, first, me_ref, info_ref, solved_ref, *refs):
    in_refs, refs = refs[:devices], refs[devices:]
    if not first:
        refs = refs[1:]
    (out_ref,) = refs
    me = me_ref[0]
    pairs, points, lanes = in_refs[0].shape
    share = lanes // 2
    depth = solved_ref.shape[1]
    used = lax.broadcasted_iota(jnp.int32, (depth, share), 1) < info_ref[2:3, :share]
    for pair in range(pairs):
        for half in range(2):
            kept = jnp.where(used, solved_ref[pair][:, half * share : (half + 1) * share], 0.0)
            out_ref[2 * pair + half, :, :share] = kept
            for step, block in enumerate(in_refs):
                rows = pl.ds(pl.multiple_of((me ^ step) * points, points), points)
                out_ref[2 * pair + half, rows, share:] = block[pair][:, half * share : (half + 1) * share]


def exchange(blocks):
    devices = len(blocks)
    return [blocks[0]] + [
        lax.ppermute(blocks[step], "col", [(i, i ^ step) for i in range(devices)]) for step in range(1, devices)
    ]


def sum_over_groups(value):
    groups = lax.axis_size("grp")
    terms = [value] + [
        lax.ppermute(value, "grp", [(i, i ^ step) for i in range(groups)]) for step in range(1, groups)
    ]
    while len(terms) > 1:
        terms = [terms[at] + terms[at + 1] for at in range(0, len(terms), 2)]
    return terms[0]


def on_device(
    state_now,
    force_now,
    force_old,
    velocity,
    second_deriv,
    eig_basis,
    eig_inverse,
    eig_values,
    kept_modes,
    col_owner,
):
    comps, points, columns = state_now.shape
    devices = lax.axis_size("col")
    depth = devices * points
    share = columns // devices
    lanes = 2 * share
    pairs = GROUPS
    chunks = comps // (2 * pairs)
    me = lax.axis_index("col").astype(jnp.int32).reshape(1)
    owner = col_owner.reshape(1, columns)

    info, wave = call(
        functools.partial(plan_kernel, devices),
        [shaped((8, columns), jnp.int32), shaped((8, lanes))],
        [scalar(), whole((1, columns)), whole((2, columns))],
        [whole((8, columns)), whole((8, lanes))],
        1000000,
        100000,
    )(me, owner, kept_modes)

    field = (2 * pairs, points, columns)
    sent = (2, pairs, points, lanes)
    back = (pairs, points, lanes)
    moved = 4 * 2 * pairs * points * columns

    forward = []
    for chunk in range(chunks):
        forward.append(
            exchange(
                call(
                    functools.partial(pack_kernel, devices),
                    [shaped(sent)] * devices,
                    [whole((8, columns)), whole((2, columns))] + [part(field, chunk)] * 3,
                    [whole(sent)] * devices,
                    12 * 2 * pairs * points * columns * columns,
                    5 * moved,
                )(info, kept_modes, state_now, force_now, force_old)
            )
        )

    operator = shaped((depth, 3 * depth), BF16)
    operators = call(
        operators_kernel,
        [operator, operator, operator, shaped((depth, lanes))],
        [whole((depth, depth))] * 3 + [whole((1, depth))],
        [whole((depth, 3 * depth))] * 3 + [whole((depth, lanes))],
        1000000,
        30 * depth * depth,
    )(second_deriv, eig_inverse, eig_basis, eig_values.reshape(1, depth))
    values = operators[3]

    solved, returned = [], []
    for chunk in range(chunks):
        width = pairs * lanes
        outs = call(
            functools.partial(solve_kernel, devices),
            [shaped(back)] * devices + [shaped((pairs, depth, lanes))],
            [scalar(), whole((8, lanes)), whole((depth, lanes))]
            + [whole((depth, 3 * depth))] * 3
            + [whole(sent)] * devices,
            [whole(back)] * devices + [whole((pairs, depth, lanes))],
            18 * depth * depth * width,
            18 * depth * depth + 16 * depth * width,
            [pltpu.VMEM((depth, width), F32)] * 3,
        )(me, wave, values, *operators[:3], *forward[chunk])
        solved.append(outs[devices])
        returned.append(exchange(outs[:devices]))

    state_next, emf, extra = None, None, []
    for chunk in range(chunks):
        first = chunk == 0
        outs = call(
            functools.partial(unpack_kernel, devices, chunk, first),
            [shaped(state_now.shape), shaped((3, points))] + [shaped(back)] * devices,
            [whole((8, columns)), whole((2, columns)), whole(velocity.shape)]
            + [whole(back)] * devices
            + ([] if first else [untouched(), whole((3, points))]),
            [part(field, chunk), whole((3, points))] + [whole(back)] * devices,
            12 * 2 * pairs * points * columns * columns,
            6 * moved,
            aliases={} if first else {3 + devices: 0},
        )(info, kept_modes, velocity, *returned[chunk], *([] if first else [state_next, emf]))
        state_next, emf = outs[:2]
        extra.append(exchange(outs[2:]))
    mean_emf = sum_over_groups(emf)

    owned = None
    for chunk in range(chunks):
        first = chunk == 0
        owned = call(
            functools.partial(assemble_kernel, devices, first),
            shaped((comps, depth, lanes)),
            [scalar(), whole((8, columns)), whole((pairs, depth, lanes))]
            + [whole(back)] * devices
            + ([] if first else [untouched()]),
            part((2 * pairs, depth, lanes), chunk),
            1000000,
            16 * pairs * depth * lanes,
            aliases={} if first else {3 + devices: 0},
        )(me, info, solved[chunk], *extra[chunk], *([] if first else [owned]))
    return (state_next, owned, mean_emf)


def solution(mesh):
    return jax.shard_map(
        on_device,
        mesh=mesh,
        in_specs=(
            P(None, "col", "grp"),
            P(None, "col", "grp"),
            P(None, "col", "grp"),
            P(None, "col", "grp"),
            P(),
            P(),
            P(),
            P(),
            P(None, "grp"),
            P("grp", None),
        ),
        out_specs=(P(None, "col", "grp"), P(None, None, ("grp", "col")), P(None, "col")),
        check_vma=False,
    )
```

```python
import functools

import jax
import jax.numpy as jnp
from jax import lax
from jax.experimental import pallas as pl
from jax.experimental.pallas import tpu as pltpu
from jax.sharding import PartitionSpec as P

KMAX = 2048
TIME_STEP = 2.0
RK_ALPHA = -3.0 / 40.0
RK_BETA = 5.0 / 24.0
RK_GAMMA = 5.0 / 12.0
RK_ZETA = -17.0 / 60.0
WAVE_SCALE = 8.0
VMEM_LIMIT = 56 * 1024 * 1024
GROUPS = 3
LANES = 128

F32 = jnp.float32
BF16 = jnp.bfloat16


def call(body, out_shape, in_specs, out_specs, flops, nbytes, scratch=(), aliases=None):
    return pl.pallas_call(
        body,
        grid=(1,),
        out_shape=out_shape,
        in_specs=in_specs,
        out_specs=out_specs,
        scratch_shapes=list(scratch),
        input_output_aliases=aliases or {},
        cost_estimate=pl.CostEstimate(flops=flops, bytes_accessed=nbytes, transcendentals=0),
        compiler_params=pltpu.CompilerParams(vmem_limit_bytes=VMEM_LIMIT),
    )


def whole(shape):
    return pl.BlockSpec(shape, lambda i: (0,) * len(shape))


def part(shape, at):
    return pl.BlockSpec(shape, lambda i: (at,) + (0,) * (len(shape) - 1))


def scalar():
    return pl.BlockSpec(memory_space=pltpu.SMEM)


def untouched():
    return pl.BlockSpec(memory_space=pl.ANY)


def shaped(shape, dtype=F32):
    return jax.ShapeDtypeStruct(shape, dtype)


def three_parts(x):
    high = x.astype(BF16)
    rest = x - high.astype(F32)
    middle = rest.astype(BF16)
    low = (rest - middle.astype(F32)).astype(BF16)
    return jnp.concatenate([high, middle, low], axis=0)


def sum_parts(x):
    rows = x.shape[0] // 3
    return x[:rows] + x[rows : 2 * rows] + x[2 * rows :]


def two_parts(x):
    high = x.astype(BF16)
    low = (x - high.astype(F32)).astype(BF16)
    return high, low


def selector(places, rows):
    columns = places.shape[1]
    return (lax.broadcasted_iota(jnp.int32, (rows, columns), 0) == places).astype(F32).astype(BF16)


def wave_row(modes):
    wave_x = modes[0:1, :].astype(F32)
    wave_z = modes[1:2, :].astype(F32)
    return (wave_x * wave_x + wave_z * wave_z) * (WAVE_SCALE / (KMAX * KMAX))


NT = (((1,), (1,)), ((), ()))


def plan_kernel(devices, me_ref, owner_ref, modes_ref, info_ref, wave_ref):
    columns = owner_ref.shape[1]
    share = columns // devices
    rows = -(-devices // 8) * 8
    me = me_ref[0]
    owner = owner_ref[...]
    owned = (lax.broadcasted_iota(jnp.int32, (rows, columns), 0) == owner).astype(F32)
    before = (
        lax.broadcasted_iota(jnp.int32, (LANES, LANES), 0) < lax.broadcasted_iota(jnp.int32, (LANES, LANES), 1)
    ).astype(F32)
    carry = jnp.zeros((rows, 1), F32)
    earlier = []
    for at in range(columns // LANES):
        block = owned[:, at * LANES : (at + 1) * LANES]
        earlier.append(jnp.dot(block, before, preferred_element_type=F32) + carry)
        carry = carry + jnp.sum(block, axis=1, keepdims=True)
    counts = carry
    rank = jnp.sum(owned * jnp.concatenate(earlier, axis=1), axis=0, keepdims=True)
    surplus = jnp.maximum(counts - share, 0.0)
    lower = (lax.broadcasted_iota(jnp.int32, (rows, columns), 0) < owner).astype(F32)
    number = jnp.sum(lower * surplus, axis=0, keepdims=True) + (rank - share)
    free = share - jnp.minimum(counts, share)
    start = jnp.zeros((1, 1), F32)
    solver = owner
    slot = rank
    beyond = rank >= share
    for device in range(devices):
        here = free[device : device + 1, :]
        inside = beyond & (number >= start) & (number < start + here)
        solver = jnp.where(inside, device, solver)
        slot = jnp.where(inside, share - here + number - start, slot)
        start = start + here
    place = (solver ^ me) * share + slot.astype(jnp.int32)
    extra = jnp.where(beyond, (owner ^ me) * share + rank.astype(jnp.int32) - share, -1)
    mine = jnp.sum((owner == me).astype(F32), axis=1, keepdims=True).astype(jnp.int32)
    info_ref[...] = jnp.concatenate(
        [place, extra, jnp.broadcast_to(mine, (1, columns)), jnp.zeros((5, columns), jnp.int32)], axis=0
    )
    wave = jnp.broadcast_to(wave_row(modes_ref[...]), (16, columns))
    picked = sum_parts(
        lax.dot_general(three_parts(wave), selector(place, share), NT, preferred_element_type=F32)
    )
    wave_ref[...] = jnp.concatenate([picked, picked], axis=1)[:8]


def pack_kernel(devices, info_ref, modes_ref, state_ref, now_ref, old_ref, *out_refs):
    comps, points, columns = state_ref.shape
    share = columns // devices
    wave = wave_row(modes_ref[...]).reshape(1, 1, columns)
    state = state_ref[...]
    forcing = RK_GAMMA * now_ref[...] + RK_ZETA * old_ref[...]
    local = state + TIME_STEP * (forcing - RK_ALPHA * (wave * state))
    rows = comps * points
    both = jnp.concatenate([state.reshape(rows, columns), local.reshape(rows, columns)], axis=0)
    placed = sum_parts(
        lax.dot_general(
            three_parts(both), selector(info_ref[0:1, :], columns), NT, preferred_element_type=F32
        )
    )
    for step, out in enumerate(out_refs):
        taken = placed[:, step * share : (step + 1) * share]
        for kind in range(2):
            for pair in range(comps // 2):
                real = (kind * comps + 2 * pair) * points
                imag = real + points
                out[kind, pair] = jnp.concatenate(
                    [taken[real : real + points], taken[imag : imag + points]], axis=1
                )


def operators_kernel(deriv_ref, inverse_ref, basis_ref, values_ref, deriv_out, inverse_out, basis_out, values_out):
    for source, target in ((deriv_ref, deriv_out), (inverse_ref, inverse_out), (basis_ref, basis_out)):
        high, low = two_parts(source[...])
        target[...] = jnp.concatenate([high, high, low], axis=1)
    lanes = values_out.shape[1]
    values_out[...] = jnp.transpose(jnp.broadcast_to(values_ref[...], (lanes, values_ref.shape[1])))


def apply(operator, x):
    high, low = two_parts(x)
    return jnp.dot(operator, jnp.concatenate([high, low, high], axis=0), preferred_element_type=F32)


def solve_kernel(devices, me_ref, wave_ref, values_ref, deriv_ref, inverse_ref, basis_ref, *refs):
    in_refs, refs = refs[:devices], refs[devices:]
    out_refs, (solved_ref, state, local, after) = refs[:devices], refs[devices:]
    me = me_ref[0]
    _, pairs, points, lanes = in_refs[0].shape
    for step, block in enumerate(in_refs):
        rows = pl.ds(pl.multiple_of((me ^ step) * points, points), points)
        for pair in range(pairs):
            state[rows, pair * lanes : (pair + 1) * lanes] = block[0, pair]
            local[rows, pair * lanes : (pair + 1) * lanes] = block[1, pair]
    rhs = local[...] + (TIME_STEP * RK_ALPHA) * apply(deriv_ref[...], state[...])
    project = apply(inverse_ref[...], rhs)
    damping = 1.0 + TIME_STEP * RK_BETA * (values_ref[...] + wave_ref[0:1, :])
    project = project / jnp.concatenate([damping] * pairs, axis=1)
    after[...] = apply(basis_ref[...], project)
    for pair in range(pairs):
        solved_ref[pair] = after[:, pair * lanes : (pair + 1) * lanes]
    for step, block in enumerate(out_refs):
        rows = pl.ds(pl.multiple_of((me ^ step) * points, points), points)
        for pair in range(pairs):
            block[pair] = after[rows, pair * lanes : (pair + 1) * lanes]


def unpack_kernel(devices, chunk, first, info_ref, modes_ref, velocity_ref, *refs):
    in_refs, refs = refs[:devices], refs[devices:]
    if not first:
        (_, emf_in), refs = refs[:2], refs[2:]
    (state_ref, emf_ref), out_refs = refs[:2], refs[2:]
    pairs, points, lanes = in_refs[0].shape
    share = lanes // 2
    columns = devices * share
    got = []
    for pair in range(pairs):
        for half in range(2):
            got.append(
                jnp.concatenate(
                    [block[pair][:, half * share : (half + 1) * share] for block in in_refs], axis=1
                )
            )
    got = jnp.concatenate(got, axis=0)
    state = sum_parts(
        jnp.dot(three_parts(got), selector(info_ref[0:1, :], columns), preferred_element_type=F32)
    )
    state_ref[...] = state.reshape(2 * pairs, points, columns)
    extra = sum_parts(
        lax.dot_general(
            three_parts(state), selector(info_ref[1:2, :], columns), NT, preferred_element_type=F32
        )
    )
    for step, out in enumerate(out_refs):
        taken = extra[:, step * share : (step + 1) * share]
        for pair in range(pairs):
            real = 2 * pair * points
            imag = real + points
            out[pair] = jnp.concatenate([taken[real : real + points], taken[imag : imag + points]], axis=1)
    weight = jnp.where(modes_ref[0:1, :] > 0, 2.0, 1.0).astype(F32)
    totals = [jnp.zeros((points, columns), F32)] * 3
    for pair in range(pairs):
        field = chunk * pairs + pair
        real = weight * state[2 * pair * points : (2 * pair + 1) * points]
        imag = weight * state[(2 * pair + 1) * points : (2 * pair + 2) * points]
        for sign, i, j in ((1.0, (field + 1) % 3, (field + 2) % 3), (-1.0, (field + 2) % 3, (field + 1) % 3)):
            totals[i] = totals[i] + sign * (velocity_ref[2 * j] * real + velocity_ref[2 * j + 1] * imag)
    rows = []
    for total in totals:
        folded = total[:, :LANES]
        for at in range(1, columns // LANES):
            folded = folded + total[:, at * LANES : (at + 1) * LANES]
        rows.append(jnp.sum(jnp.transpose(folded), axis=0, keepdims=True))
    rows = jnp.concatenate(rows, axis=0)
    emf_ref[...] = rows if first else rows + emf_in[...]


def assemble_kernel(devices, first, me_ref, info_ref, solved_ref, *refs):
    in_refs, refs = refs[:devices], refs[devices:]
    if not first:
        refs = refs[1:]
    (out_ref,) = refs
    me = me_ref[0]
    pairs, points, lanes = in_refs[0].shape
    share = lanes // 2
    depth = solved_ref.shape[1]
    used = lax.broadcasted_iota(jnp.int32, (depth, share), 1) < info_ref[2:3, :share]
    for pair in range(pairs):
        for half in range(2):
            kept = jnp.where(used, solved_ref[pair][:, half * share : (half + 1) * share], 0.0)
            out_ref[2 * pair + half, :, :share] = kept
            for step, block in enumerate(in_refs):
                rows = pl.ds(pl.multiple_of((me ^ step) * points, points), points)
                out_ref[2 * pair + half, rows, share:] = block[pair][:, half * share : (half + 1) * share]


def exchange(blocks):
    devices = len(blocks)
    arrived = list(blocks)
    for step in crossing_first(devices):
        arrived[step] = lax.ppermute(blocks[step], "col", [(i, i ^ step) for i in range(devices)])
    return arrived


def crossing_first(devices):
    return sorted(range(1, devices), key=lambda step: -((step.bit_length() << 16) + (step >> 1 << 1)))


def sum_over_groups(value):
    groups = lax.axis_size("grp")
    terms = [value] + [
        lax.ppermute(value, "grp", [(i, i ^ step) for i in range(groups)]) for step in range(1, groups)
    ]
    while len(terms) > 1:
        terms = [terms[at] + terms[at + 1] for at in range(0, len(terms), 2)]
    return terms[0]


def on_device(
    state_now,
    force_now,
    force_old,
    velocity,
    second_deriv,
    eig_basis,
    eig_inverse,
    eig_values,
    kept_modes,
    col_owner,
):
    comps, points, columns = state_now.shape
    devices = lax.axis_size("col")
    depth = devices * points
    share = columns // devices
    lanes = 2 * share
    pairs = GROUPS
    chunks = comps // (2 * pairs)
    me = lax.axis_index("col").astype(jnp.int32).reshape(1)
    owner = col_owner.reshape(1, columns)

    info, wave = call(
        functools.partial(plan_kernel, devices),
        [shaped((8, columns), jnp.int32), shaped((8, lanes))],
        [scalar(), whole((1, columns)), whole((2, columns))],
        [whole((8, columns)), whole((8, lanes))],
        1000000,
        100000,
    )(me, owner, kept_modes)

    field = (2 * pairs, points, columns)
    sent = (2, pairs, points, lanes)
    back = (pairs, points, lanes)
    moved = 4 * 2 * pairs * points * columns

    forward = []
    for chunk in range(chunks):
        forward.append(
            exchange(
                call(
                    functools.partial(pack_kernel, devices),
                    [shaped(sent)] * devices,
                    [whole((8, columns)), whole((2, columns))] + [part(field, chunk)] * 3,
                    [whole(sent)] * devices,
                    12 * 2 * pairs * points * columns * columns,
                    5 * moved,
                )(info, kept_modes, state_now, force_now, force_old)
            )
        )

    operator = shaped((depth, 3 * depth), BF16)
    operators = call(
        operators_kernel,
        [operator, operator, operator, shaped((depth, lanes))],
        [whole((depth, depth))] * 3 + [whole((1, depth))],
        [whole((depth, 3 * depth))] * 3 + [whole((depth, lanes))],
        1000000,
        30 * depth * depth,
    )(second_deriv, eig_inverse, eig_basis, eig_values.reshape(1, depth))
    values = operators[3]

    solved, returned = [], []
    for chunk in range(chunks):
        width = pairs * lanes
        outs = call(
            functools.partial(solve_kernel, devices),
            [shaped(back)] * devices + [shaped((pairs, depth, lanes))],
            [scalar(), whole((8, lanes)), whole((depth, lanes))]
            + [whole((depth, 3 * depth))] * 3
            + [whole(sent)] * devices,
            [whole(back)] * devices + [whole((pairs, depth, lanes))],
            18 * depth * depth * width,
            18 * depth * depth + 16 * depth * width,
            [pltpu.VMEM((depth, width), F32)] * 3,
        )(me, wave, values, *operators[:3], *forward[chunk])
        solved.append(outs[devices])
        returned.append(exchange(outs[:devices]))

    state_next, emf, extra = None, None, []
    for chunk in range(chunks):
        first = chunk == 0
        outs = call(
            functools.partial(unpack_kernel, devices, chunk, first),
            [shaped(state_now.shape), shaped((3, points))] + [shaped(back)] * devices,
            [whole((8, columns)), whole((2, columns)), whole(velocity.shape)]
            + [whole(back)] * devices
            + ([] if first else [untouched(), whole((3, points))]),
            [part(field, chunk), whole((3, points))] + [whole(back)] * devices,
            12 * 2 * pairs * points * columns * columns,
            6 * moved,
            aliases={} if first else {3 + devices: 0},
        )(info, kept_modes, velocity, *returned[chunk], *([] if first else [state_next, emf]))
        state_next, emf = outs[:2]
        extra.append(exchange(outs[2:]))
    mean_emf = sum_over_groups(emf)

    owned = None
    for chunk in range(chunks):
        first = chunk == 0
        owned = call(
            functools.partial(assemble_kernel, devices, first),
            shaped((comps, depth, lanes)),
            [scalar(), whole((8, columns)), whole((pairs, depth, lanes))]
            + [whole(back)] * devices
            + ([] if first else [untouched()]),
            part((2 * pairs, depth, lanes), chunk),
            1000000,
            16 * pairs * depth * lanes,
            aliases={} if first else {3 + devices: 0},
        )(me, info, solved[chunk], *extra[chunk], *([] if first else [owned]))
    return (state_next, owned, mean_emf)


def solution(mesh):
    return jax.shard_map(
        on_device,
        mesh=mesh,
        in_specs=(
            P(None, "col", "grp"),
            P(None, "col", "grp"),
            P(None, "col", "grp"),
            P(None, "col", "grp"),
            P(),
            P(),
            P(),
            P(),
            P(None, "grp"),
            P("grp", None),
        ),
        out_specs=(P(None, "col", "grp"), P(None, None, ("grp", "col")), P(None, "col")),
        check_vma=False,
    )
```

```python
import functools

import jax
import jax.numpy as jnp
from jax import lax
from jax.experimental import pallas as pl
from jax.experimental.pallas import tpu as pltpu
from jax.sharding import PartitionSpec as P

KMAX = 2048
TIME_STEP = 2.0
RK_ALPHA = -3.0 / 40.0
RK_BETA = 5.0 / 24.0
RK_GAMMA = 5.0 / 12.0
RK_ZETA = -17.0 / 60.0
WAVE_SCALE = 8.0
VMEM_LIMIT = 56 * 1024 * 1024
GROUPS = 3
LANES = 128

F32 = jnp.float32
BF16 = jnp.bfloat16


def call(body, out_shape, in_specs, out_specs, flops, nbytes, scratch=(), aliases=None):
    return pl.pallas_call(
        body,
        grid=(1,),
        out_shape=out_shape,
        in_specs=in_specs,
        out_specs=out_specs,
        scratch_shapes=list(scratch),
        input_output_aliases=aliases or {},
        cost_estimate=pl.CostEstimate(flops=flops, bytes_accessed=nbytes, transcendentals=0),
        compiler_params=pltpu.CompilerParams(vmem_limit_bytes=VMEM_LIMIT),
    )


def whole(shape):
    return pl.BlockSpec(shape, lambda i: (0,) * len(shape))


def part(shape, at):
    return pl.BlockSpec(shape, lambda i: (at,) + (0,) * (len(shape) - 1))


def scalar():
    return pl.BlockSpec(memory_space=pltpu.SMEM)


def untouched():
    return pl.BlockSpec(memory_space=pl.ANY)


def shaped(shape, dtype=F32):
    return jax.ShapeDtypeStruct(shape, dtype)


def three_parts(x):
    high = x.astype(BF16)
    rest = x - high.astype(F32)
    middle = rest.astype(BF16)
    low = (rest - middle.astype(F32)).astype(BF16)
    return jnp.concatenate([high, middle, low], axis=0)


def sum_parts(x):
    rows = x.shape[0] // 3
    return x[:rows] + x[rows : 2 * rows] + x[2 * rows :]


def two_parts(x):
    high = x.astype(BF16)
    low = (x - high.astype(F32)).astype(BF16)
    return high, low


def selector(places, rows):
    columns = places.shape[1]
    return (lax.broadcasted_iota(jnp.int32, (rows, columns), 0) == places).astype(F32).astype(BF16)


def wave_row(modes):
    wave_x = modes[0:1, :].astype(F32)
    wave_z = modes[1:2, :].astype(F32)
    return (wave_x * wave_x + wave_z * wave_z) * (WAVE_SCALE / (KMAX * KMAX))


NT = (((1,), (1,)), ((), ()))


def plan_kernel(devices, me_ref, owner_ref, modes_ref, info_ref, wave_ref):
    columns = owner_ref.shape[1]
    share = columns // devices
    rows = -(-devices // 8) * 8
    me = me_ref[0]
    owner = owner_ref[...]
    owned = (lax.broadcasted_iota(jnp.int32, (rows, columns), 0) == owner).astype(F32)
    before = (
        lax.broadcasted_iota(jnp.int32, (LANES, LANES), 0) < lax.broadcasted_iota(jnp.int32, (LANES, LANES), 1)
    ).astype(F32)
    carry = jnp.zeros((rows, 1), F32)
    earlier = []
    for at in range(columns // LANES):
        block = owned[:, at * LANES : (at + 1) * LANES]
        earlier.append(jnp.dot(block, before, preferred_element_type=F32) + carry)
        carry = carry + jnp.sum(block, axis=1, keepdims=True)
    counts = carry
    rank = jnp.sum(owned * jnp.concatenate(earlier, axis=1), axis=0, keepdims=True)
    surplus = jnp.maximum(counts - share, 0.0)
    lower = (lax.broadcasted_iota(jnp.int32, (rows, columns), 0) < owner).astype(F32)
    number = jnp.sum(lower * surplus, axis=0, keepdims=True) + (rank - share)
    free = share - jnp.minimum(counts, share)
    start = jnp.zeros((1, 1), F32)
    solver = owner
    slot = rank
    beyond = rank >= share
    for device in range(devices):
        here = free[device : device + 1, :]
        inside = beyond & (number >= start) & (number < start + here)
        solver = jnp.where(inside, device, solver)
        slot = jnp.where(inside, share - here + number - start, slot)
        start = start + here
    place = (solver ^ me) * share + slot.astype(jnp.int32)
    extra = jnp.where(beyond, (owner ^ me) * share + rank.astype(jnp.int32) - share, -1)
    mine = jnp.sum((owner == me).astype(F32), axis=1, keepdims=True).astype(jnp.int32)
    info_ref[...] = jnp.concatenate(
        [place, extra, jnp.broadcast_to(mine, (1, columns)), jnp.zeros((5, columns), jnp.int32)], axis=0
    )
    wave = jnp.broadcast_to(wave_row(modes_ref[...]), (16, columns))
    picked = sum_parts(
        lax.dot_general(three_parts(wave), selector(place, share), NT, preferred_element_type=F32)
    )
    wave_ref[...] = jnp.concatenate([picked, picked], axis=1)[:8]


def pack_kernel(devices, info_ref, modes_ref, state_ref, now_ref, old_ref, *out_refs):
    comps, points, columns = state_ref.shape
    share = columns // devices
    wave = wave_row(modes_ref[...]).reshape(1, 1, columns)
    state = state_ref[...]
    forcing = RK_GAMMA * now_ref[...] + RK_ZETA * old_ref[...]
    local = state + TIME_STEP * (forcing - RK_ALPHA * (wave * state))
    rows = comps * points
    both = jnp.concatenate([state.reshape(rows, columns), local.reshape(rows, columns)], axis=0)
    placed = sum_parts(
        lax.dot_general(
            three_parts(both), selector(info_ref[0:1, :], columns), NT, preferred_element_type=F32
        )
    )
    for step, out in zip(steps_of(devices), out_refs):
        taken = placed[:, step * share : (step + 1) * share]
        for kind in range(2):
            for pair in range(comps // 2):
                real = (kind * comps + 2 * pair) * points
                imag = real + points
                out[kind, pair] = jnp.concatenate(
                    [taken[real : real + points], taken[imag : imag + points]], axis=1
                )


def operators_kernel(deriv_ref, inverse_ref, basis_ref, values_ref, deriv_out, inverse_out, basis_out, values_out):
    for source, target in ((deriv_ref, deriv_out), (inverse_ref, inverse_out), (basis_ref, basis_out)):
        high, low = two_parts(source[...])
        target[...] = jnp.concatenate([high, high, low], axis=1)
    lanes = values_out.shape[1]
    values_out[...] = jnp.transpose(jnp.broadcast_to(values_ref[...], (lanes, values_ref.shape[1])))


def apply(operator, x):
    high, low = two_parts(x)
    return jnp.dot(operator, jnp.concatenate([high, low, high], axis=0), preferred_element_type=F32)


def solve_kernel(devices, me_ref, wave_ref, values_ref, deriv_ref, inverse_ref, basis_ref, *refs):
    in_refs, refs = refs[:devices], refs[devices:]
    out_refs, (solved_ref, state, local, after) = refs[:devices], refs[devices:]
    me = me_ref[0]
    _, pairs, points, lanes = in_refs[0].shape
    for step, block in zip(steps_of(devices), in_refs):
        rows = pl.ds(pl.multiple_of((me ^ step) * points, points), points)
        for pair in range(pairs):
            state[rows, pair * lanes : (pair + 1) * lanes] = block[0, pair]
            local[rows, pair * lanes : (pair + 1) * lanes] = block[1, pair]
    rhs = local[...] + (TIME_STEP * RK_ALPHA) * apply(deriv_ref[...], state[...])
    project = apply(inverse_ref[...], rhs)
    damping = 1.0 + TIME_STEP * RK_BETA * (values_ref[...] + wave_ref[0:1, :])
    project = project / jnp.concatenate([damping] * pairs, axis=1)
    after[...] = apply(basis_ref[...], project)
    for pair in range(pairs):
        solved_ref[pair] = after[:, pair * lanes : (pair + 1) * lanes]
    for step, block in zip(steps_of(devices), out_refs):
        rows = pl.ds(pl.multiple_of((me ^ step) * points, points), points)
        for pair in range(pairs):
            block[pair] = after[rows, pair * lanes : (pair + 1) * lanes]


def unpack_kernel(devices, chunk, first, info_ref, modes_ref, velocity_ref, *refs):
    in_refs, refs = refs[:devices], refs[devices:]
    if not first:
        (_, emf_in), refs = refs[:2], refs[2:]
    (state_ref, emf_ref), out_refs = refs[:2], refs[2:]
    pairs, points, lanes = in_refs[0].shape
    share = lanes // 2
    columns = devices * share
    order = steps_of(devices)
    blocks = [in_refs[order.index(step)] for step in range(devices)]
    got = []
    for pair in range(pairs):
        for half in range(2):
            got.append(
                jnp.concatenate(
                    [block[pair][:, half * share : (half + 1) * share] for block in blocks], axis=1
                )
            )
    got = jnp.concatenate(got, axis=0)
    state = sum_parts(
        jnp.dot(three_parts(got), selector(info_ref[0:1, :], columns), preferred_element_type=F32)
    )
    state_ref[...] = state.reshape(2 * pairs, points, columns)
    extra = sum_parts(
        lax.dot_general(
            three_parts(state), selector(info_ref[1:2, :], columns), NT, preferred_element_type=F32
        )
    )
    for step, out in zip(steps_of(devices), out_refs):
        taken = extra[:, step * share : (step + 1) * share]
        for pair in range(pairs):
            real = 2 * pair * points
            imag = real + points
            out[pair] = jnp.concatenate([taken[real : real + points], taken[imag : imag + points]], axis=1)
    weight = jnp.where(modes_ref[0:1, :] > 0, 2.0, 1.0).astype(F32)
    totals = [jnp.zeros((points, columns), F32)] * 3
    for pair in range(pairs):
        field = chunk * pairs + pair
        real = weight * state[2 * pair * points : (2 * pair + 1) * points]
        imag = weight * state[(2 * pair + 1) * points : (2 * pair + 2) * points]
        for sign, i, j in ((1.0, (field + 1) % 3, (field + 2) % 3), (-1.0, (field + 2) % 3, (field + 1) % 3)):
            totals[i] = totals[i] + sign * (velocity_ref[2 * j] * real + velocity_ref[2 * j + 1] * imag)
    rows = []
    for total in totals:
        folded = total[:, :LANES]
        for at in range(1, columns // LANES):
            folded = folded + total[:, at * LANES : (at + 1) * LANES]
        rows.append(jnp.sum(jnp.transpose(folded), axis=0, keepdims=True))
    rows = jnp.concatenate(rows, axis=0)
    emf_ref[...] = rows if first else rows + emf_in[...]


def assemble_kernel(devices, first, me_ref, info_ref, solved_ref, *refs):
    in_refs, refs = refs[:devices], refs[devices:]
    if not first:
        refs = refs[1:]
    (out_ref,) = refs
    me = me_ref[0]
    pairs, points, lanes = in_refs[0].shape
    share = lanes // 2
    depth = solved_ref.shape[1]
    used = lax.broadcasted_iota(jnp.int32, (depth, share), 1) < info_ref[2:3, :share]
    for pair in range(pairs):
        for half in range(2):
            kept = jnp.where(used, solved_ref[pair][:, half * share : (half + 1) * share], 0.0)
            out_ref[2 * pair + half, :, :share] = kept
            for step, block in zip(steps_of(devices), in_refs):
                rows = pl.ds(pl.multiple_of((me ^ step) * points, points), points)
                out_ref[2 * pair + half, rows, share:] = block[pair][:, half * share : (half + 1) * share]


def steps_of(devices):
    return [0] + sorted(range(1, devices), key=lambda step: -((step.bit_length() << 16) + (step >> 1 << 1)))


def exchange(blocks):
    devices = len(blocks)
    return [
        block if step == 0 else lax.ppermute(block, "col", [(i, i ^ step) for i in range(devices)])
        for step, block in zip(steps_of(devices), blocks)
    ]


def sum_over_groups(value):
    groups = lax.axis_size("grp")
    terms = [value] + [
        lax.ppermute(value, "grp", [(i, i ^ step) for i in range(groups)]) for step in range(1, groups)
    ]
    while len(terms) > 1:
        terms = [terms[at] + terms[at + 1] for at in range(0, len(terms), 2)]
    return terms[0]


def on_device(
    state_now,
    force_now,
    force_old,
    velocity,
    second_deriv,
    eig_basis,
    eig_inverse,
    eig_values,
    kept_modes,
    col_owner,
):
    comps, points, columns = state_now.shape
    devices = lax.axis_size("col")
    depth = devices * points
    share = columns // devices
    lanes = 2 * share
    pairs = GROUPS
    chunks = comps // (2 * pairs)
    me = lax.axis_index("col").astype(jnp.int32).reshape(1)
    owner = col_owner.reshape(1, columns)

    info, wave = call(
        functools.partial(plan_kernel, devices),
        [shaped((8, columns), jnp.int32), shaped((8, lanes))],
        [scalar(), whole((1, columns)), whole((2, columns))],
        [whole((8, columns)), whole((8, lanes))],
        1000000,
        100000,
    )(me, owner, kept_modes)

    field = (2 * pairs, points, columns)
    sent = (2, pairs, points, lanes)
    back = (pairs, points, lanes)
    moved = 4 * 2 * pairs * points * columns

    forward = []
    for chunk in range(chunks):
        forward.append(
            exchange(
                call(
                    functools.partial(pack_kernel, devices),
                    [shaped(sent)] * devices,
                    [whole((8, columns)), whole((2, columns))] + [part(field, chunk)] * 3,
                    [whole(sent)] * devices,
                    12 * 2 * pairs * points * columns * columns,
                    5 * moved,
                )(info, kept_modes, state_now, force_now, force_old)
            )
        )

    operator = shaped((depth, 3 * depth), BF16)
    operators = call(
        operators_kernel,
        [operator, operator, operator, shaped((depth, lanes))],
        [whole((depth, depth))] * 3 + [whole((1, depth))],
        [whole((depth, 3 * depth))] * 3 + [whole((depth, lanes))],
        1000000,
        30 * depth * depth,
    )(second_deriv, eig_inverse, eig_basis, eig_values.reshape(1, depth))
    values = operators[3]

    solved, returned = [], []
    for chunk in range(chunks):
        width = pairs * lanes
        outs = call(
            functools.partial(solve_kernel, devices),
            [shaped(back)] * devices + [shaped((pairs, depth, lanes))],
            [scalar(), whole((8, lanes)), whole((depth, lanes))]
            + [whole((depth, 3 * depth))] * 3
            + [whole(sent)] * devices,
            [whole(back)] * devices + [whole((pairs, depth, lanes))],
            18 * depth * depth * width,
            18 * depth * depth + 16 * depth * width,
            [pltpu.VMEM((depth, width), F32)] * 3,
        )(me, wave, values, *operators[:3], *forward[chunk])
        solved.append(outs[devices])
        returned.append(exchange(outs[:devices]))

    state_next, emf, extra = None, None, []
    for chunk in range(chunks):
        first = chunk == 0
        outs = call(
            functools.partial(unpack_kernel, devices, chunk, first),
            [shaped(state_now.shape), shaped((3, points))] + [shaped(back)] * devices,
            [whole((8, columns)), whole((2, columns)), whole(velocity.shape)]
            + [whole(back)] * devices
            + ([] if first else [untouched(), whole((3, points))]),
            [part(field, chunk), whole((3, points))] + [whole(back)] * devices,
            12 * 2 * pairs * points * columns * columns,
            6 * moved,
            aliases={} if first else {3 + devices: 0},
        )(info, kept_modes, velocity, *returned[chunk], *([] if first else [state_next, emf]))
        state_next, emf = outs[:2]
        extra.append(exchange(outs[2:]))
    mean_emf = sum_over_groups(emf)

    owned = None
    for chunk in range(chunks):
        first = chunk == 0
        owned = call(
            functools.partial(assemble_kernel, devices, first),
            shaped((comps, depth, lanes)),
            [scalar(), whole((8, columns)), whole((pairs, depth, lanes))]
            + [whole(back)] * devices
            + ([] if first else [untouched()]),
            part((2 * pairs, depth, lanes), chunk),
            1000000,
            16 * pairs * depth * lanes,
            aliases={} if first else {3 + devices: 0},
        )(me, info, solved[chunk], *extra[chunk], *([] if first else [owned]))
    return (state_next, owned, mean_emf)


def solution(mesh):
    return jax.shard_map(
        on_device,
        mesh=mesh,
        in_specs=(
            P(None, "col", "grp"),
            P(None, "col", "grp"),
            P(None, "col", "grp"),
            P(None, "col", "grp"),
            P(),
            P(),
            P(),
            P(),
            P(None, "grp"),
            P("grp", None),
        ),
        out_specs=(P(None, "col", "grp"), P(None, None, ("grp", "col")), P(None, "col")),
        check_vma=False,
    )
```

```python
import functools

import jax
import jax.numpy as jnp
from jax import lax
from jax.experimental import pallas as pl
from jax.experimental.pallas import tpu as pltpu
from jax.sharding import PartitionSpec as P

KMAX = 2048
TIME_STEP = 2.0
RK_ALPHA = -3.0 / 40.0
RK_BETA = 5.0 / 24.0
RK_GAMMA = 5.0 / 12.0
RK_ZETA = -17.0 / 60.0
WAVE_SCALE = 8.0
VMEM_LIMIT = 56 * 1024 * 1024
GROUPS = 1
LANES = 128

F32 = jnp.float32
BF16 = jnp.bfloat16


def call(body, out_shape, in_specs, out_specs, flops, nbytes, scratch=(), aliases=None):
    return pl.pallas_call(
        body,
        grid=(1,),
        out_shape=out_shape,
        in_specs=in_specs,
        out_specs=out_specs,
        scratch_shapes=list(scratch),
        input_output_aliases=aliases or {},
        cost_estimate=pl.CostEstimate(flops=flops, bytes_accessed=nbytes, transcendentals=0),
        compiler_params=pltpu.CompilerParams(vmem_limit_bytes=VMEM_LIMIT),
    )


def whole(shape):
    return pl.BlockSpec(shape, lambda i: (0,) * len(shape))


def part(shape, at):
    return pl.BlockSpec(shape, lambda i: (at,) + (0,) * (len(shape) - 1))


def scalar():
    return pl.BlockSpec(memory_space=pltpu.SMEM)


def untouched():
    return pl.BlockSpec(memory_space=pl.ANY)


def shaped(shape, dtype=F32):
    return jax.ShapeDtypeStruct(shape, dtype)


def three_parts(x):
    high = x.astype(BF16)
    rest = x - high.astype(F32)
    middle = rest.astype(BF16)
    low = (rest - middle.astype(F32)).astype(BF16)
    return jnp.concatenate([high, middle, low], axis=0)


def sum_parts(x):
    rows = x.shape[0] // 3
    return x[:rows] + x[rows : 2 * rows] + x[2 * rows :]


def two_parts(x):
    high = x.astype(BF16)
    low = (x - high.astype(F32)).astype(BF16)
    return high, low


def selector(places, rows):
    columns = places.shape[1]
    return (lax.broadcasted_iota(jnp.int32, (rows, columns), 0) == places).astype(F32).astype(BF16)


def wave_row(modes):
    wave_x = modes[0:1, :].astype(F32)
    wave_z = modes[1:2, :].astype(F32)
    return (wave_x * wave_x + wave_z * wave_z) * (WAVE_SCALE / (KMAX * KMAX))


NT = (((1,), (1,)), ((), ()))


def plan_kernel(devices, me_ref, owner_ref, modes_ref, info_ref, wave_ref):
    columns = owner_ref.shape[1]
    share = columns // devices
    rows = -(-devices // 8) * 8
    me = me_ref[0]
    owner = owner_ref[...]
    owned = (lax.broadcasted_iota(jnp.int32, (rows, columns), 0) == owner).astype(F32)
    before = (
        lax.broadcasted_iota(jnp.int32, (LANES, LANES), 0) < lax.broadcasted_iota(jnp.int32, (LANES, LANES), 1)
    ).astype(F32)
    carry = jnp.zeros((rows, 1), F32)
    earlier = []
    for at in range(columns // LANES):
        block = owned[:, at * LANES : (at + 1) * LANES]
        earlier.append(jnp.dot(block, before, preferred_element_type=F32) + carry)
        carry = carry + jnp.sum(block, axis=1, keepdims=True)
    counts = carry
    rank = jnp.sum(owned * jnp.concatenate(earlier, axis=1), axis=0, keepdims=True)
    surplus = jnp.maximum(counts - share, 0.0)
    lower = (lax.broadcasted_iota(jnp.int32, (rows, columns), 0) < owner).astype(F32)
    number = jnp.sum(lower * surplus, axis=0, keepdims=True) + (rank - share)
    free = share - jnp.minimum(counts, share)
    start = jnp.zeros((1, 1), F32)
    solver = owner
    slot = rank
    beyond = rank >= share
    for device in range(devices):
        here = free[device : device + 1, :]
        inside = beyond & (number >= start) & (number < start + here)
        solver = jnp.where(inside, device, solver)
        slot = jnp.where(inside, share - here + number - start, slot)
        start = start + here
    place = (solver ^ me) * share + slot.astype(jnp.int32)
    extra = jnp.where(beyond, (owner ^ me) * share + rank.astype(jnp.int32) - share, -1)
    mine = jnp.sum((owner == me).astype(F32), axis=1, keepdims=True).astype(jnp.int32)
    info_ref[...] = jnp.concatenate(
        [place, extra, jnp.broadcast_to(mine, (1, columns)), jnp.zeros((5, columns), jnp.int32)], axis=0
    )
    wave = jnp.broadcast_to(wave_row(modes_ref[...]), (16, columns))
    picked = sum_parts(
        lax.dot_general(three_parts(wave), selector(place, share), NT, preferred_element_type=F32)
    )
    wave_ref[...] = jnp.concatenate([picked, picked], axis=1)[:8]


def pack_kernel(devices, info_ref, modes_ref, state_ref, now_ref, old_ref, *out_refs):
    comps, points, columns = state_ref.shape
    share = columns // devices
    wave = wave_row(modes_ref[...]).reshape(1, 1, columns)
    state = state_ref[...]
    forcing = RK_GAMMA * now_ref[...] + RK_ZETA * old_ref[...]
    local = state + TIME_STEP * (forcing - RK_ALPHA * (wave * state))
    rows = comps * points
    both = jnp.concatenate([state.reshape(rows, columns), local.reshape(rows, columns)], axis=0)
    placed = sum_parts(
        lax.dot_general(
            three_parts(both), selector(info_ref[0:1, :], columns), NT, preferred_element_type=F32
        )
    )
    for step, out in zip(steps_of(devices), out_refs):
        taken = placed[:, step * share : (step + 1) * share]
        for kind in range(2):
            for pair in range(comps // 2):
                real = (kind * comps + 2 * pair) * points
                imag = real + points
                out[kind, pair] = jnp.concatenate(
                    [taken[real : real + points], taken[imag : imag + points]], axis=1
                )


def operators_kernel(deriv_ref, inverse_ref, basis_ref, values_ref, deriv_out, inverse_out, basis_out, values_out):
    for source, target in ((deriv_ref, deriv_out), (inverse_ref, inverse_out), (basis_ref, basis_out)):
        high, low = two_parts(source[...])
        target[...] = jnp.concatenate([high, high, low], axis=1)
    lanes = values_out.shape[1]
    values_out[...] = jnp.transpose(jnp.broadcast_to(values_ref[...], (lanes, values_ref.shape[1])))


def apply(operator, x):
    high, low = two_parts(x)
    return jnp.dot(operator, jnp.concatenate([high, low, high], axis=0), preferred_element_type=F32)


def solve_kernel(devices, me_ref, wave_ref, values_ref, deriv_ref, inverse_ref, basis_ref, *refs):
    in_refs, refs = refs[:devices], refs[devices:]
    out_refs, (solved_ref, state, local, after) = refs[:devices], refs[devices:]
    me = me_ref[0]
    _, pairs, points, lanes = in_refs[0].shape
    for step, block in zip(steps_of(devices), in_refs):
        rows = pl.ds(pl.multiple_of((me ^ step) * points, points), points)
        for pair in range(pairs):
            state[rows, pair * lanes : (pair + 1) * lanes] = block[0, pair]
            local[rows, pair * lanes : (pair + 1) * lanes] = block[1, pair]
    rhs = local[...] + (TIME_STEP * RK_ALPHA) * apply(deriv_ref[...], state[...])
    project = apply(inverse_ref[...], rhs)
    damping = 1.0 + TIME_STEP * RK_BETA * (values_ref[...] + wave_ref[0:1, :])
    project = project / jnp.concatenate([damping] * pairs, axis=1)
    after[...] = apply(basis_ref[...], project)
    for pair in range(pairs):
        solved_ref[pair] = after[:, pair * lanes : (pair + 1) * lanes]
    for step, block in zip(steps_of(devices), out_refs):
        rows = pl.ds(pl.multiple_of((me ^ step) * points, points), points)
        for pair in range(pairs):
            block[pair] = after[rows, pair * lanes : (pair + 1) * lanes]


def unpack_kernel(devices, chunk, first, info_ref, modes_ref, velocity_ref, *refs):
    in_refs, refs = refs[:devices], refs[devices:]
    if not first:
        (_, emf_in), refs = refs[:2], refs[2:]
    (state_ref, emf_ref), out_refs = refs[:2], refs[2:]
    pairs, points, lanes = in_refs[0].shape
    share = lanes // 2
    columns = devices * share
    order = steps_of(devices)
    blocks = [in_refs[order.index(step)] for step in range(devices)]
    got = []
    for pair in range(pairs):
        for half in range(2):
            got.append(
                jnp.concatenate(
                    [block[pair][:, half * share : (half + 1) * share] for block in blocks], axis=1
                )
            )
    got = jnp.concatenate(got, axis=0)
    state = sum_parts(
        jnp.dot(three_parts(got), selector(info_ref[0:1, :], columns), preferred_element_type=F32)
    )
    state_ref[...] = state.reshape(2 * pairs, points, columns)
    extra = sum_parts(
        lax.dot_general(
            three_parts(state), selector(info_ref[1:2, :], columns), NT, preferred_element_type=F32
        )
    )
    for step, out in zip(steps_of(devices), out_refs):
        taken = extra[:, step * share : (step + 1) * share]
        for pair in range(pairs):
            real = 2 * pair * points
            imag = real + points
            out[pair] = jnp.concatenate([taken[real : real + points], taken[imag : imag + points]], axis=1)
    weight = jnp.where(modes_ref[0:1, :] > 0, 2.0, 1.0).astype(F32)
    totals = [jnp.zeros((points, columns), F32)] * 3
    for pair in range(pairs):
        field = chunk * pairs + pair
        real = weight * state[2 * pair * points : (2 * pair + 1) * points]
        imag = weight * state[(2 * pair + 1) * points : (2 * pair + 2) * points]
        for sign, i, j in ((1.0, (field + 1) % 3, (field + 2) % 3), (-1.0, (field + 2) % 3, (field + 1) % 3)):
            totals[i] = totals[i] + sign * (velocity_ref[2 * j] * real + velocity_ref[2 * j + 1] * imag)
    rows = []
    for total in totals:
        folded = total[:, :LANES]
        for at in range(1, columns // LANES):
            folded = folded + total[:, at * LANES : (at + 1) * LANES]
        rows.append(jnp.sum(jnp.transpose(folded), axis=0, keepdims=True))
    rows = jnp.concatenate(rows, axis=0)
    emf_ref[...] = rows if first else rows + emf_in[...]


def assemble_kernel(devices, first, me_ref, info_ref, solved_ref, *refs):
    in_refs, refs = refs[:devices], refs[devices:]
    if not first:
        refs = refs[1:]
    (out_ref,) = refs
    me = me_ref[0]
    pairs, points, lanes = in_refs[0].shape
    share = lanes // 2
    depth = solved_ref.shape[1]
    used = lax.broadcasted_iota(jnp.int32, (depth, share), 1) < info_ref[2:3, :share]
    for pair in range(pairs):
        for half in range(2):
            kept = jnp.where(used, solved_ref[pair][:, half * share : (half + 1) * share], 0.0)
            out_ref[2 * pair + half, :, :share] = kept
            for step, block in zip(steps_of(devices), in_refs):
                rows = pl.ds(pl.multiple_of((me ^ step) * points, points), points)
                out_ref[2 * pair + half, rows, share:] = block[pair][:, half * share : (half + 1) * share]


def steps_of(devices):
    return [0] + sorted(range(1, devices), key=lambda step: -((step.bit_length() << 16) + (step >> 1 << 1)))


def exchange(blocks):
    devices = len(blocks)
    return [
        block if step == 0 else lax.ppermute(block, "col", [(i, i ^ step) for i in range(devices)])
        for step, block in zip(steps_of(devices), blocks)
    ]


def sum_over_groups(value):
    groups = lax.axis_size("grp")
    terms = [value] + [
        lax.ppermute(value, "grp", [(i, i ^ step) for i in range(groups)]) for step in range(1, groups)
    ]
    while len(terms) > 1:
        terms = [terms[at] + terms[at + 1] for at in range(0, len(terms), 2)]
    return terms[0]


def on_device(
    state_now,
    force_now,
    force_old,
    velocity,
    second_deriv,
    eig_basis,
    eig_inverse,
    eig_values,
    kept_modes,
    col_owner,
):
    comps, points, columns = state_now.shape
    devices = lax.axis_size("col")
    depth = devices * points
    share = columns // devices
    lanes = 2 * share
    pairs = GROUPS
    chunks = comps // (2 * pairs)
    me = lax.axis_index("col").astype(jnp.int32).reshape(1)
    owner = col_owner.reshape(1, columns)

    info, wave = call(
        functools.partial(plan_kernel, devices),
        [shaped((8, columns), jnp.int32), shaped((8, lanes))],
        [scalar(), whole((1, columns)), whole((2, columns))],
        [whole((8, columns)), whole((8, lanes))],
        1000000,
        100000,
    )(me, owner, kept_modes)

    field = (2 * pairs, points, columns)
    sent = (2, pairs, points, lanes)
    back = (pairs, points, lanes)
    moved = 4 * 2 * pairs * points * columns

    forward = []
    for chunk in range(chunks):
        forward.append(
            exchange(
                call(
                    functools.partial(pack_kernel, devices),
                    [shaped(sent)] * devices,
                    [whole((8, columns)), whole((2, columns))] + [part(field, chunk)] * 3,
                    [whole(sent)] * devices,
                    12 * 2 * pairs * points * columns * columns,
                    5 * moved,
                )(info, kept_modes, state_now, force_now, force_old)
            )
        )

    operator = shaped((depth, 3 * depth), BF16)
    operators = call(
        operators_kernel,
        [operator, operator, operator, shaped((depth, lanes))],
        [whole((depth, depth))] * 3 + [whole((1, depth))],
        [whole((depth, 3 * depth))] * 3 + [whole((depth, lanes))],
        1000000,
        30 * depth * depth,
    )(second_deriv, eig_inverse, eig_basis, eig_values.reshape(1, depth))
    values = operators[3]

    solved, returned = [], []
    for chunk in range(chunks):
        width = pairs * lanes
        outs = call(
            functools.partial(solve_kernel, devices),
            [shaped(back)] * devices + [shaped((pairs, depth, lanes))],
            [scalar(), whole((8, lanes)), whole((depth, lanes))]
            + [whole((depth, 3 * depth))] * 3
            + [whole(sent)] * devices,
            [whole(back)] * devices + [whole((pairs, depth, lanes))],
            18 * depth * depth * width,
            18 * depth * depth + 16 * depth * width,
            [pltpu.VMEM((depth, width), F32)] * 3,
        )(me, wave, values, *operators[:3], *forward[chunk])
        solved.append(outs[devices])
        returned.append(exchange(outs[:devices]))

    state_next, emf, extra = None, None, []
    for chunk in range(chunks):
        first = chunk == 0
        outs = call(
            functools.partial(unpack_kernel, devices, chunk, first),
            [shaped(state_now.shape), shaped((3, points))] + [shaped(back)] * devices,
            [whole((8, columns)), whole((2, columns)), whole(velocity.shape)]
            + [whole(back)] * devices
            + ([] if first else [untouched(), whole((3, points))]),
            [part(field, chunk), whole((3, points))] + [whole(back)] * devices,
            12 * 2 * pairs * points * columns * columns,
            6 * moved,
            aliases={} if first else {3 + devices: 0},
        )(info, kept_modes, velocity, *returned[chunk], *([] if first else [state_next, emf]))
        state_next, emf = outs[:2]
        extra.append(exchange(outs[2:]))
    mean_emf = sum_over_groups(emf)

    owned = None
    for chunk in range(chunks):
        first = chunk == 0
        owned = call(
            functools.partial(assemble_kernel, devices, first),
            shaped((comps, depth, lanes)),
            [scalar(), whole((8, columns)), whole((pairs, depth, lanes))]
            + [whole(back)] * devices
            + ([] if first else [untouched()]),
            part((2 * pairs, depth, lanes), chunk),
            1000000,
            16 * pairs * depth * lanes,
            aliases={} if first else {3 + devices: 0},
        )(me, info, solved[chunk], *extra[chunk], *([] if first else [owned]))
    return (state_next, owned, mean_emf)


def solution(mesh):
    return jax.shard_map(
        on_device,
        mesh=mesh,
        in_specs=(
            P(None, "col", "grp"),
            P(None, "col", "grp"),
            P(None, "col", "grp"),
            P(None, "col", "grp"),
            P(),
            P(),
            P(),
            P(),
            P(None, "grp"),
            P("grp", None),
        ),
        out_specs=(P(None, "col", "grp"), P(None, None, ("grp", "col")), P(None, "col")),
        check_vma=False,
    )
```

```python
import functools

import jax
import jax.numpy as jnp
from jax import lax
from jax.experimental import pallas as pl
from jax.experimental.pallas import tpu as pltpu
from jax.sharding import PartitionSpec as P

KMAX = 2048
TIME_STEP = 2.0
RK_ALPHA = -3.0 / 40.0
RK_BETA = 5.0 / 24.0
RK_GAMMA = 5.0 / 12.0
RK_ZETA = -17.0 / 60.0
WAVE_SCALE = 8.0
VMEM_LIMIT = 56 * 1024 * 1024
GROUPS = 1
LANES = 128

F32 = jnp.float32
BF16 = jnp.bfloat16


def call(body, out_shape, in_specs, out_specs, flops, nbytes, scratch=(), aliases=None):
    return pl.pallas_call(
        body,
        grid=(1,),
        out_shape=out_shape,
        in_specs=in_specs,
        out_specs=out_specs,
        scratch_shapes=list(scratch),
        input_output_aliases=aliases or {},
        cost_estimate=pl.CostEstimate(flops=flops, bytes_accessed=nbytes, transcendentals=0),
        compiler_params=pltpu.CompilerParams(vmem_limit_bytes=VMEM_LIMIT),
    )


def whole(shape):
    return pl.BlockSpec(shape, lambda i: (0,) * len(shape))


def part(shape, at):
    return pl.BlockSpec(shape, lambda i: (at,) + (0,) * (len(shape) - 1))


def scalar():
    return pl.BlockSpec(memory_space=pltpu.SMEM)


def untouched():
    return pl.BlockSpec(memory_space=pl.ANY)


def shaped(shape, dtype=F32):
    return jax.ShapeDtypeStruct(shape, dtype)


def three_parts(x):
    high = x.astype(BF16)
    rest = x - high.astype(F32)
    middle = rest.astype(BF16)
    low = (rest - middle.astype(F32)).astype(BF16)
    return jnp.concatenate([high, middle, low], axis=0)


def sum_parts(x):
    rows = x.shape[0] // 3
    return x[:rows] + x[rows : 2 * rows] + x[2 * rows :]


def two_parts(x):
    high = x.astype(BF16)
    low = (x - high.astype(F32)).astype(BF16)
    return high, low


def selector(places, rows):
    columns = places.shape[1]
    return (lax.broadcasted_iota(jnp.int32, (rows, columns), 0) == places).astype(F32).astype(BF16)


def wave_row(modes):
    wave_x = modes[0:1, :].astype(F32)
    wave_z = modes[1:2, :].astype(F32)
    return (wave_x * wave_x + wave_z * wave_z) * (WAVE_SCALE / (KMAX * KMAX))


NT = (((1,), (1,)), ((), ()))


def plan_kernel(devices, me_ref, owner_ref, modes_ref, info_ref, wave_ref):
    columns = owner_ref.shape[1]
    share = columns // devices
    rows = -(-devices // 8) * 8
    me = me_ref[0]
    owner = owner_ref[...]
    owned = (lax.broadcasted_iota(jnp.int32, (rows, columns), 0) == owner).astype(F32)
    before = (
        lax.broadcasted_iota(jnp.int32, (LANES, LANES), 0) < lax.broadcasted_iota(jnp.int32, (LANES, LANES), 1)
    ).astype(F32)
    carry = jnp.zeros((rows, 1), F32)
    earlier = []
    for at in range(columns // LANES):
        block = owned[:, at * LANES : (at + 1) * LANES]
        earlier.append(jnp.dot(block, before, preferred_element_type=F32) + carry)
        carry = carry + jnp.sum(block, axis=1, keepdims=True)
    counts = carry
    rank = jnp.sum(owned * jnp.concatenate(earlier, axis=1), axis=0, keepdims=True)
    surplus = jnp.maximum(counts - share, 0.0)
    lower = (lax.broadcasted_iota(jnp.int32, (rows, columns), 0) < owner).astype(F32)
    number = jnp.sum(lower * surplus, axis=0, keepdims=True) + (rank - share)
    free = share - jnp.minimum(counts, share)
    start = jnp.zeros((1, 1), F32)
    solver = owner
    slot = rank
    beyond = rank >= share
    for device in range(devices):
        here = free[device : device + 1, :]
        inside = beyond & (number >= start) & (number < start + here)
        solver = jnp.where(inside, device, solver)
        slot = jnp.where(inside, share - here + number - start, slot)
        start = start + here
    place = (solver ^ me) * share + slot.astype(jnp.int32)
    extra = jnp.where(beyond, (owner ^ me) * share + rank.astype(jnp.int32) - share, -1)
    mine = jnp.sum((owner == me).astype(F32), axis=1, keepdims=True).astype(jnp.int32)
    info_ref[...] = jnp.concatenate(
        [place, extra, jnp.broadcast_to(mine, (1, columns)), jnp.zeros((5, columns), jnp.int32)], axis=0
    )
    wave = jnp.broadcast_to(wave_row(modes_ref[...]), (16, columns))
    picked = sum_parts(
        lax.dot_general(three_parts(wave), selector(place, share), NT, preferred_element_type=F32)
    )
    wave_ref[...] = jnp.concatenate([picked, picked], axis=1)[:8]


def pack_kernel(devices, me_ref, info_ref, modes_ref, state_ref, now_ref, old_ref, out_ref):
    me = me_ref[0]
    comps, points, columns = state_ref.shape
    share = columns // devices
    wave = wave_row(modes_ref[...]).reshape(1, 1, columns)
    state = state_ref[...]
    forcing = RK_GAMMA * now_ref[...] + RK_ZETA * old_ref[...]
    local = state + TIME_STEP * (forcing - RK_ALPHA * (wave * state))
    rows = comps * points
    both = jnp.concatenate([state.reshape(rows, columns), local.reshape(rows, columns)], axis=0)
    placed = sum_parts(
        lax.dot_general(
            three_parts(both), selector(info_ref[0:1, :], columns), NT, preferred_element_type=F32
        )
    )
    for step in range(devices):
        taken = placed[:, step * share : (step + 1) * share]
        for kind in range(2):
            for pair in range(comps // 2):
                real = (kind * comps + 2 * pair) * points
                imag = real + points
                out_ref[me ^ step, kind, pair] = jnp.concatenate(
                    [taken[real : real + points], taken[imag : imag + points]], axis=1
                )


def operators_kernel(deriv_ref, inverse_ref, basis_ref, values_ref, deriv_out, inverse_out, basis_out, values_out):
    for source, target in ((deriv_ref, deriv_out), (inverse_ref, inverse_out), (basis_ref, basis_out)):
        high, low = two_parts(source[...])
        target[...] = jnp.concatenate([high, high, low], axis=1)
    lanes = values_out.shape[1]
    values_out[...] = jnp.transpose(jnp.broadcast_to(values_ref[...], (lanes, values_ref.shape[1])))


def apply(operator, x):
    high, low = two_parts(x)
    return jnp.dot(operator, jnp.concatenate([high, low, high], axis=0), preferred_element_type=F32)


def solve_kernel(devices, wave_ref, values_ref, deriv_ref, inverse_ref, basis_ref, in_ref, out_ref, solved_ref, state, local):
    _, _, pairs, points, lanes = in_ref.shape
    for device in range(devices):
        rows = slice(device * points, (device + 1) * points)
        for pair in range(pairs):
            state[rows, pair * lanes : (pair + 1) * lanes] = in_ref[device, 0, pair]
            local[rows, pair * lanes : (pair + 1) * lanes] = in_ref[device, 1, pair]
    rhs = local[...] + (TIME_STEP * RK_ALPHA) * apply(deriv_ref[...], state[...])
    project = apply(inverse_ref[...], rhs)
    damping = 1.0 + TIME_STEP * RK_BETA * (values_ref[...] + wave_ref[0:1, :])
    project = project / jnp.concatenate([damping] * pairs, axis=1)
    after = apply(basis_ref[...], project)
    for pair in range(pairs):
        solved = after[:, pair * lanes : (pair + 1) * lanes]
        solved_ref[pair] = solved
        for device in range(devices):
            out_ref[device, pair] = solved[device * points : (device + 1) * points]


def unpack_kernel(devices, chunk, first, me_ref, info_ref, modes_ref, velocity_ref, in_ref, *refs):
    me = me_ref[0]
    if not first:
        (_, emf_in), refs = refs[:2], refs[2:]
    state_ref, emf_ref, out_ref = refs
    _, pairs, points, lanes = in_ref.shape
    share = lanes // 2
    columns = devices * share
    got = []
    for pair in range(pairs):
        for half in range(2):
            got.append(
                jnp.concatenate(
                    [in_ref[me ^ step, pair][:, half * share : (half + 1) * share] for step in range(devices)], axis=1
                )
            )
    got = jnp.concatenate(got, axis=0)
    state = sum_parts(
        jnp.dot(three_parts(got), selector(info_ref[0:1, :], columns), preferred_element_type=F32)
    )
    state_ref[...] = state.reshape(2 * pairs, points, columns)
    extra = sum_parts(
        lax.dot_general(
            three_parts(state), selector(info_ref[1:2, :], columns), NT, preferred_element_type=F32
        )
    )
    for step in range(devices):
        taken = extra[:, step * share : (step + 1) * share]
        for pair in range(pairs):
            real = 2 * pair * points
            imag = real + points
            out_ref[me ^ step, pair] = jnp.concatenate([taken[real : real + points], taken[imag : imag + points]], axis=1)
    weight = jnp.where(modes_ref[0:1, :] > 0, 2.0, 1.0).astype(F32)
    totals = [jnp.zeros((points, columns), F32)] * 3
    for pair in range(pairs):
        field = chunk * pairs + pair
        real = weight * state[2 * pair * points : (2 * pair + 1) * points]
        imag = weight * state[(2 * pair + 1) * points : (2 * pair + 2) * points]
        for sign, i, j in ((1.0, (field + 1) % 3, (field + 2) % 3), (-1.0, (field + 2) % 3, (field + 1) % 3)):
            totals[i] = totals[i] + sign * (velocity_ref[2 * j] * real + velocity_ref[2 * j + 1] * imag)
    rows = []
    for total in totals:
        folded = total[:, :LANES]
        for at in range(1, columns // LANES):
            folded = folded + total[:, at * LANES : (at + 1) * LANES]
        rows.append(jnp.sum(jnp.transpose(folded), axis=0, keepdims=True))
    rows = jnp.concatenate(rows, axis=0)
    emf_ref[...] = rows if first else rows + emf_in[...]


def assemble_kernel(devices, first, info_ref, solved_ref, in_ref, *refs):
    out_ref = refs[-1]
    _, pairs, points, lanes = in_ref.shape
    share = lanes // 2
    depth = solved_ref.shape[1]
    used = lax.broadcasted_iota(jnp.int32, (depth, share), 1) < info_ref[2:3, :share]
    for pair in range(pairs):
        for half in range(2):
            kept = jnp.where(used, solved_ref[pair][:, half * share : (half + 1) * share], 0.0)
            out_ref[2 * pair + half, :, :share] = kept
            for device in range(devices):
                rows = slice(device * points, (device + 1) * points)
                out_ref[2 * pair + half, rows, share:] = in_ref[device, pair][:, half * share : (half + 1) * share]


def exchange(blocks):
    return lax.all_to_all(blocks, "col", split_axis=0, concat_axis=0, tiled=True)


def sum_over_groups(value):
    groups = lax.axis_size("grp")
    terms = [value] + [
        lax.ppermute(value, "grp", [(i, i ^ step) for i in range(groups)]) for step in range(1, groups)
    ]
    while len(terms) > 1:
        terms = [terms[at] + terms[at + 1] for at in range(0, len(terms), 2)]
    return terms[0]


def on_device(
    state_now,
    force_now,
    force_old,
    velocity,
    second_deriv,
    eig_basis,
    eig_inverse,
    eig_values,
    kept_modes,
    col_owner,
):
    comps, points, columns = state_now.shape
    devices = lax.axis_size("col")
    depth = devices * points
    share = columns // devices
    lanes = 2 * share
    pairs = GROUPS
    chunks = comps // (2 * pairs)
    me = lax.axis_index("col").astype(jnp.int32).reshape(1)
    owner = col_owner.reshape(1, columns)

    info, wave = call(
        functools.partial(plan_kernel, devices),
        [shaped((8, columns), jnp.int32), shaped((8, lanes))],
        [scalar(), whole((1, columns)), whole((2, columns))],
        [whole((8, columns)), whole((8, lanes))],
        1000000,
        100000,
    )(me, owner, kept_modes)

    field = (2 * pairs, points, columns)
    sent = (devices, 2, pairs, points, lanes)
    back = (devices, pairs, points, lanes)
    moved = 4 * 2 * pairs * points * columns

    forward = []
    for chunk in range(chunks):
        forward.append(
            exchange(
                call(
                    functools.partial(pack_kernel, devices),
                    shaped(sent),
                    [scalar(), whole((8, columns)), whole((2, columns))] + [part(field, chunk)] * 3,
                    whole(sent),
                    12 * 2 * pairs * points * columns * columns,
                    5 * moved,
                )(me, info, kept_modes, state_now, force_now, force_old)
            )
        )

    operator = shaped((depth, 3 * depth), BF16)
    operators = call(
        operators_kernel,
        [operator, operator, operator, shaped((depth, lanes))],
        [whole((depth, depth))] * 3 + [whole((1, depth))],
        [whole((depth, 3 * depth))] * 3 + [whole((depth, lanes))],
        1000000,
        30 * depth * depth,
    )(second_deriv, eig_inverse, eig_basis, eig_values.reshape(1, depth))
    values = operators[3]

    solved, returned = [], []
    for chunk in range(chunks):
        width = pairs * lanes
        outs = call(
            functools.partial(solve_kernel, devices),
            [shaped(back), shaped((pairs, depth, lanes))],
            [whole((8, lanes)), whole((depth, lanes))] + [whole((depth, 3 * depth))] * 3 + [whole(sent)],
            [whole(back), whole((pairs, depth, lanes))],
            18 * depth * depth * width,
            18 * depth * depth + 16 * depth * width,
            [pltpu.VMEM((depth, width), F32)] * 2,
        )(wave, values, *operators[:3], forward[chunk])
        solved.append(outs[1])
        returned.append(exchange(outs[0]))

    state_next, emf, extra = None, None, []
    for chunk in range(chunks):
        first = chunk == 0
        outs = call(
            functools.partial(unpack_kernel, devices, chunk, first),
            [shaped(state_now.shape), shaped((3, points)), shaped(back)],
            [scalar(), whole((8, columns)), whole((2, columns)), whole(velocity.shape), whole(back)]
            + ([] if first else [untouched(), whole((3, points))]),
            [part(field, chunk), whole((3, points)), whole(back)],
            12 * 2 * pairs * points * columns * columns,
            6 * moved,
            aliases={} if first else {5: 0},
        )(me, info, kept_modes, velocity, returned[chunk], *([] if first else [state_next, emf]))
        state_next, emf = outs[:2]
        extra.append(exchange(outs[2]))
    mean_emf = sum_over_groups(emf)

    owned = None
    for chunk in range(chunks):
        first = chunk == 0
        owned = call(
            functools.partial(assemble_kernel, devices, first),
            shaped((comps, depth, lanes)),
            [whole((8, columns)), whole((pairs, depth, lanes)), whole(back)] + ([] if first else [untouched()]),
            part((2 * pairs, depth, lanes), chunk),
            1000000,
            16 * pairs * depth * lanes,
            aliases={} if first else {3: 0},
        )(info, solved[chunk], extra[chunk], *([] if first else [owned]))
    return (state_next, owned, mean_emf)


def solution(mesh):
    return jax.shard_map(
        on_device,
        mesh=mesh,
        in_specs=(
            P(None, "col", "grp"),
            P(None, "col", "grp"),
            P(None, "col", "grp"),
            P(None, "col", "grp"),
            P(),
            P(),
            P(),
            P(),
            P(None, "grp"),
            P("grp", None),
        ),
        out_specs=(P(None, "col", "grp"), P(None, None, ("grp", "col")), P(None, "col")),
        check_vma=False,
    )
```

```python
import functools

import jax
import jax.numpy as jnp
from jax import lax
from jax.experimental import pallas as pl
from jax.experimental.pallas import tpu as pltpu
from jax.sharding import PartitionSpec as P

KMAX = 2048
TIME_STEP = 2.0
RK_ALPHA = -3.0 / 40.0
RK_BETA = 5.0 / 24.0
RK_GAMMA = 5.0 / 12.0
RK_ZETA = -17.0 / 60.0
WAVE_SCALE = 8.0
VMEM_LIMIT = 24 * 1024 * 1024
GROUPS = 3
LANES = 128

F32 = jnp.float32
BF16 = jnp.bfloat16


def call(body, out_shape, in_specs, out_specs, flops, nbytes, scratch=(), aliases=None):
    return pl.pallas_call(
        body,
        grid=(1,),
        out_shape=out_shape,
        in_specs=in_specs,
        out_specs=out_specs,
        scratch_shapes=list(scratch),
        input_output_aliases=aliases or {},
        cost_estimate=pl.CostEstimate(flops=flops, bytes_accessed=nbytes, transcendentals=0),
        compiler_params=pltpu.CompilerParams(vmem_limit_bytes=VMEM_LIMIT),
    )


def whole(shape):
    return pl.BlockSpec(shape, lambda i: (0,) * len(shape))


def part(shape, at):
    return pl.BlockSpec(shape, lambda i: (at,) + (0,) * (len(shape) - 1))


def scalar():
    return pl.BlockSpec(memory_space=pltpu.SMEM)


def untouched():
    return pl.BlockSpec(memory_space=pl.ANY)


def shaped(shape, dtype=F32):
    return jax.ShapeDtypeStruct(shape, dtype)


def three_parts(x):
    high = x.astype(BF16)
    rest = x - high.astype(F32)
    middle = rest.astype(BF16)
    low = (rest - middle.astype(F32)).astype(BF16)
    return jnp.concatenate([high, middle, low], axis=0)


def sum_parts(x):
    rows = x.shape[0] // 3
    return x[:rows] + x[rows : 2 * rows] + x[2 * rows :]


def two_parts(x):
    high = x.astype(BF16)
    low = (x - high.astype(F32)).astype(BF16)
    return high, low


def selector(places, rows):
    columns = places.shape[1]
    return (lax.broadcasted_iota(jnp.int32, (rows, columns), 0) == places).astype(F32).astype(BF16)


def wave_row(modes):
    wave_x = modes[0:1, :].astype(F32)
    wave_z = modes[1:2, :].astype(F32)
    return (wave_x * wave_x + wave_z * wave_z) * (WAVE_SCALE / (KMAX * KMAX))


NT = (((1,), (1,)), ((), ()))


def plan_kernel(devices, me_ref, owner_ref, modes_ref, info_ref, wave_ref):
    columns = owner_ref.shape[1]
    share = columns // devices
    rows = -(-devices // 8) * 8
    me = me_ref[0]
    owner = owner_ref[...]
    owned = (lax.broadcasted_iota(jnp.int32, (rows, columns), 0) == owner).astype(F32)
    before = (
        lax.broadcasted_iota(jnp.int32, (LANES, LANES), 0) < lax.broadcasted_iota(jnp.int32, (LANES, LANES), 1)
    ).astype(F32)
    carry = jnp.zeros((rows, 1), F32)
    earlier = []
    for at in range(columns // LANES):
        block = owned[:, at * LANES : (at + 1) * LANES]
        earlier.append(jnp.dot(block, before, preferred_element_type=F32) + carry)
        carry = carry + jnp.sum(block, axis=1, keepdims=True)
    counts = carry
    rank = jnp.sum(owned * jnp.concatenate(earlier, axis=1), axis=0, keepdims=True)
    surplus = jnp.maximum(counts - share, 0.0)
    lower = (lax.broadcasted_iota(jnp.int32, (rows, columns), 0) < owner).astype(F32)
    number = jnp.sum(lower * surplus, axis=0, keepdims=True) + (rank - share)
    free = share - jnp.minimum(counts, share)
    start = jnp.zeros((1, 1), F32)
    solver = owner
    slot = rank
    beyond = rank >= share
    for device in range(devices):
        here = free[device : device + 1, :]
        inside = beyond & (number >= start) & (number < start + here)
        solver = jnp.where(inside, device, solver)
        slot = jnp.where(inside, share - here + number - start, slot)
        start = start + here
    place = (solver ^ me) * share + slot.astype(jnp.int32)
    extra = jnp.where(beyond, (owner ^ me) * share + rank.astype(jnp.int32) - share, -1)
    mine = jnp.sum((owner == me).astype(F32), axis=1, keepdims=True).astype(jnp.int32)
    info_ref[...] = jnp.concatenate(
        [place, extra, jnp.broadcast_to(mine, (1, columns)), jnp.zeros((5, columns), jnp.int32)], axis=0
    )
    wave = jnp.broadcast_to(wave_row(modes_ref[...]), (16, columns))
    picked = sum_parts(
        lax.dot_general(three_parts(wave), selector(place, share), NT, preferred_element_type=F32)
    )
    wave_ref[...] = jnp.concatenate([picked, picked], axis=1)[:8]


def pack_kernel(devices, info_ref, modes_ref, state_ref, now_ref, old_ref, *out_refs):
    comps, points, columns = state_ref.shape
    share = columns // devices
    wave = wave_row(modes_ref[...]).reshape(1, 1, columns)
    state = state_ref[...]
    forcing = RK_GAMMA * now_ref[...] + RK_ZETA * old_ref[...]
    local = state + TIME_STEP * (forcing - RK_ALPHA * (wave * state))
    rows = comps * points
    both = jnp.concatenate([state.reshape(rows, columns), local.reshape(rows, columns)], axis=0)
    placed = sum_parts(
        lax.dot_general(
            three_parts(both), selector(info_ref[0:1, :], columns), NT, preferred_element_type=F32
        )
    )
    for step, out in zip(steps_of(devices), out_refs):
        taken = placed[:, step * share : (step + 1) * share]
        for kind in range(2):
            for pair in range(comps // 2):
                real = (kind * comps + 2 * pair) * points
                imag = real + points
                out[kind, pair] = jnp.concatenate(
                    [taken[real : real + points], taken[imag : imag + points]], axis=1
                )


def operators_kernel(deriv_ref, inverse_ref, basis_ref, values_ref, deriv_out, inverse_out, basis_out, values_out):
    for source, target in ((deriv_ref, deriv_out), (inverse_ref, inverse_out), (basis_ref, basis_out)):
        high, low = two_parts(source[...])
        target[...] = jnp.concatenate([high, high, low], axis=1)
    lanes = values_out.shape[1]
    values_out[...] = jnp.transpose(jnp.broadcast_to(values_ref[...], (lanes, values_ref.shape[1])))


def apply(operator, x):
    high, low = two_parts(x)
    return jnp.dot(operator, jnp.concatenate([high, low, high], axis=0), preferred_element_type=F32)


def solve_kernel(devices, me_ref, wave_ref, values_ref, deriv_ref, inverse_ref, basis_ref, *refs):
    in_refs, refs = refs[:devices], refs[devices:]
    out_refs, (solved_ref, state, local, after) = refs[:devices], refs[devices:]
    me = me_ref[0]
    _, pairs, points, lanes = in_refs[0].shape
    for step, block in zip(steps_of(devices), in_refs):
        rows = pl.ds(pl.multiple_of((me ^ step) * points, points), points)
        for pair in range(pairs):
            state[rows, pair * lanes : (pair + 1) * lanes] = block[0, pair]
            local[rows, pair * lanes : (pair + 1) * lanes] = block[1, pair]
    rhs = local[...] + (TIME_STEP * RK_ALPHA) * apply(deriv_ref[...], state[...])
    project = apply(inverse_ref[...], rhs)
    damping = 1.0 + TIME_STEP * RK_BETA * (values_ref[...] + wave_ref[0:1, :])
    project = project / jnp.concatenate([damping] * pairs, axis=1)
    after[...] = apply(basis_ref[...], project)
    for pair in range(pairs):
        solved_ref[pair] = after[:, pair * lanes : (pair + 1) * lanes]
    for step, block in zip(steps_of(devices), out_refs):
        rows = pl.ds(pl.multiple_of((me ^ step) * points, points), points)
        for pair in range(pairs):
            block[pair] = after[rows, pair * lanes : (pair + 1) * lanes]


def unpack_kernel(devices, first, info_ref, *refs):
    in_refs, refs = refs[:devices], refs[devices:]
    if not first:
        refs = refs[1:]
    state_ref, out_refs = refs[0], refs[1:]
    pairs, points, lanes = in_refs[0].shape
    share = lanes // 2
    columns = devices * share
    order = steps_of(devices)
    blocks = [in_refs[order.index(step)] for step in range(devices)]
    got = []
    for pair in range(pairs):
        for half in range(2):
            got.append(
                jnp.concatenate(
                    [block[pair][:, half * share : (half + 1) * share] for block in blocks], axis=1
                )
            )
    got = jnp.concatenate(got, axis=0)
    state = sum_parts(
        jnp.dot(three_parts(got), selector(info_ref[0:1, :], columns), preferred_element_type=F32)
    )
    state_ref[...] = state.reshape(2 * pairs, points, columns)
    extra = sum_parts(
        lax.dot_general(
            three_parts(state), selector(info_ref[1:2, :], columns), NT, preferred_element_type=F32
        )
    )
    for step, out in zip(steps_of(devices), out_refs):
        taken = extra[:, step * share : (step + 1) * share]
        for pair in range(pairs):
            real = 2 * pair * points
            imag = real + points
            out[pair] = jnp.concatenate([taken[real : real + points], taken[imag : imag + points]], axis=1)


def emf_kernel(modes_ref, velocity_ref, state_ref, later_ref, emf_ref):
    _, points, columns = state_ref.shape
    weight = jnp.where(modes_ref[0:1, :] > 0, 2.0, 1.0).astype(F32)
    totals = [jnp.zeros((points, columns), F32)] * 3
    for field in range(3):
        real = weight * state_ref[2 * field]
        imag = weight * state_ref[2 * field + 1]
        for sign, i, j in ((1.0, (field + 1) % 3, (field + 2) % 3), (-1.0, (field + 2) % 3, (field + 1) % 3)):
            totals[i] = totals[i] + sign * (velocity_ref[2 * j] * real + velocity_ref[2 * j + 1] * imag)
    rows = []
    for total in totals:
        folded = total[:, :LANES]
        for at in range(1, columns // LANES):
            folded = folded + total[:, at * LANES : (at + 1) * LANES]
        rows.append(jnp.sum(jnp.transpose(folded), axis=0, keepdims=True))
    emf_ref[...] = jnp.concatenate(rows, axis=0)


def assemble_kernel(devices, first, me_ref, info_ref, solved_ref, *refs):
    in_refs, refs = refs[:devices], refs[devices:]
    if not first:
        refs = refs[1:]
    (out_ref,) = refs
    me = me_ref[0]
    pairs, points, lanes = in_refs[0].shape
    share = lanes // 2
    depth = solved_ref.shape[1]
    used = lax.broadcasted_iota(jnp.int32, (depth, share), 1) < info_ref[2:3, :share]
    for pair in range(pairs):
        for half in range(2):
            kept = jnp.where(used, solved_ref[pair][:, half * share : (half + 1) * share], 0.0)
            out_ref[2 * pair + half, :, :share] = kept
            for step, block in zip(steps_of(devices), in_refs):
                rows = pl.ds(pl.multiple_of((me ^ step) * points, points), points)
                out_ref[2 * pair + half, rows, share:] = block[pair][:, half * share : (half + 1) * share]


def steps_of(devices):
    return [0] + sorted(range(1, devices), key=lambda step: -((step.bit_length() << 16) + (step >> 1 << 1)))


def exchange(blocks):
    devices = len(blocks)
    return [
        block if step == 0 else lax.ppermute(block, "col", [(i, i ^ step) for i in range(devices)])
        for step, block in zip(steps_of(devices), blocks)
    ]


def sum_over_groups(value):
    groups = lax.axis_size("grp")
    terms = [value] + [
        lax.ppermute(value, "grp", [(i, i ^ step) for i in range(groups)]) for step in range(1, groups)
    ]
    while len(terms) > 1:
        terms = [terms[at] + terms[at + 1] for at in range(0, len(terms), 2)]
    return terms[0]


def on_device(
    state_now,
    force_now,
    force_old,
    velocity,
    second_deriv,
    eig_basis,
    eig_inverse,
    eig_values,
    kept_modes,
    col_owner,
):
    comps, points, columns = state_now.shape
    devices = lax.axis_size("col")
    depth = devices * points
    share = columns // devices
    lanes = 2 * share
    pairs = GROUPS
    chunks = comps // (2 * pairs)
    me = lax.axis_index("col").astype(jnp.int32).reshape(1)
    owner = col_owner.reshape(1, columns)

    info, wave = call(
        functools.partial(plan_kernel, devices),
        [shaped((8, columns), jnp.int32), shaped((8, lanes))],
        [scalar(), whole((1, columns)), whole((2, columns))],
        [whole((8, columns)), whole((8, lanes))],
        1000000,
        100000,
    )(me, owner, kept_modes)

    field = (2 * pairs, points, columns)
    sent = (2, pairs, points, lanes)
    back = (pairs, points, lanes)
    moved = 4 * 2 * pairs * points * columns

    forward = []
    for chunk in range(chunks):
        forward.append(
            exchange(
                call(
                    functools.partial(pack_kernel, devices),
                    [shaped(sent)] * devices,
                    [whole((8, columns)), whole((2, columns))] + [part(field, chunk)] * 3,
                    [whole(sent)] * devices,
                    12 * 2 * pairs * points * columns * columns,
                    5 * moved,
                )(info, kept_modes, state_now, force_now, force_old)
            )
        )

    operator = shaped((depth, 3 * depth), BF16)
    operators = call(
        operators_kernel,
        [operator, operator, operator, shaped((depth, lanes))],
        [whole((depth, depth))] * 3 + [whole((1, depth))],
        [whole((depth, 3 * depth))] * 3 + [whole((depth, lanes))],
        1000000,
        30 * depth * depth,
    )(second_deriv, eig_inverse, eig_basis, eig_values.reshape(1, depth))
    values = operators[3]

    solved, returned = [], []
    for chunk in range(chunks):
        width = pairs * lanes
        outs = call(
            functools.partial(solve_kernel, devices),
            [shaped(back)] * devices + [shaped((pairs, depth, lanes))],
            [scalar(), whole((8, lanes)), whole((depth, lanes))]
            + [whole((depth, 3 * depth))] * 3
            + [whole(sent)] * devices,
            [whole(back)] * devices + [whole((pairs, depth, lanes))],
            18 * depth * depth * width,
            18 * depth * depth + 16 * depth * width,
            [pltpu.VMEM((depth, width), F32)] * 3,
        )(me, wave, values, *operators[:3], *forward[chunk])
        solved.append(outs[devices])
        returned.append(exchange(outs[:devices]))

    state_next, extra = None, []
    for chunk in range(chunks):
        first = chunk == 0
        outs = call(
            functools.partial(unpack_kernel, devices, first),
            [shaped(state_now.shape)] + [shaped(back)] * devices,
            [whole((8, columns))] + [whole(back)] * devices + ([] if first else [untouched()]),
            [part(field, chunk)] + [whole(back)] * devices,
            12 * 2 * pairs * points * columns * columns,
            6 * moved,
            aliases={} if first else {1 + devices: 0},
        )(info, *returned[chunk], *([] if first else [state_next]))
        state_next = outs[0]
        extra.append(exchange(outs[1:]))
    emf = call(
        emf_kernel,
        shaped((3, points)),
        [whole((2, columns)), whole(velocity.shape), whole(velocity.shape), untouched()],
        whole((3, points)),
        30 * comps * points * columns,
        8 * comps * points * columns,
    )(kept_modes, velocity, state_next, extra[-1][1 + devices // 2])
    mean_emf = sum_over_groups(emf)

    owned = None
    for chunk in range(chunks):
        first = chunk == 0
        owned = call(
            functools.partial(assemble_kernel, devices, first),
            shaped((comps, depth, lanes)),
            [scalar(), whole((8, columns)), whole((pairs, depth, lanes))]
            + [whole(back)] * devices
            + ([] if first else [untouched()]),
            part((2 * pairs, depth, lanes), chunk),
            1000000,
            16 * pairs * depth * lanes,
            aliases={} if first else {3 + devices: 0},
        )(me, info, solved[chunk], *extra[chunk], *([] if first else [owned]))
    return (state_next, owned, mean_emf)


def solution(mesh):
    return jax.shard_map(
        on_device,
        mesh=mesh,
        in_specs=(
            P(None, "col", "grp"),
            P(None, "col", "grp"),
            P(None, "col", "grp"),
            P(None, "col", "grp"),
            P(),
            P(),
            P(),
            P(),
            P(None, "grp"),
            P("grp", None),
        ),
        out_specs=(P(None, "col", "grp"), P(None, None, ("grp", "col")), P(None, "col")),
        check_vma=False,
    )
```

```python
import functools

import jax
import jax.numpy as jnp
from jax import lax
from jax.experimental import pallas as pl
from jax.experimental.pallas import tpu as pltpu
from jax.sharding import PartitionSpec as P

KMAX = 2048
TIME_STEP = 2.0
RK_ALPHA = -3.0 / 40.0
RK_BETA = 5.0 / 24.0
RK_GAMMA = 5.0 / 12.0
RK_ZETA = -17.0 / 60.0
WAVE_SCALE = 8.0
VMEM_LIMIT = 24 * 1024 * 1024
CHUNKS = (2, 1)
LANES = 128
HEAVY = 10

F32 = jnp.float32
BF16 = jnp.bfloat16


def call(body, out_shape, in_specs, out_specs, weight, scratch=(), aliases=None):
    return pl.pallas_call(
        body,
        out_shape=out_shape,
        in_specs=in_specs,
        out_specs=out_specs,
        scratch_shapes=list(scratch),
        input_output_aliases=aliases or {},
        cost_estimate=pl.CostEstimate(flops=weight * 10**9, bytes_accessed=weight * 10**6, transcendentals=0),
        compiler_params=pltpu.CompilerParams(vmem_limit_bytes=VMEM_LIMIT),
    )


LOCAL = pl.BlockSpec(memory_space=pltpu.VMEM)
SCALAR = pl.BlockSpec(memory_space=pltpu.SMEM)
FAR = pl.BlockSpec(memory_space=pltpu.HBM)
ANYWHERE = pl.BlockSpec(memory_space=pl.ANY)


def shaped(shape, dtype=F32):
    return jax.ShapeDtypeStruct(shape, dtype)


def three_parts(x):
    high = x.astype(BF16)
    rest = x - high.astype(F32)
    middle = rest.astype(BF16)
    low = (rest - middle.astype(F32)).astype(BF16)
    return jnp.concatenate([high, middle, low], axis=0)


def sum_parts(x):
    rows = x.shape[0] // 3
    return x[:rows] + x[rows : 2 * rows] + x[2 * rows :]


def two_parts(x):
    high = x.astype(BF16)
    low = (x - high.astype(F32)).astype(BF16)
    return high, low


def selector(places, rows):
    columns = places.shape[1]
    return (lax.broadcasted_iota(jnp.int32, (rows, columns), 0) == places).astype(F32).astype(BF16)


def wave_row(modes):
    wave_x = modes[0:1, :].astype(F32)
    wave_z = modes[1:2, :].astype(F32)
    return (wave_x * wave_x + wave_z * wave_z) * (WAVE_SCALE / (KMAX * KMAX))


NT = (((1,), (1,)), ((), ()))


def plan(devices, me, owner, modes):
    columns = owner.shape[1]
    share = columns // devices
    rows = -(-devices // 8) * 8
    owned = (lax.broadcasted_iota(jnp.int32, (rows, columns), 0) == owner).astype(F32)
    before = (
        lax.broadcasted_iota(jnp.int32, (LANES, LANES), 0) < lax.broadcasted_iota(jnp.int32, (LANES, LANES), 1)
    ).astype(F32)
    carry = jnp.zeros((rows, 1), F32)
    earlier = []
    for at in range(columns // LANES):
        block = owned[:, at * LANES : (at + 1) * LANES]
        earlier.append(jnp.dot(block, before, preferred_element_type=F32) + carry)
        carry = carry + jnp.sum(block, axis=1, keepdims=True)
    counts = carry
    rank = jnp.sum(owned * jnp.concatenate(earlier, axis=1), axis=0, keepdims=True)
    surplus = jnp.maximum(counts - share, 0.0)
    lower = (lax.broadcasted_iota(jnp.int32, (rows, columns), 0) < owner).astype(F32)
    number = jnp.sum(lower * surplus, axis=0, keepdims=True) + (rank - share)
    free = share - jnp.minimum(counts, share)
    start = jnp.zeros((1, 1), F32)
    solver = owner
    slot = rank
    beyond = rank >= share
    for device in range(devices):
        here = free[device : device + 1, :]
        inside = beyond & (number >= start) & (number < start + here)
        solver = jnp.where(inside, device, solver)
        slot = jnp.where(inside, share - here + number - start, slot)
        start = start + here
    place = (solver ^ me) * share + slot.astype(jnp.int32)
    extra = jnp.where(beyond, (owner ^ me) * share + rank.astype(jnp.int32) - share, -1)
    mine = jnp.sum((owner == me).astype(F32), axis=1, keepdims=True).astype(jnp.int32)
    info = jnp.concatenate(
        [place, extra, jnp.broadcast_to(mine, (1, columns)), jnp.zeros((5, columns), jnp.int32)], axis=0
    )
    wave = jnp.broadcast_to(wave_row(modes), (16, columns))
    picked = sum_parts(
        lax.dot_general(three_parts(wave), selector(place, share), NT, preferred_element_type=F32)
    )
    return info, jnp.concatenate([picked, picked], axis=1)[:8]


def pack(devices, points, wave, place, state, now, old, out_refs):
    comps, _, columns = state.shape
    share = columns // devices
    wave = wave.reshape(1, 1, columns)
    forcing = RK_GAMMA * now + RK_ZETA * old
    local = state + TIME_STEP * (forcing - RK_ALPHA * (wave * state))
    rows = comps * points
    both = jnp.concatenate([state.reshape(rows, columns), local.reshape(rows, columns)], axis=0)
    placed = sum_parts(
        lax.dot_general(three_parts(both), selector(place, columns), NT, preferred_element_type=F32)
    )
    for step, out in zip(steps_of(devices), out_refs):
        taken = placed[:, step * share : (step + 1) * share]
        for kind in range(2):
            for pair in range(comps // 2):
                real = (kind * comps + 2 * pair) * points
                imag = real + points
                out[kind, pair] = jnp.concatenate(
                    [taken[real : real + points], taken[imag : imag + points]], axis=1
                )


def first_kernel(
    devices, me_ref, owner_hbm, modes_hbm, state_hbm, now_hbm, old_hbm, info_ref, wave_ref, *refs
):
    out_refs, (owner_ref, modes_ref, state_ref, now_ref, old_ref, sems) = refs[:devices], refs[devices:]
    comps, points, _ = state_ref.shape
    copies = [
        pltpu.make_async_copy(source, target, sems.at[at])
        for at, (source, target) in enumerate(
            (
                (owner_hbm, owner_ref),
                (modes_hbm, modes_ref),
                (state_hbm.at[:comps], state_ref),
                (now_hbm.at[:comps], now_ref),
                (old_hbm.at[:comps], old_ref),
            )
        )
    ]
    for copy in copies:
        copy.start()
    copies[0].wait()
    copies[1].wait()
    info, wave = plan(devices, me_ref[0], owner_ref[...], modes_ref[...])
    info_ref[...] = info
    wave_ref[...] = wave
    for copy in copies[2:]:
        copy.wait()
    wave = wave_row(modes_ref[...])
    pack(devices, points, wave, info[0:1], state_ref[...], now_ref[...], old_ref[...], out_refs)


def pack_kernel(devices, done, info_ref, modes_ref, state_hbm, now_hbm, old_hbm, after_ref, *refs):
    out_refs, (state_ref, now_ref, old_ref, sems) = refs[:devices], refs[devices:]
    comps, points, _ = state_ref.shape
    copies = [
        pltpu.make_async_copy(source.at[done : done + comps], target, sems.at[at])
        for at, (source, target) in enumerate(
            ((state_hbm, state_ref), (now_hbm, now_ref), (old_hbm, old_ref))
        )
    ]
    for copy in copies:
        copy.start()
    for copy in copies:
        copy.wait()
    wave = wave_row(modes_ref[...])
    pack(devices, points, wave, info_ref[0:1, :], state_ref[...], now_ref[...], old_ref[...], out_refs)


def operators_kernel(deriv_ref, inverse_ref, basis_ref, values_ref, deriv_out, inverse_out, basis_out, values_out):
    for source, target in ((deriv_ref, deriv_out), (inverse_ref, inverse_out), (basis_ref, basis_out)):
        high, low = two_parts(source[...])
        target[...] = jnp.concatenate([high, high, low], axis=1)
    lanes = values_out.shape[1]
    values_out[...] = jnp.transpose(jnp.broadcast_to(values_ref[...], (lanes, values_ref.shape[1])))


def apply(operator, x):
    high, low = two_parts(x)
    return jnp.dot(operator, jnp.concatenate([high, low, high], axis=0), preferred_element_type=F32)


def solve_kernel(devices, me_ref, wave_ref, values_ref, deriv_ref, inverse_ref, basis_ref, *refs):
    in_refs, refs = refs[:devices], refs[devices:]
    out_refs, (solved_ref, state, local, after) = refs[-devices - 4 : -4], refs[-4:]
    me = me_ref[0]
    _, pairs, points, lanes = in_refs[0].shape
    for step, block in zip(steps_of(devices), in_refs):
        rows = pl.ds(pl.multiple_of((me ^ step) * points, points), points)
        for pair in range(pairs):
            state[rows, pair * lanes : (pair + 1) * lanes] = block[0, pair]
            local[rows, pair * lanes : (pair + 1) * lanes] = block[1, pair]
    rhs = local[...] + (TIME_STEP * RK_ALPHA) * apply(deriv_ref[...], state[...])
    project = apply(inverse_ref[...], rhs)
    damping = 1.0 + TIME_STEP * RK_BETA * (values_ref[...] + wave_ref[0:1, :])
    project = project / jnp.concatenate([damping] * pairs, axis=1)
    after[...] = apply(basis_ref[...], project)
    for pair in range(pairs):
        solved_ref[pair] = after[:, pair * lanes : (pair + 1) * lanes]
    for step, block in zip(steps_of(devices), out_refs):
        rows = pl.ds(pl.multiple_of((me ^ step) * points, points), points)
        for pair in range(pairs):
            block[pair] = after[rows, pair * lanes : (pair + 1) * lanes]


def unpack_kernel(devices, done, info_ref, *refs):
    in_refs, refs = refs[:devices], refs[devices:]
    if done:
        refs = refs[2:]
    state_hbm, out_refs, (state_ref, sem) = refs[0], refs[1:-2], refs[-2:]
    pairs, points, lanes = in_refs[0].shape
    share = lanes // 2
    columns = devices * share
    order = steps_of(devices)
    blocks = [in_refs[order.index(step)] for step in range(devices)]
    got = []
    for pair in range(pairs):
        for half in range(2):
            got.append(
                jnp.concatenate(
                    [block[pair][:, half * share : (half + 1) * share] for block in blocks], axis=1
                )
            )
    got = jnp.concatenate(got, axis=0)
    state = sum_parts(
        jnp.dot(three_parts(got), selector(info_ref[0:1, :], columns), preferred_element_type=F32)
    )
    state_ref[...] = state.reshape(2 * pairs, points, columns)
    copy = pltpu.make_async_copy(state_ref, state_hbm.at[done : done + 2 * pairs], sem)
    copy.start()
    extra = sum_parts(
        lax.dot_general(
            three_parts(state), selector(info_ref[1:2, :], columns), NT, preferred_element_type=F32
        )
    )
    for step, out in zip(steps_of(devices), out_refs):
        taken = extra[:, step * share : (step + 1) * share]
        for pair in range(pairs):
            real = 2 * pair * points
            imag = real + points
            out[pair] = jnp.concatenate([taken[real : real + points], taken[imag : imag + points]], axis=1)
    copy.wait()


def emf_kernel(modes_ref, velocity_ref, state_ref, later_ref, emf_ref):
    _, points, columns = state_ref.shape
    weight = jnp.where(modes_ref[0:1, :] > 0, 2.0, 1.0).astype(F32)
    totals = [jnp.zeros((points, columns), F32)] * 3
    for field in range(3):
        real = weight * state_ref[2 * field]
        imag = weight * state_ref[2 * field + 1]
        for sign, i, j in ((1.0, (field + 1) % 3, (field + 2) % 3), (-1.0, (field + 2) % 3, (field + 1) % 3)):
            totals[i] = totals[i] + sign * (velocity_ref[2 * j] * real + velocity_ref[2 * j + 1] * imag)
    rows = []
    for total in totals:
        folded = total[:, :LANES]
        for at in range(1, columns // LANES):
            folded = folded + total[:, at * LANES : (at + 1) * LANES]
        rows.append(jnp.sum(jnp.transpose(folded), axis=0, keepdims=True))
    emf_ref[...] = jnp.concatenate(rows, axis=0)


def assemble_kernel(devices, done, me_ref, info_ref, solved_ref, *refs):
    in_refs, refs = refs[:devices], refs[devices:]
    if done:
        refs = refs[1:]
    out_hbm, whole, sems = refs
    me = me_ref[0]
    pairs, points, lanes = in_refs[0].shape
    share = lanes // 2
    depth = solved_ref.shape[1]
    used = lax.broadcasted_iota(jnp.int32, (depth, share), 1) < info_ref[2:3, :share]
    copies = []
    for pair in range(pairs):
        for half in range(2):
            comp = 2 * pair + half
            kept = jnp.where(used, solved_ref[pair][:, half * share : (half + 1) * share], 0.0)
            whole[comp, :, :share] = kept
            for step, block in zip(steps_of(devices), in_refs):
                rows = pl.ds(pl.multiple_of((me ^ step) * points, points), points)
                whole[comp, rows, share:] = block[pair][:, half * share : (half + 1) * share]
            copies.append(pltpu.make_async_copy(whole.at[comp], out_hbm.at[done + comp], sems.at[comp]))
            copies[-1].start()
    for copy in copies:
        copy.wait()


def steps_of(devices):
    return [0] + sorted(range(1, devices), key=lambda step: -((step.bit_length() << 16) + (step >> 1 << 1)))


def exchange(blocks):
    devices = len(blocks)
    return [
        block if step == 0 else lax.ppermute(block, "col", [(i, i ^ step) for i in range(devices)])
        for step, block in zip(steps_of(devices), blocks)
    ]


def sum_over_groups(value):
    groups = lax.axis_size("grp")
    terms = [value] + [
        lax.ppermute(value, "grp", [(i, i ^ step) for i in range(groups)]) for step in range(1, groups)
    ]
    while len(terms) > 1:
        terms = [terms[at] + terms[at + 1] for at in range(0, len(terms), 2)]
    return terms[0]


def on_device(
    state_now,
    force_now,
    force_old,
    velocity,
    second_deriv,
    eig_basis,
    eig_inverse,
    eig_values,
    kept_modes,
    col_owner,
):
    comps, points, columns = state_now.shape
    devices = lax.axis_size("col")
    depth = devices * points
    share = columns // devices
    lanes = 2 * share
    starts = [2 * sum(CHUNKS[:at]) for at in range(len(CHUNKS))]
    me = lax.axis_index("col").astype(jnp.int32).reshape(1)
    owner = col_owner.reshape(1, columns)
    state_far, now_far, old_far, modes_far, owner_far = (
        pltpu.with_memory_space_constraint(array, pltpu.HBM)
        for array in (state_now, force_now, force_old, kept_modes, owner)
    )
    fields = (state_far, now_far, old_far)

    forward = []
    for pairs, done in zip(CHUNKS, starts):
        sent = [shaped((2, pairs, points, lanes))] * devices
        loaded = [pltpu.VMEM((2 * pairs, points, columns), F32)] * 3
        if done == 0:
            outs = call(
                functools.partial(first_kernel, devices),
                [shaped((8, columns), jnp.int32), shaped((8, lanes))] + sent,
                [SCALAR] + [FAR] * 5,
                [LOCAL] * (2 + devices),
                1,
                [pltpu.VMEM((1, columns), jnp.int32), pltpu.VMEM((2, columns), jnp.int32)]
                + loaded
                + [pltpu.SemaphoreType.DMA((5,))],
            )(me, owner_far, modes_far, *fields)
            info, wave = outs[:2]
            blocks = outs[2:]
        else:
            blocks = call(
                functools.partial(pack_kernel, devices, done),
                sent,
                [LOCAL] * 2 + [FAR] * 3 + [ANYWHERE],
                [LOCAL] * devices,
                HEAVY,
                loaded + [pltpu.SemaphoreType.DMA((3,))],
            )(info, kept_modes, *fields, forward[-1][3])
        forward.append(exchange(blocks))

    operator = shaped((depth, 3 * depth), BF16)
    operators = call(
        operators_kernel,
        [operator, operator, operator, shaped((depth, lanes))],
        [LOCAL] * 4,
        [LOCAL] * 4,
        HEAVY,
    )(second_deriv, eig_inverse, eig_basis, eig_values.reshape(1, depth))

    solved, returned = [], []
    for pairs, blocks in zip(CHUNKS, forward):
        width = pairs * lanes
        outs = call(
            functools.partial(solve_kernel, devices),
            [shaped((pairs, points, lanes))] * devices + [shaped((pairs, depth, lanes))],
            [SCALAR] + [LOCAL] * (5 + devices) + [ANYWHERE] * len(returned[-1:]),
            [LOCAL] * (devices + 1),
            HEAVY,
            [pltpu.VMEM((depth, width), F32)] * 3,
        )(me, wave, operators[3], *operators[:3], *blocks, *[sent[1] for sent in returned[-1:]])
        solved.append(outs[devices])
        returned.append(exchange(outs[:devices]))

    state_next, extra = None, []
    for pairs, done, blocks in zip(CHUNKS, starts, returned):
        outs = call(
            functools.partial(unpack_kernel, devices, done),
            [shaped(state_now.shape)] + [shaped((pairs, points, lanes))] * devices,
            [LOCAL] * (1 + devices) + ([FAR, ANYWHERE] if done else []),
            [FAR] + [LOCAL] * devices,
            HEAVY,
            [pltpu.VMEM((2 * pairs, points, columns), F32), pltpu.SemaphoreType.DMA],
            aliases={1 + devices: 0} if done else {},
        )(info, *blocks, *([state_next, extra[-1][1]] if done else []))
        state_next = outs[0]
        extra.append(exchange(outs[1:]))
    emf = call(
        emf_kernel, shaped((3, points)), [LOCAL] * 3 + [ANYWHERE], LOCAL, 1
    )(kept_modes, velocity, state_next, extra[-1][1])
    mean_emf = sum_over_groups(emf)

    owned = None
    for pairs, done, column, blocks in zip(CHUNKS, starts, solved, extra):
        owned = call(
            functools.partial(assemble_kernel, devices, done),
            shaped((comps, depth, lanes)),
            [SCALAR] + [LOCAL] * (2 + devices) + ([FAR] if done else []),
            FAR,
            1,
            [pltpu.VMEM((2 * pairs, depth, lanes), F32), pltpu.SemaphoreType.DMA((2 * pairs,))],
            aliases={3 + devices: 0} if done else {},
        )(me, info, column, *blocks, *([owned] if done else []))
    return (state_next, owned, mean_emf)


def solution(mesh):
    return jax.shard_map(
        on_device,
        mesh=mesh,
        in_specs=(
            P(None, "col", "grp"),
            P(None, "col", "grp"),
            P(None, "col", "grp"),
            P(None, "col", "grp"),
            P(),
            P(),
            P(),
            P(),
            P(None, "grp"),
            P("grp", None),
        ),
        out_specs=(P(None, "col", "grp"), P(None, None, ("grp", "col")), P(None, "col")),
        check_vma=False,
    )
```

```python
import functools

import jax
import jax.numpy as jnp
from jax import lax
from jax.experimental import pallas as pl
from jax.experimental.pallas import tpu as pltpu
from jax.sharding import PartitionSpec as P

KMAX = 2048
TIME_STEP = 2.0
RK_ALPHA = -3.0 / 40.0
RK_BETA = 5.0 / 24.0
RK_GAMMA = 5.0 / 12.0
RK_ZETA = -17.0 / 60.0
WAVE_SCALE = 8.0
VMEM_LIMIT = 24 * 1024 * 1024
PAIRS = 3
LANES = 128
HEAVY = 10

F32 = jnp.float32
BF16 = jnp.bfloat16


def call(body, out_shape, in_specs, out_specs, weight, scratch=(), aliases=None):
    return pl.pallas_call(
        body,
        out_shape=out_shape,
        in_specs=in_specs,
        out_specs=out_specs,
        scratch_shapes=list(scratch),
        input_output_aliases=aliases or {},
        cost_estimate=pl.CostEstimate(flops=weight * 10**9, bytes_accessed=weight * 10**6, transcendentals=0),
        compiler_params=pltpu.CompilerParams(vmem_limit_bytes=VMEM_LIMIT),
    )


LOCAL = pl.BlockSpec(memory_space=pltpu.VMEM)
SCALAR = pl.BlockSpec(memory_space=pltpu.SMEM)
FAR = pl.BlockSpec(memory_space=pltpu.HBM)
ANYWHERE = pl.BlockSpec(memory_space=pl.ANY)


def shaped(shape, dtype=F32):
    return jax.ShapeDtypeStruct(shape, dtype)


def three_parts(x):
    high = x.astype(BF16)
    rest = x - high.astype(F32)
    middle = rest.astype(BF16)
    low = (rest - middle.astype(F32)).astype(BF16)
    return jnp.concatenate([high, middle, low], axis=0)


def sum_parts(x):
    rows = x.shape[0] // 3
    return x[:rows] + x[rows : 2 * rows] + x[2 * rows :]


def two_parts(x):
    high = x.astype(BF16)
    low = (x - high.astype(F32)).astype(BF16)
    return high, low


def selector(places, rows):
    columns = places.shape[1]
    return (lax.broadcasted_iota(jnp.int32, (rows, columns), 0) == places).astype(F32).astype(BF16)


def wave_row(modes):
    wave_x = modes[0:1, :].astype(F32)
    wave_z = modes[1:2, :].astype(F32)
    return (wave_x * wave_x + wave_z * wave_z) * (WAVE_SCALE / (KMAX * KMAX))


NT = (((1,), (1,)), ((), ()))


def plan(devices, me, owner, modes):
    columns = owner.shape[1]
    share = columns // devices
    rows = -(-devices // 8) * 8
    owned = (lax.broadcasted_iota(jnp.int32, (rows, columns), 0) == owner).astype(F32)
    before = (
        lax.broadcasted_iota(jnp.int32, (LANES, LANES), 0) < lax.broadcasted_iota(jnp.int32, (LANES, LANES), 1)
    ).astype(F32)
    carry = jnp.zeros((rows, 1), F32)
    earlier = []
    for at in range(columns // LANES):
        block = owned[:, at * LANES : (at + 1) * LANES]
        earlier.append(jnp.dot(block, before, preferred_element_type=F32) + carry)
        carry = carry + jnp.sum(block, axis=1, keepdims=True)
    counts = carry
    rank = jnp.sum(owned * jnp.concatenate(earlier, axis=1), axis=0, keepdims=True)
    surplus = jnp.maximum(counts - share, 0.0)
    lower = (lax.broadcasted_iota(jnp.int32, (rows, columns), 0) < owner).astype(F32)
    number = jnp.sum(lower * surplus, axis=0, keepdims=True) + (rank - share)
    free = share - jnp.minimum(counts, share)
    start = jnp.zeros((1, 1), F32)
    solver = owner
    slot = rank
    beyond = rank >= share
    for device in range(devices):
        here = free[device : device + 1, :]
        inside = beyond & (number >= start) & (number < start + here)
        solver = jnp.where(inside, device, solver)
        slot = jnp.where(inside, share - here + number - start, slot)
        start = start + here
    place = (solver ^ me) * share + slot.astype(jnp.int32)
    extra = jnp.where(beyond, (owner ^ me) * share + rank.astype(jnp.int32) - share, -1)
    mine = jnp.sum((owner == me).astype(F32), axis=1, keepdims=True).astype(jnp.int32)
    info = jnp.concatenate(
        [place, extra, jnp.broadcast_to(mine, (1, columns)), jnp.zeros((5, columns), jnp.int32)], axis=0
    )
    wave = jnp.broadcast_to(wave_row(modes), (16, columns))
    picked = sum_parts(
        lax.dot_general(three_parts(wave), selector(place, share), NT, preferred_element_type=F32)
    )
    return info, jnp.concatenate([picked, picked], axis=1)[:8]


def pack(devices, wave, chosen, state, now, old, out_refs, pair):
    comps, points, columns = state.shape
    share = columns // devices
    wave = wave.reshape(1, 1, columns)
    forcing = RK_GAMMA * now + RK_ZETA * old
    local = state + TIME_STEP * (forcing - RK_ALPHA * (wave * state))
    rows = comps * points
    both = jnp.concatenate([state.reshape(rows, columns), local.reshape(rows, columns)], axis=0)
    placed = sum_parts(lax.dot_general(three_parts(both), chosen, NT, preferred_element_type=F32))
    for step, out in zip(steps_of(devices, points), out_refs):
        taken = placed[:, step * share : (step + 1) * share]
        for kind in range(2):
            real = 2 * kind * points
            imag = real + points
            out[kind, pair] = jnp.concatenate([taken[real : real + points], taken[imag : imag + points]], axis=1)


def first_kernel(
    devices, me_ref, owner_hbm, modes_hbm, state_hbm, now_hbm, old_hbm, info_ref, wave_ref, *refs
):
    out_refs, (owner_ref, modes_ref, state_ref, now_ref, old_ref, sems) = refs[:devices], refs[devices:]
    columns = owner_ref.shape[1]
    copies = [
        pltpu.make_async_copy(owner_hbm, owner_ref, sems.at[0]),
        pltpu.make_async_copy(modes_hbm, modes_ref, sems.at[1]),
    ]
    for pair in range(PAIRS):
        comps = slice(2 * pair, 2 * pair + 2)
        for at, (source, target) in enumerate(((state_hbm, state_ref), (now_hbm, now_ref), (old_hbm, old_ref))):
            copies.append(
                pltpu.make_async_copy(source.at[comps], target.at[comps], sems.at[2 + 3 * pair + at])
            )
    for copy in copies:
        copy.start()
    copies[0].wait()
    copies[1].wait()
    info, wave = plan(devices, me_ref[0], owner_ref[...], modes_ref[...])
    info_ref[...] = info
    wave_ref[...] = wave
    wave = wave_row(modes_ref[...])
    chosen = selector(info[0:1], columns)
    for pair in range(PAIRS):
        for copy in copies[2 + 3 * pair : 5 + 3 * pair]:
            copy.wait()
        comps = slice(2 * pair, 2 * pair + 2)
        pack(devices, wave, chosen, state_ref[comps], now_ref[comps], old_ref[comps], out_refs, pair)


def operators_kernel(
    deriv_ref, inverse_ref, basis_ref, values_ref, high_out, low_out, both_high_out, both_low_out, basis_out, values_out
):
    high, low = two_parts(inverse_ref[...])
    high_out[...] = high
    low_out[...] = low
    both = (TIME_STEP * RK_ALPHA) * apply(jnp.concatenate([high, high, low], axis=1), deriv_ref[...])
    high, low = two_parts(both)
    both_high_out[...] = high
    both_low_out[...] = low
    high, low = two_parts(basis_ref[...])
    basis_out[...] = jnp.concatenate([high, high, low], axis=1)
    lanes = values_out.shape[1]
    values_out[...] = jnp.transpose(jnp.broadcast_to(values_ref[...], (lanes, values_ref.shape[1])))


def apply(operator, x):
    high, low = two_parts(x)
    return jnp.dot(operator, jnp.concatenate([high, low, high], axis=0), preferred_element_type=F32)


def projected(me, operators, steps, blocks, state, local):
    _, pairs, points, lanes = blocks[0].shape
    fill = LANES // points
    for at, (step, block) in enumerate(zip(steps, blocks)):
        first = at // fill * LANES
        rows = pl.ds(pl.multiple_of(first + ((me ^ step) % fill) * points, points), points)
        for pair in range(pairs):
            state[rows, pair * lanes : (pair + 1) * lanes] = block[0, pair]
            local[rows, pair * lanes : (pair + 1) * lanes] = block[1, pair]
    high, low, both_high, both_low = operators
    matrix, values = [], []
    for first in range(0, len(steps), fill):
        depth = pl.ds(pl.multiple_of((me ^ steps[first]) // fill * LANES, LANES), LANES)
        rows = slice(first // fill * LANES, (first // fill + 1) * LANES)
        for upper, lower, x in ((high, low, local), (both_high, both_low, state)):
            x_high, x_low = two_parts(x[rows, :])
            matrix += [upper[:, depth], upper[:, depth], lower[:, depth]]
            values += [x_high, x_low, x_high]
    return jnp.dot(
        jnp.concatenate(matrix, axis=1), jnp.concatenate(values, axis=0), preferred_element_type=F32
    )


def solve_early_kernel(steps, me_ref, *refs):
    operators, in_refs, (out_ref, state, local) = refs[:4], refs[4:-3], refs[-3:]
    out_ref[...] = projected(me_ref[0], operators, steps, in_refs, state, local)


def solve_late_kernel(steps, order, me_ref, wave_ref, values_ref, basis_ref, early_ref, *refs):
    operators, refs = refs[:4], refs[4:]
    in_refs, refs = refs[: len(steps)], refs[len(steps) :]
    out_refs, (solved_ref, state, local, after) = refs[:-4], refs[-4:]
    me = me_ref[0]
    pairs, points, lanes = out_refs[0].shape
    project = early_ref[...] + projected(me, operators, steps, in_refs, state, local)
    damping = 1.0 + TIME_STEP * RK_BETA * (values_ref[...] + wave_ref[0:1, :])
    project = project / jnp.concatenate([damping] * pairs, axis=1)
    after[...] = apply(basis_ref[...], project)
    for pair in range(pairs):
        solved_ref[pair] = after[:, pair * lanes : (pair + 1) * lanes]
    for step, block in zip(order, out_refs):
        rows = pl.ds(pl.multiple_of((me ^ step) * points, points), points)
        for pair in range(pairs):
            block[pair] = after[rows, pair * lanes : (pair + 1) * lanes]


def side_by_side(steps, blocks):
    pairs, _, lanes = blocks[0].shape
    share = lanes // 2
    sorted_blocks = [blocks[steps.index(step)] for step in sorted(steps)]
    rows = []
    for pair in range(pairs):
        for half in range(2):
            rows.append(
                jnp.concatenate(
                    [block[pair][:, half * share : (half + 1) * share] for block in sorted_blocks], axis=1
                )
            )
    return jnp.concatenate(rows, axis=0)


def surplus_early_kernel(steps, info_ref, *refs):
    in_refs, (out_ref, late_ref) = refs[:-2], refs[-2:]
    columns = info_ref.shape[1]
    share = in_refs[0].shape[2] // 2
    chosen = lax.dot_general(
        selector(info_ref[0:1, :], columns), selector(info_ref[1:2, :], columns), NT, preferred_element_type=F32
    ).astype(BF16)
    devices = columns // share
    late = [step for step in range(devices) if step not in steps]
    first, last = late[0] * share, (late[-1] + 1) * share
    late_ref[...] = chosen[first:last]
    kept = jnp.concatenate([chosen[:first], chosen[last:]], axis=0)
    out_ref[...] = sum_parts(
        jnp.dot(three_parts(side_by_side(steps, in_refs)), kept, preferred_element_type=F32)
    )


def surplus_late_kernel(steps, order, early_ref, chosen_ref, *refs):
    in_refs, out_refs = refs[: len(steps)], refs[len(steps) :]
    pairs, points, lanes = in_refs[0].shape
    share = lanes // 2
    extra = early_ref[...] + sum_parts(
        jnp.dot(three_parts(side_by_side(steps, in_refs)), chosen_ref[...], preferred_element_type=F32)
    )
    for step, out in zip(order, out_refs):
        taken = extra[:, step * share : (step + 1) * share]
        for pair in range(pairs):
            real = 2 * pair * points
            imag = real + points
            out[pair] = jnp.concatenate([taken[real : real + points], taken[imag : imag + points]], axis=1)


def state_kernel(order, info_ref, modes_ref, velocity_ref, *refs):
    in_refs, (_, state_hbm, emf_ref, state_ref, sem) = refs[: len(order)], refs[len(order) :]
    comps, points, columns = state_ref.shape
    state = sum_parts(
        jnp.dot(
            three_parts(side_by_side(order, in_refs)),
            selector(info_ref[0:1, :], columns),
            preferred_element_type=F32,
        )
    )
    state_ref[...] = state.reshape(comps, points, columns)
    copy = pltpu.make_async_copy(state_ref, state_hbm, sem)
    copy.start()
    emf_ref[...] = emf_of(modes_ref[...], velocity_ref, state_ref)
    copy.wait()


def emf_of(modes, velocity_ref, state_ref):
    _, points, columns = state_ref.shape
    weight = jnp.where(modes[0:1, :] > 0, 2.0, 1.0).astype(F32)
    totals = [jnp.zeros((points, columns), F32)] * 3
    for field in range(3):
        real = weight * state_ref[2 * field]
        imag = weight * state_ref[2 * field + 1]
        for sign, i, j in ((1.0, (field + 1) % 3, (field + 2) % 3), (-1.0, (field + 2) % 3, (field + 1) % 3)):
            totals[i] = totals[i] + sign * (velocity_ref[2 * j] * real + velocity_ref[2 * j + 1] * imag)
    rows = []
    for total in totals:
        folded = total[:, :LANES]
        for at in range(1, columns // LANES):
            folded = folded + total[:, at * LANES : (at + 1) * LANES]
        rows.append(jnp.sum(jnp.transpose(folded), axis=0, keepdims=True))
    return jnp.concatenate(rows, axis=0)


def assemble(me, steps, used, solved_ref, in_refs, out_hbm, rows_ref, sems):
    pairs, points, lanes = in_refs[0].shape
    share = lanes // 2
    fill = LANES // points
    copies = []
    for first in range(0, len(steps), fill):
        depth = pl.ds(pl.multiple_of((me ^ steps[first]) // fill * LANES, LANES), LANES)
        rows = slice(first // fill * LANES, (first // fill + 1) * LANES)
        for pair in range(pairs):
            solved = solved_ref[pair, depth, :]
            for half in range(2):
                comp = 2 * pair + half
                kept = solved[:, half * share : (half + 1) * share]
                rows_ref[comp, rows, :share] = jnp.where(used < 0, 0.0, kept)
                for at in range(first, first + fill):
                    place = pl.ds(
                        pl.multiple_of(first // fill * LANES + ((me ^ steps[at]) % fill) * points, points), points
                    )
                    rows_ref[comp, place, share:] = in_refs[at][pair][:, half * share : (half + 1) * share]
                copies.append(
                    pltpu.make_async_copy(
                        rows_ref.at[comp, rows], out_hbm.at[comp, depth], sems.at[first // fill * 2 * pairs + comp]
                    )
                )
                copies[-1].start()
    for copy in copies:
        copy.wait()


def unused(info_ref, share):
    lane = lax.broadcasted_iota(jnp.int32, (LANES, share), 1)
    return jnp.where(lane < info_ref[2:3, :share], 0, -1)


def assemble_early_kernel(steps, me_ref, info_ref, solved_ref, *refs):
    in_refs, (out_hbm, rows_ref, sems) = refs[: len(steps)], refs[len(steps) :]
    share = in_refs[0].shape[2] // 2
    assemble(me_ref[0], steps, unused(info_ref, share), solved_ref, in_refs, out_hbm, rows_ref, sems)


def assemble_late_kernel(steps, terms, me_ref, info_ref, solved_ref, *refs):
    in_refs, refs = refs[: len(steps)], refs[len(steps) :]
    parts, (_, out_hbm, emf_ref, rows_ref, sems) = refs[:terms], refs[terms:]
    parts = [ref[...] for ref in parts]
    while len(parts) > 1:
        parts = [parts[at] + parts[at + 1] for at in range(0, len(parts), 2)]
    emf_ref[...] = parts[0]
    share = in_refs[0].shape[2] // 2
    assemble(me_ref[0], steps, unused(info_ref, share), solved_ref, in_refs, out_hbm, rows_ref, sems)


def late_steps(devices, points):
    return list(range(devices // 2, devices // 2 + LANES // points))


def early_steps(devices, points):
    half = devices // 2
    return list(range(half + LANES // points, devices)) + list(range(half))


def steps_of(devices, points):
    return early_steps(devices, points) + late_steps(devices, points)


def exchange(blocks, steps):
    devices = len(blocks)
    return [
        block if step == 0 else lax.ppermute(block, "col", [(i, i ^ step) for i in range(devices)])
        for step, block in zip(steps, blocks)
    ]


def from_groups(value):
    groups = lax.axis_size("grp")
    return [value] + [
        lax.ppermute(value, "grp", [(i, i ^ step) for i in range(groups)]) for step in range(1, groups)
    ]


def on_device(
    state_now,
    force_now,
    force_old,
    velocity,
    second_deriv,
    eig_basis,
    eig_inverse,
    eig_values,
    kept_modes,
    col_owner,
):
    comps, points, columns = state_now.shape
    devices = lax.axis_size("col")
    depth = devices * points
    share = columns // devices
    lanes = 2 * share
    width = PAIRS * lanes
    steps = steps_of(devices, points)
    early, late = early_steps(devices, points), late_steps(devices, points)
    split = len(early)
    early_rows, late_rows = split * points, len(late) * points
    back = [shaped((PAIRS, points, lanes))] * devices
    me = lax.axis_index("col").astype(jnp.int32).reshape(1)
    far = [
        pltpu.with_memory_space_constraint(array, pltpu.HBM)
        for array in (col_owner.reshape(1, columns), kept_modes, state_now, force_now, force_old)
    ]

    outs = call(
        functools.partial(first_kernel, devices),
        [shaped((8, columns), jnp.int32), shaped((8, lanes))] + [shaped((2, PAIRS, points, lanes))] * devices,
        [SCALAR] + [FAR] * 5,
        [LOCAL] * (2 + devices),
        1,
        [pltpu.VMEM((1, columns), jnp.int32), pltpu.VMEM((2, columns), jnp.int32)]
        + [pltpu.VMEM((comps, points, columns), F32)] * 3
        + [pltpu.SemaphoreType.DMA((2 + 3 * PAIRS,))],
    )(me, *far)
    info, wave = outs[:2]
    forward = exchange(outs[2:], steps)

    square = shaped((depth, depth), BF16)
    operators = call(
        operators_kernel,
        [square] * 4 + [shaped((depth, 3 * depth), BF16), shaped((depth, lanes))],
        [LOCAL] * 4,
        [LOCAL] * 6,
        HEAVY,
    )(second_deriv, eig_inverse, eig_basis, eig_values.reshape(1, depth))
    basis, values = operators[4:]

    begun = call(
        functools.partial(solve_early_kernel, early),
        shaped((depth, width)),
        [SCALAR] + [LOCAL] * (4 + split),
        LOCAL,
        HEAVY,
        [pltpu.VMEM((early_rows, width), F32)] * 2,
    )(me, *operators[:4], *forward[:split])
    outs = call(
        functools.partial(solve_late_kernel, late, steps),
        back + [shaped((PAIRS, depth, lanes))],
        [SCALAR] + [LOCAL] * (8 + len(late)),
        [LOCAL] * (devices + 1),
        1,
        [pltpu.VMEM((late_rows, width), F32)] * 2 + [pltpu.VMEM((depth, width), F32)],
    )(me, wave, values, basis, begun, *operators[:4], *forward[split:])
    solved = outs[devices]
    returned = exchange(outs[:devices], steps)

    begun, chosen = call(
        functools.partial(surplus_early_kernel, early),
        [shaped((comps * points, columns)), shaped((len(late) * share, columns), BF16)],
        [LOCAL] * (1 + split),
        [LOCAL] * 2,
        HEAVY,
    )(info, *returned[:split])
    outs = call(
        functools.partial(surplus_late_kernel, late, steps),
        back,
        [LOCAL] * (2 + len(late)),
        [LOCAL] * devices,
        1,
    )(begun, chosen, *returned[split:])
    extra = exchange(outs, steps)

    state_next, emf = call(
        functools.partial(state_kernel, steps),
        [shaped(state_now.shape), shaped((3, points))],
        [LOCAL] * (3 + devices) + [ANYWHERE],
        [FAR, LOCAL],
        HEAVY,
        [pltpu.VMEM(state_now.shape, F32), pltpu.SemaphoreType.DMA],
    )(info, kept_modes, velocity, *returned, extra[split])
    terms = from_groups(emf)

    owned = call(
        functools.partial(assemble_early_kernel, early),
        shaped((comps, depth, lanes)),
        [SCALAR] + [LOCAL] * (2 + split),
        FAR,
        HEAVY,
        [
            pltpu.VMEM((comps, early_rows, lanes), F32),
            pltpu.SemaphoreType.DMA((comps * early_rows // LANES,)),
        ],
    )(me, info, solved, *extra[:split])
    owned, mean_emf = call(
        functools.partial(assemble_late_kernel, late, len(terms)),
        [shaped((comps, depth, lanes)), shaped((3, points))],
        [SCALAR] + [LOCAL] * (2 + len(late) + len(terms)) + [FAR],
        [FAR, LOCAL],
        1,
        [pltpu.VMEM((comps, late_rows, lanes), F32), pltpu.SemaphoreType.DMA((comps,))],
        aliases={3 + len(late) + len(terms): 0},
    )(me, info, solved, *extra[split:], *terms, owned)
    return (state_next, owned, mean_emf)


def solution(mesh):
    return jax.shard_map(
        on_device,
        mesh=mesh,
        in_specs=(
            P(None, "col", "grp"),
            P(None, "col", "grp"),
            P(None, "col", "grp"),
            P(None, "col", "grp"),
            P(),
            P(),
            P(),
            P(),
            P(None, "grp"),
            P("grp", None),
        ),
        out_specs=(P(None, "col", "grp"), P(None, None, ("grp", "col")), P(None, "col")),
        check_vma=False,
    )
```

```python
import functools

import jax
import jax.numpy as jnp
from jax import lax
from jax.experimental import pallas as pl
from jax.experimental.pallas import tpu as pltpu
from jax.sharding import PartitionSpec as P

KMAX = 2048
TIME_STEP = 2.0
RK_ALPHA = -3.0 / 40.0
RK_BETA = 5.0 / 24.0
RK_GAMMA = 5.0 / 12.0
RK_ZETA = -17.0 / 60.0
WAVE_SCALE = 8.0
VMEM_LIMIT = 24 * 1024 * 1024
PAIRS = 3
LANES = 128
HEAVY = 10

F32 = jnp.float32
BF16 = jnp.bfloat16


def call(body, out_shape, in_specs, out_specs, weight, scratch=(), aliases=None):
    return pl.pallas_call(
        body,
        out_shape=out_shape,
        in_specs=in_specs,
        out_specs=out_specs,
        scratch_shapes=list(scratch),
        input_output_aliases=aliases or {},
        cost_estimate=pl.CostEstimate(flops=weight * 10**9, bytes_accessed=weight * 10**6, transcendentals=0),
        compiler_params=pltpu.CompilerParams(vmem_limit_bytes=VMEM_LIMIT),
    )


LOCAL = pl.BlockSpec(memory_space=pltpu.VMEM)
SCALAR = pl.BlockSpec(memory_space=pltpu.SMEM)
FAR = pl.BlockSpec(memory_space=pltpu.HBM)
ANYWHERE = pl.BlockSpec(memory_space=pl.ANY)


def shaped(shape, dtype=F32):
    return jax.ShapeDtypeStruct(shape, dtype)


def three_parts(x):
    high = x.astype(BF16)
    rest = x - high.astype(F32)
    middle = rest.astype(BF16)
    low = (rest - middle.astype(F32)).astype(BF16)
    return jnp.concatenate([high, middle, low], axis=0)


def sum_parts(x):
    rows = x.shape[0] // 3
    return x[:rows] + x[rows : 2 * rows] + x[2 * rows :]


def two_parts(x):
    high = x.astype(BF16)
    low = (x - high.astype(F32)).astype(BF16)
    return high, low


def selector(places, rows):
    columns = places.shape[1]
    return (lax.broadcasted_iota(jnp.int32, (rows, columns), 0) == places).astype(F32).astype(BF16)


def wave_row(modes):
    wave_x = modes[0:1, :].astype(F32)
    wave_z = modes[1:2, :].astype(F32)
    return (wave_x * wave_x + wave_z * wave_z) * (WAVE_SCALE / (KMAX * KMAX))


NT = (((1,), (1,)), ((), ()))


def plan(devices, me, owner, modes):
    columns = owner.shape[1]
    share = columns // devices
    rows = -(-devices // 8) * 8
    owned = (lax.broadcasted_iota(jnp.int32, (rows, columns), 0) == owner).astype(F32)
    before = (
        lax.broadcasted_iota(jnp.int32, (LANES, LANES), 0) < lax.broadcasted_iota(jnp.int32, (LANES, LANES), 1)
    ).astype(F32)
    carry = jnp.zeros((rows, 1), F32)
    earlier = []
    for at in range(columns // LANES):
        block = owned[:, at * LANES : (at + 1) * LANES]
        earlier.append(jnp.dot(block, before, preferred_element_type=F32) + carry)
        carry = carry + jnp.sum(block, axis=1, keepdims=True)
    counts = carry
    rank = jnp.sum(owned * jnp.concatenate(earlier, axis=1), axis=0, keepdims=True)
    surplus = jnp.maximum(counts - share, 0.0)
    lower = (lax.broadcasted_iota(jnp.int32, (rows, columns), 0) < owner).astype(F32)
    number = jnp.sum(lower * surplus, axis=0, keepdims=True) + (rank - share)
    free = share - jnp.minimum(counts, share)
    start = jnp.zeros((1, 1), F32)
    solver = owner
    slot = rank
    beyond = rank >= share
    for device in range(devices):
        here = free[device : device + 1, :]
        inside = beyond & (number >= start) & (number < start + here)
        solver = jnp.where(inside, device, solver)
        slot = jnp.where(inside, share - here + number - start, slot)
        start = start + here
    place = (solver ^ me) * share + slot.astype(jnp.int32)
    extra = jnp.where(beyond, (owner ^ me) * share + rank.astype(jnp.int32) - share, -1)
    mine = jnp.sum((owner == me).astype(F32), axis=1, keepdims=True).astype(jnp.int32)
    info = jnp.concatenate(
        [place, extra, jnp.broadcast_to(mine, (1, columns)), jnp.zeros((5, columns), jnp.int32)], axis=0
    )
    wave = jnp.broadcast_to(wave_row(modes), (16, columns))
    picked = sum_parts(
        lax.dot_general(three_parts(wave), selector(place, share), NT, preferred_element_type=F32)
    )
    return info, jnp.concatenate([picked, picked], axis=1)[:8]


def pack(devices, wave, chosen, state, now, old, out_refs, pair):
    comps, points, columns = state.shape
    share = columns // devices
    wave = wave.reshape(1, 1, columns)
    forcing = RK_GAMMA * now + RK_ZETA * old
    local = state + TIME_STEP * (forcing - RK_ALPHA * (wave * state))
    rows = comps * points
    both = jnp.concatenate([state.reshape(rows, columns), local.reshape(rows, columns)], axis=0)
    placed = sum_parts(lax.dot_general(three_parts(both), chosen, NT, preferred_element_type=F32))
    for step, out in zip(steps_of(devices, points), out_refs):
        taken = placed[:, step * share : (step + 1) * share]
        for kind in range(2):
            real = 2 * kind * points
            imag = real + points
            out[kind, pair] = jnp.concatenate([taken[real : real + points], taken[imag : imag + points]], axis=1)


def first_kernel(
    devices, me_ref, owner_hbm, modes_hbm, state_hbm, now_hbm, old_hbm, info_ref, wave_ref, *refs
):
    out_refs, (owner_ref, modes_ref, state_ref, now_ref, old_ref, sems) = refs[:devices], refs[devices:]
    columns = owner_ref.shape[1]
    copies = [
        pltpu.make_async_copy(owner_hbm, owner_ref, sems.at[0]),
        pltpu.make_async_copy(modes_hbm, modes_ref, sems.at[1]),
    ]
    for pair in range(PAIRS):
        comps = slice(2 * pair, 2 * pair + 2)
        for at, (source, target) in enumerate(((state_hbm, state_ref), (now_hbm, now_ref), (old_hbm, old_ref))):
            copies.append(
                pltpu.make_async_copy(source.at[comps], target.at[comps], sems.at[2 + 3 * pair + at])
            )
    for copy in copies:
        copy.start()
    copies[0].wait()
    copies[1].wait()
    info, wave = plan(devices, me_ref[0], owner_ref[...], modes_ref[...])
    info_ref[...] = info
    wave_ref[...] = wave
    wave = wave_row(modes_ref[...])
    chosen = selector(info[0:1], columns)
    for pair in range(PAIRS):
        for copy in copies[2 + 3 * pair : 5 + 3 * pair]:
            copy.wait()
        comps = slice(2 * pair, 2 * pair + 2)
        pack(devices, wave, chosen, state_ref[comps], now_ref[comps], old_ref[comps], out_refs, pair)


def operators_kernel(
    deriv_ref, inverse_ref, basis_ref, values_ref, high_out, low_out, both_high_out, both_low_out, basis_out, values_out
):
    high, low = two_parts(inverse_ref[...])
    high_out[...] = high
    low_out[...] = low
    both = (TIME_STEP * RK_ALPHA) * apply(jnp.concatenate([high, high, low], axis=1), deriv_ref[...])
    high, low = two_parts(both)
    both_high_out[...] = high
    both_low_out[...] = low
    high, low = two_parts(basis_ref[...])
    basis_out[...] = jnp.concatenate([high, high, low], axis=1)
    lanes = values_out.shape[1]
    values_out[...] = jnp.transpose(jnp.broadcast_to(values_ref[...], (lanes, values_ref.shape[1])))


def apply(operator, x):
    high, low = two_parts(x)
    return jnp.dot(operator, jnp.concatenate([high, low, high], axis=0), preferred_element_type=F32)


def projected(me, operators, steps, blocks, state, local):
    _, pairs, points, lanes = blocks[0].shape
    fill = LANES // points
    for at, (step, block) in enumerate(zip(steps, blocks)):
        first = at // fill * LANES
        rows = pl.ds(pl.multiple_of(first + ((me ^ step) % fill) * points, points), points)
        for pair in range(pairs):
            state[rows, pair * lanes : (pair + 1) * lanes] = block[0, pair]
            local[rows, pair * lanes : (pair + 1) * lanes] = block[1, pair]
    high, low, both_high, both_low = operators
    matrix, values = [], []
    for first in range(0, len(steps), fill):
        depth = pl.ds(pl.multiple_of((me ^ steps[first]) // fill * LANES, LANES), LANES)
        rows = slice(first // fill * LANES, (first // fill + 1) * LANES)
        for upper, lower, x in ((high, low, local), (both_high, both_low, state)):
            x_high, x_low = two_parts(x[rows, :])
            matrix += [upper[:, depth], upper[:, depth], lower[:, depth]]
            values += [x_high, x_low, x_high]
    return jnp.dot(
        jnp.concatenate(matrix, axis=1), jnp.concatenate(values, axis=0), preferred_element_type=F32
    )


def solve_early_kernel(steps, me_ref, *refs):
    operators, in_refs, (out_ref, state, local) = refs[:4], refs[4:-3], refs[-3:]
    out_ref[...] = projected(me_ref[0], operators, steps, in_refs, state, local)


def solve_late_kernel(steps, order, me_ref, wave_ref, values_ref, basis_ref, early_ref, *refs):
    operators, refs = refs[:4], refs[4:]
    in_refs, refs = refs[: len(steps)], refs[len(steps) :]
    out_refs, (solved_ref, state, local, after) = refs[:-4], refs[-4:]
    me = me_ref[0]
    pairs, points, lanes = out_refs[0].shape
    project = early_ref[...] + projected(me, operators, steps, in_refs, state, local)
    damping = 1.0 + TIME_STEP * RK_BETA * (values_ref[...] + wave_ref[0:1, :])
    project = project / jnp.concatenate([damping] * pairs, axis=1)
    after[...] = apply(basis_ref[...], project)
    for pair in range(pairs):
        solved_ref[pair] = after[:, pair * lanes : (pair + 1) * lanes]
    for step, block in zip(order, out_refs):
        rows = pl.ds(pl.multiple_of((me ^ step) * points, points), points)
        for pair in range(pairs):
            block[pair] = after[rows, pair * lanes : (pair + 1) * lanes]


def side_by_side(steps, blocks):
    pairs, _, lanes = blocks[0].shape
    share = lanes // 2
    sorted_blocks = [blocks[steps.index(step)] for step in sorted(steps)]
    rows = []
    for pair in range(pairs):
        for half in range(2):
            rows.append(
                jnp.concatenate(
                    [block[pair][:, half * share : (half + 1) * share] for block in sorted_blocks], axis=1
                )
            )
    return jnp.concatenate(rows, axis=0)


def surplus_early_kernel(steps, info_ref, *refs):
    in_refs, (out_ref, late_ref) = refs[:-2], refs[-2:]
    columns = info_ref.shape[1]
    share = in_refs[0].shape[2] // 2
    chosen = lax.dot_general(
        selector(info_ref[0:1, :], columns), selector(info_ref[1:2, :], columns), NT, preferred_element_type=F32
    ).astype(BF16)
    devices = columns // share
    late = [step for step in range(devices) if step not in steps]
    first, last = late[0] * share, (late[-1] + 1) * share
    late_ref[...] = chosen[first:last]
    kept = jnp.concatenate([chosen[:first], chosen[last:]], axis=0)
    out_ref[...] = sum_parts(
        jnp.dot(three_parts(side_by_side(steps, in_refs)), kept, preferred_element_type=F32)
    )


def surplus_late_kernel(steps, order, early_ref, chosen_ref, *refs):
    in_refs, out_refs = refs[: len(steps)], refs[len(steps) :]
    pairs, points, lanes = in_refs[0].shape
    share = lanes // 2
    extra = early_ref[...] + sum_parts(
        jnp.dot(three_parts(side_by_side(steps, in_refs)), chosen_ref[...], preferred_element_type=F32)
    )
    for step, out in zip(order, out_refs):
        taken = extra[:, step * share : (step + 1) * share]
        for pair in range(pairs):
            real = 2 * pair * points
            imag = real + points
            out[pair] = jnp.concatenate([taken[real : real + points], taken[imag : imag + points]], axis=1)


def state_kernel(order, info_ref, modes_ref, velocity_ref, *refs):
    in_refs, (_, state_hbm, emf_ref, state_ref, sem) = refs[: len(order)], refs[len(order) :]
    comps, points, columns = state_ref.shape
    state = sum_parts(
        jnp.dot(
            three_parts(side_by_side(order, in_refs)),
            selector(info_ref[0:1, :], columns),
            preferred_element_type=F32,
        )
    )
    state_ref[...] = state.reshape(comps, points, columns)
    copy = pltpu.make_async_copy(state_ref, state_hbm, sem)
    copy.start()
    emf_ref[...] = emf_of(modes_ref[...], velocity_ref, state_ref)
    copy.wait()


def emf_of(modes, velocity_ref, state_ref):
    _, points, columns = state_ref.shape
    weight = jnp.where(modes[0:1, :] > 0, 2.0, 1.0).astype(F32)
    totals = [jnp.zeros((points, columns), F32)] * 3
    for field in range(3):
        real = weight * state_ref[2 * field]
        imag = weight * state_ref[2 * field + 1]
        for sign, i, j in ((1.0, (field + 1) % 3, (field + 2) % 3), (-1.0, (field + 2) % 3, (field + 1) % 3)):
            totals[i] = totals[i] + sign * (velocity_ref[2 * j] * real + velocity_ref[2 * j + 1] * imag)
    rows = []
    for total in totals:
        folded = total[:, :LANES]
        for at in range(1, columns // LANES):
            folded = folded + total[:, at * LANES : (at + 1) * LANES]
        rows.append(jnp.sum(jnp.transpose(folded), axis=0, keepdims=True))
    return jnp.concatenate(rows, axis=0)


def assemble(me, steps, used, solved_ref, in_refs, out_hbm, rows_ref, sems):
    pairs, points, lanes = in_refs[0].shape
    share = lanes // 2
    fill = LANES // points
    copies = []
    for first in range(0, len(steps), fill):
        depth = pl.ds(pl.multiple_of((me ^ steps[first]) // fill * LANES, LANES), LANES)
        rows = slice(first // fill * LANES, (first // fill + 1) * LANES)
        for pair in range(pairs):
            solved = solved_ref[pair, depth, :]
            for half in range(2):
                comp = 2 * pair + half
                kept = solved[:, half * share : (half + 1) * share]
                rows_ref[comp, rows, :share] = jnp.where(used < 0, 0.0, kept)
                for at in range(first, first + fill):
                    place = pl.ds(
                        pl.multiple_of(first // fill * LANES + ((me ^ steps[at]) % fill) * points, points), points
                    )
                    rows_ref[comp, place, share:] = in_refs[at][pair][:, half * share : (half + 1) * share]
                copies.append(
                    pltpu.make_async_copy(
                        rows_ref.at[comp, rows], out_hbm.at[comp, depth], sems.at[first // fill * 2 * pairs + comp]
                    )
                )
                copies[-1].start()
    for copy in copies:
        copy.wait()


def unused(info_ref, share):
    lane = lax.broadcasted_iota(jnp.int32, (LANES, share), 1)
    return jnp.where(lane < info_ref[2:3, :share], 0, -1)


def assemble_early_kernel(steps, me_ref, info_ref, solved_ref, *refs):
    in_refs, (out_hbm, rows_ref, sems) = refs[: len(steps)], refs[len(steps) :]
    share = in_refs[0].shape[2] // 2
    assemble(me_ref[0], steps, unused(info_ref, share), solved_ref, in_refs, out_hbm, rows_ref, sems)


def assemble_late_kernel(steps, terms, me_ref, info_ref, solved_ref, *refs):
    in_refs, refs = refs[: len(steps)], refs[len(steps) :]
    parts, (_, out_hbm, emf_ref, rows_ref, sems) = refs[:terms], refs[terms:]
    parts = [ref[...] for ref in parts]
    while len(parts) > 1:
        parts = [parts[at] + parts[at + 1] for at in range(0, len(parts), 2)]
    emf_ref[...] = parts[0]
    share = in_refs[0].shape[2] // 2
    assemble(me_ref[0], steps, unused(info_ref, share), solved_ref, in_refs, out_hbm, rows_ref, sems)


def late_steps(devices, points):
    return list(range(devices // 2, devices // 2 + LANES // points))


def early_steps(devices, points):
    fill, half = LANES // points, devices // 2
    return list(range(fill)) + list(range(half + fill, devices)) + list(range(fill, half))


def steps_of(devices, points):
    return early_steps(devices, points) + late_steps(devices, points)


def exchange(blocks, steps):
    devices = len(blocks)
    return [
        block if step == 0 else lax.ppermute(block, "col", [(i, i ^ step) for i in range(devices)])
        for step, block in zip(steps, blocks)
    ]


def from_groups(value):
    groups = lax.axis_size("grp")
    return [value] + [
        lax.ppermute(value, "grp", [(i, i ^ step) for i in range(groups)]) for step in range(1, groups)
    ]


def on_device(
    state_now,
    force_now,
    force_old,
    velocity,
    second_deriv,
    eig_basis,
    eig_inverse,
    eig_values,
    kept_modes,
    col_owner,
):
    comps, points, columns = state_now.shape
    devices = lax.axis_size("col")
    depth = devices * points
    share = columns // devices
    lanes = 2 * share
    width = PAIRS * lanes
    steps = steps_of(devices, points)
    early, late = early_steps(devices, points), late_steps(devices, points)
    split = len(early)
    early_rows, late_rows = split * points, len(late) * points
    back = [shaped((PAIRS, points, lanes))] * devices
    me = lax.axis_index("col").astype(jnp.int32).reshape(1)
    far = [
        pltpu.with_memory_space_constraint(array, pltpu.HBM)
        for array in (col_owner.reshape(1, columns), kept_modes, state_now, force_now, force_old)
    ]

    outs = call(
        functools.partial(first_kernel, devices),
        [shaped((8, columns), jnp.int32), shaped((8, lanes))] + [shaped((2, PAIRS, points, lanes))] * devices,
        [SCALAR] + [FAR] * 5,
        [LOCAL] * (2 + devices),
        1,
        [pltpu.VMEM((1, columns), jnp.int32), pltpu.VMEM((2, columns), jnp.int32)]
        + [pltpu.VMEM((comps, points, columns), F32)] * 3
        + [pltpu.SemaphoreType.DMA((2 + 3 * PAIRS,))],
    )(me, *far)
    info, wave = outs[:2]
    forward = exchange(outs[2:], steps)

    square = shaped((depth, depth), BF16)
    operators = call(
        operators_kernel,
        [square] * 4 + [shaped((depth, 3 * depth), BF16), shaped((depth, lanes))],
        [LOCAL] * 4,
        [LOCAL] * 6,
        HEAVY,
    )(second_deriv, eig_inverse, eig_basis, eig_values.reshape(1, depth))
    basis, values = operators[4:]

    begun = call(
        functools.partial(solve_early_kernel, early),
        shaped((depth, width)),
        [SCALAR] + [LOCAL] * (4 + split),
        LOCAL,
        HEAVY,
        [pltpu.VMEM((early_rows, width), F32)] * 2,
    )(me, *operators[:4], *forward[:split])
    outs = call(
        functools.partial(solve_late_kernel, late, steps),
        back + [shaped((PAIRS, depth, lanes))],
        [SCALAR] + [LOCAL] * (8 + len(late)),
        [LOCAL] * (devices + 1),
        1,
        [pltpu.VMEM((late_rows, width), F32)] * 2 + [pltpu.VMEM((depth, width), F32)],
    )(me, wave, values, basis, begun, *operators[:4], *forward[split:])
    solved = outs[devices]
    returned = exchange(outs[:devices], steps)

    begun, chosen = call(
        functools.partial(surplus_early_kernel, early),
        [shaped((comps * points, columns)), shaped((len(late) * share, columns), BF16)],
        [LOCAL] * (1 + split),
        [LOCAL] * 2,
        HEAVY,
    )(info, *returned[:split])
    outs = call(
        functools.partial(surplus_late_kernel, late, steps),
        back,
        [LOCAL] * (2 + len(late)),
        [LOCAL] * devices,
        1,
    )(begun, chosen, *returned[split:])
    extra = exchange(outs, steps)

    state_next, emf = call(
        functools.partial(state_kernel, steps),
        [shaped(state_now.shape), shaped((3, points))],
        [LOCAL] * (3 + devices) + [ANYWHERE],
        [FAR, LOCAL],
        HEAVY,
        [pltpu.VMEM(state_now.shape, F32), pltpu.SemaphoreType.DMA],
    )(info, kept_modes, velocity, *returned, extra[early.index(3)])
    terms = from_groups(emf)

    owned = call(
        functools.partial(assemble_early_kernel, early),
        shaped((comps, depth, lanes)),
        [SCALAR] + [LOCAL] * (2 + split),
        FAR,
        HEAVY,
        [
            pltpu.VMEM((comps, early_rows, lanes), F32),
            pltpu.SemaphoreType.DMA((comps * early_rows // LANES,)),
        ],
    )(me, info, solved, *extra[:split])
    owned, mean_emf = call(
        functools.partial(assemble_late_kernel, late, len(terms)),
        [shaped((comps, depth, lanes)), shaped((3, points))],
        [SCALAR] + [LOCAL] * (2 + len(late) + len(terms)) + [FAR],
        [FAR, LOCAL],
        1,
        [pltpu.VMEM((comps, late_rows, lanes), F32), pltpu.SemaphoreType.DMA((comps,))],
        aliases={3 + len(late) + len(terms): 0},
    )(me, info, solved, *extra[split:], *terms, owned)
    return (state_next, owned, mean_emf)


def solution(mesh):
    return jax.shard_map(
        on_device,
        mesh=mesh,
        in_specs=(
            P(None, "col", "grp"),
            P(None, "col", "grp"),
            P(None, "col", "grp"),
            P(None, "col", "grp"),
            P(),
            P(),
            P(),
            P(),
            P(None, "grp"),
            P("grp", None),
        ),
        out_specs=(P(None, "col", "grp"), P(None, None, ("grp", "col")), P(None, "col")),
        check_vma=False,
    )
```

```python
import functools

import jax
import jax.numpy as jnp
from jax import lax
from jax.experimental import pallas as pl
from jax.experimental.pallas import tpu as pltpu
from jax.sharding import PartitionSpec as P

KMAX = 2048
TIME_STEP = 2.0
RK_ALPHA = -3.0 / 40.0
RK_BETA = 5.0 / 24.0
RK_GAMMA = 5.0 / 12.0
RK_ZETA = -17.0 / 60.0
WAVE_SCALE = 8.0
VMEM_LIMIT = 24 * 1024 * 1024
PAIRS = 3
LANES = 128
HEAVY = 10

F32 = jnp.float32
BF16 = jnp.bfloat16


def call(body, out_shape, in_specs, out_specs, weight, scratch=(), aliases=None):
    return pl.pallas_call(
        body,
        out_shape=out_shape,
        in_specs=in_specs,
        out_specs=out_specs,
        scratch_shapes=list(scratch),
        input_output_aliases=aliases or {},
        cost_estimate=pl.CostEstimate(flops=weight * 10**9, bytes_accessed=weight * 10**6, transcendentals=0),
        compiler_params=pltpu.CompilerParams(vmem_limit_bytes=VMEM_LIMIT),
    )


LOCAL = pl.BlockSpec(memory_space=pltpu.VMEM)
SCALAR = pl.BlockSpec(memory_space=pltpu.SMEM)
FAR = pl.BlockSpec(memory_space=pltpu.HBM)
ANYWHERE = pl.BlockSpec(memory_space=pl.ANY)


def shaped(shape, dtype=F32):
    return jax.ShapeDtypeStruct(shape, dtype)


def three_parts(x):
    high = x.astype(BF16)
    rest = x - high.astype(F32)
    middle = rest.astype(BF16)
    low = (rest - middle.astype(F32)).astype(BF16)
    return jnp.concatenate([high, middle, low], axis=0)


def sum_parts(x):
    rows = x.shape[0] // 3
    return x[:rows] + x[rows : 2 * rows] + x[2 * rows :]


def two_parts(x):
    high = x.astype(BF16)
    low = (x - high.astype(F32)).astype(BF16)
    return high, low


def selector(places, rows):
    columns = places.shape[1]
    return (lax.broadcasted_iota(jnp.int32, (rows, columns), 0) == places).astype(F32).astype(BF16)


def wave_row(modes):
    wave_x = modes[0:1, :].astype(F32)
    wave_z = modes[1:2, :].astype(F32)
    return (wave_x * wave_x + wave_z * wave_z) * (WAVE_SCALE / (KMAX * KMAX))


NT = (((1,), (1,)), ((), ()))


def plan(devices, me, owner, modes):
    columns = owner.shape[1]
    share = columns // devices
    rows = -(-devices // 8) * 8
    owned = (lax.broadcasted_iota(jnp.int32, (rows, columns), 0) == owner).astype(F32)
    before = (
        lax.broadcasted_iota(jnp.int32, (LANES, LANES), 0) < lax.broadcasted_iota(jnp.int32, (LANES, LANES), 1)
    ).astype(F32)
    carry = jnp.zeros((rows, 1), F32)
    earlier = []
    for at in range(columns // LANES):
        block = owned[:, at * LANES : (at + 1) * LANES]
        earlier.append(jnp.dot(block, before, preferred_element_type=F32) + carry)
        carry = carry + jnp.sum(block, axis=1, keepdims=True)
    counts = carry
    rank = jnp.sum(owned * jnp.concatenate(earlier, axis=1), axis=0, keepdims=True)
    surplus = jnp.maximum(counts - share, 0.0)
    lower = (lax.broadcasted_iota(jnp.int32, (rows, columns), 0) < owner).astype(F32)
    number = jnp.sum(lower * surplus, axis=0, keepdims=True) + (rank - share)
    free = share - jnp.minimum(counts, share)
    start = jnp.zeros((1, 1), F32)
    solver = owner
    slot = rank
    beyond = rank >= share
    for device in range(devices):
        here = free[device : device + 1, :]
        inside = beyond & (number >= start) & (number < start + here)
        solver = jnp.where(inside, device, solver)
        slot = jnp.where(inside, share - here + number - start, slot)
        start = start + here
    place = (solver ^ me) * share + slot.astype(jnp.int32)
    extra = jnp.where(beyond, (owner ^ me) * share + rank.astype(jnp.int32) - share, -1)
    mine = jnp.sum((owner == me).astype(F32), axis=1, keepdims=True).astype(jnp.int32)
    info = jnp.concatenate(
        [place, extra, jnp.broadcast_to(mine, (1, columns)), jnp.zeros((5, columns), jnp.int32)], axis=0
    )
    wave = jnp.broadcast_to(wave_row(modes), (16, columns))
    picked = sum_parts(
        lax.dot_general(three_parts(wave), selector(place, share), NT, preferred_element_type=F32)
    )
    return info, jnp.concatenate([picked, picked], axis=1)[:8]


def pack(devices, wave, chosen, state, now, old, out_refs, pair):
    comps, points, columns = state.shape
    share = columns // devices
    wave = wave.reshape(1, 1, columns)
    forcing = RK_GAMMA * now + RK_ZETA * old
    local = state + TIME_STEP * (forcing - RK_ALPHA * (wave * state))
    rows = comps * points
    both = jnp.concatenate([state.reshape(rows, columns), local.reshape(rows, columns)], axis=0)
    placed = sum_parts(lax.dot_general(three_parts(both), chosen, NT, preferred_element_type=F32))
    for step, out in zip(steps_of(devices, points), out_refs):
        taken = placed[:, step * share : (step + 1) * share]
        for kind in range(2):
            real = 2 * kind * points
            imag = real + points
            out[kind, pair] = jnp.concatenate([taken[real : real + points], taken[imag : imag + points]], axis=1)


def first_kernel(
    devices, me_ref, owner_hbm, modes_hbm, state_hbm, now_hbm, old_hbm, info_ref, wave_ref, *refs
):
    out_refs, (owner_ref, modes_ref, state_ref, now_ref, old_ref, sems) = refs[:devices], refs[devices:]
    columns = owner_ref.shape[1]
    copies = [
        pltpu.make_async_copy(owner_hbm, owner_ref, sems.at[0]),
        pltpu.make_async_copy(modes_hbm, modes_ref, sems.at[1]),
    ]
    for pair in range(PAIRS):
        comps = slice(2 * pair, 2 * pair + 2)
        for at, (source, target) in enumerate(((state_hbm, state_ref), (now_hbm, now_ref), (old_hbm, old_ref))):
            copies.append(
                pltpu.make_async_copy(source.at[comps], target.at[comps], sems.at[2 + 3 * pair + at])
            )
    for copy in copies:
        copy.start()
    copies[0].wait()
    copies[1].wait()
    info, wave = plan(devices, me_ref[0], owner_ref[...], modes_ref[...])
    info_ref[...] = info
    wave_ref[...] = wave
    wave = wave_row(modes_ref[...])
    chosen = selector(info[0:1], columns)
    for pair in range(PAIRS):
        for copy in copies[2 + 3 * pair : 5 + 3 * pair]:
            copy.wait()
        comps = slice(2 * pair, 2 * pair + 2)
        pack(devices, wave, chosen, state_ref[comps], now_ref[comps], old_ref[comps], out_refs, pair)


def operators_kernel(
    deriv_ref, inverse_ref, basis_ref, values_ref, high_out, low_out, both_high_out, both_low_out, basis_out, values_out
):
    high, low = two_parts(inverse_ref[...])
    high_out[...] = high
    low_out[...] = low
    both = (TIME_STEP * RK_ALPHA) * apply(jnp.concatenate([high, high, low], axis=1), deriv_ref[...])
    high, low = two_parts(both)
    both_high_out[...] = high
    both_low_out[...] = low
    high, low = two_parts(basis_ref[...])
    basis_out[...] = jnp.concatenate([high, high, low], axis=1)
    lanes = values_out.shape[1]
    values_out[...] = jnp.transpose(jnp.broadcast_to(values_ref[...], (lanes, values_ref.shape[1])))


def apply(operator, x):
    high, low = two_parts(x)
    return jnp.dot(operator, jnp.concatenate([high, low, high], axis=0), preferred_element_type=F32)


def projected(me, operators, steps, blocks, state, local):
    _, pairs, points, lanes = blocks[0].shape
    fill = LANES // points
    for at, (step, block) in enumerate(zip(steps, blocks)):
        first = at // fill * LANES
        rows = pl.ds(pl.multiple_of(first + ((me ^ step) % fill) * points, points), points)
        for pair in range(pairs):
            state[rows, pair * lanes : (pair + 1) * lanes] = block[0, pair]
            local[rows, pair * lanes : (pair + 1) * lanes] = block[1, pair]
    high, low, both_high, both_low = operators
    matrix, values = [], []
    for first in range(0, len(steps), fill):
        depth = pl.ds(pl.multiple_of((me ^ steps[first]) // fill * LANES, LANES), LANES)
        rows = slice(first // fill * LANES, (first // fill + 1) * LANES)
        for upper, lower, x in ((high, low, local), (both_high, both_low, state)):
            x_high, x_low = two_parts(x[rows, :])
            matrix += [upper[:, depth], upper[:, depth], lower[:, depth]]
            values += [x_high, x_low, x_high]
    return jnp.dot(
        jnp.concatenate(matrix, axis=1), jnp.concatenate(values, axis=0), preferred_element_type=F32
    )


def solve_early_kernel(steps, me_ref, *refs):
    operators, in_refs, (out_ref, state, local) = refs[:4], refs[4:-3], refs[-3:]
    out_ref[...] = projected(me_ref[0], operators, steps, in_refs, state, local)


def solve_late_kernel(steps, order, me_ref, wave_ref, values_ref, basis_ref, early_ref, *refs):
    operators, refs = refs[:4], refs[4:]
    in_refs, refs = refs[: len(steps)], refs[len(steps) :]
    out_refs, (solved_ref, state, local, after) = refs[:-4], refs[-4:]
    me = me_ref[0]
    pairs, points, lanes = out_refs[0].shape
    project = early_ref[...] + projected(me, operators, steps, in_refs, state, local)
    damping = 1.0 + TIME_STEP * RK_BETA * (values_ref[...] + wave_ref[0:1, :])
    project = project / jnp.concatenate([damping] * pairs, axis=1)
    after[...] = apply(basis_ref[...], project)
    for pair in range(pairs):
        solved_ref[pair] = after[:, pair * lanes : (pair + 1) * lanes]
    for step, block in zip(order, out_refs):
        rows = pl.ds(pl.multiple_of((me ^ step) * points, points), points)
        for pair in range(pairs):
            block[pair] = after[rows, pair * lanes : (pair + 1) * lanes]


def side_by_side(steps, blocks):
    pairs, _, lanes = blocks[0].shape
    share = lanes // 2
    sorted_blocks = [blocks[steps.index(step)] for step in sorted(steps)]
    rows = []
    for pair in range(pairs):
        for half in range(2):
            rows.append(
                jnp.concatenate(
                    [block[pair][:, half * share : (half + 1) * share] for block in sorted_blocks], axis=1
                )
            )
    return jnp.concatenate(rows, axis=0)


def surplus_early_kernel(steps, info_ref, *refs):
    in_refs, (out_ref, late_ref) = refs[:-2], refs[-2:]
    columns = info_ref.shape[1]
    share = in_refs[0].shape[2] // 2
    chosen = lax.dot_general(
        selector(info_ref[0:1, :], columns), selector(info_ref[1:2, :], columns), NT, preferred_element_type=F32
    ).astype(BF16)
    devices = columns // share
    late = [step for step in range(devices) if step not in steps]
    first, last = late[0] * share, (late[-1] + 1) * share
    late_ref[...] = chosen[first:last]
    kept = jnp.concatenate([chosen[:first], chosen[last:]], axis=0)
    out_ref[...] = sum_parts(
        jnp.dot(three_parts(side_by_side(steps, in_refs)), kept, preferred_element_type=F32)
    )


def surplus_late_kernel(steps, order, early_ref, chosen_ref, *refs):
    in_refs, out_refs = refs[: len(steps)], refs[len(steps) :]
    pairs, points, lanes = in_refs[0].shape
    share = lanes // 2
    extra = early_ref[...] + sum_parts(
        jnp.dot(three_parts(side_by_side(steps, in_refs)), chosen_ref[...], preferred_element_type=F32)
    )
    for step, out in zip(order, out_refs):
        taken = extra[:, step * share : (step + 1) * share]
        for pair in range(pairs):
            real = 2 * pair * points
            imag = real + points
            out[pair] = jnp.concatenate([taken[real : real + points], taken[imag : imag + points]], axis=1)


def state_kernel(order, info_ref, modes_ref, velocity_ref, *refs):
    in_refs, (_, state_hbm, emf_ref, state_ref, sem) = refs[: len(order)], refs[len(order) :]
    comps, points, columns = state_ref.shape
    state = sum_parts(
        jnp.dot(
            three_parts(side_by_side(order, in_refs)),
            selector(info_ref[0:1, :], columns),
            preferred_element_type=F32,
        )
    )
    state_ref[...] = state.reshape(comps, points, columns)
    copy = pltpu.make_async_copy(state_ref, state_hbm, sem)
    copy.start()
    emf_ref[...] = emf_of(modes_ref[...], velocity_ref, state_ref)
    copy.wait()


def emf_of(modes, velocity_ref, state_ref):
    _, points, columns = state_ref.shape
    weight = jnp.where(modes[0:1, :] > 0, 2.0, 1.0).astype(F32)
    totals = [jnp.zeros((points, columns), F32)] * 3
    for field in range(3):
        real = weight * state_ref[2 * field]
        imag = weight * state_ref[2 * field + 1]
        for sign, i, j in ((1.0, (field + 1) % 3, (field + 2) % 3), (-1.0, (field + 2) % 3, (field + 1) % 3)):
            totals[i] = totals[i] + sign * (velocity_ref[2 * j] * real + velocity_ref[2 * j + 1] * imag)
    rows = []
    for total in totals:
        folded = total[:, :LANES]
        for at in range(1, columns // LANES):
            folded = folded + total[:, at * LANES : (at + 1) * LANES]
        rows.append(jnp.sum(jnp.transpose(folded), axis=0, keepdims=True))
    return jnp.concatenate(rows, axis=0)


def assemble(me, steps, used, solved_ref, in_refs, out_hbm, rows_ref, sems):
    pairs, points, lanes = in_refs[0].shape
    share = lanes // 2
    fill = LANES // points
    copies = []
    for first in range(0, len(steps), fill):
        depth = pl.ds(pl.multiple_of((me ^ steps[first]) // fill * LANES, LANES), LANES)
        rows = slice(first // fill * LANES, (first // fill + 1) * LANES)
        for pair in range(pairs):
            solved = solved_ref[pair, depth, :]
            for half in range(2):
                comp = 2 * pair + half
                kept = solved[:, half * share : (half + 1) * share]
                rows_ref[comp, rows, :share] = jnp.where(used < 0, 0.0, kept)
                for at in range(first, first + fill):
                    place = pl.ds(
                        pl.multiple_of(first // fill * LANES + ((me ^ steps[at]) % fill) * points, points), points
                    )
                    rows_ref[comp, place, share:] = in_refs[at][pair][:, half * share : (half + 1) * share]
                copies.append(
                    pltpu.make_async_copy(
                        rows_ref.at[comp, rows], out_hbm.at[comp, depth], sems.at[first // fill * 2 * pairs + comp]
                    )
                )
                copies[-1].start()
    for copy in copies:
        copy.wait()


def unused(info_ref, share):
    lane = lax.broadcasted_iota(jnp.int32, (LANES, share), 1)
    return jnp.where(lane < info_ref[2:3, :share], 0, -1)


def assemble_early_kernel(steps, me_ref, info_ref, solved_ref, *refs):
    in_refs, (out_hbm, rows_ref, sems) = refs[: len(steps)], refs[len(steps) :]
    share = in_refs[0].shape[2] // 2
    assemble(me_ref[0], steps, unused(info_ref, share), solved_ref, in_refs, out_hbm, rows_ref, sems)


def assemble_late_kernel(steps, me_ref, info_ref, solved_ref, *refs):
    in_refs, refs = refs[: len(steps)], refs[len(steps) :]
    terms_ref, _, out_hbm, emf_ref, rows_ref, sems = refs
    emf = terms_ref[0]
    for group in range(1, terms_ref.shape[0]):
        emf = emf + terms_ref[group]
    emf_ref[...] = emf
    share = in_refs[0].shape[2] // 2
    assemble(me_ref[0], steps, unused(info_ref, share), solved_ref, in_refs, out_hbm, rows_ref, sems)


def late_steps(devices, points):
    return list(range(devices // 2, devices // 2 + LANES // points))


def early_steps(devices, points):
    fill, half = LANES // points, devices // 2
    return list(range(fill)) + list(range(half + fill, devices)) + list(range(fill, half))


def steps_of(devices, points):
    return early_steps(devices, points) + late_steps(devices, points)


def exchange(blocks, steps):
    devices = len(blocks)
    return [
        block if step == 0 else lax.ppermute(block, "col", [(i, i ^ step) for i in range(devices)])
        for step, block in zip(steps, blocks)
    ]


def on_device(
    state_now,
    force_now,
    force_old,
    velocity,
    second_deriv,
    eig_basis,
    eig_inverse,
    eig_values,
    kept_modes,
    col_owner,
):
    comps, points, columns = state_now.shape
    devices = lax.axis_size("col")
    depth = devices * points
    share = columns // devices
    lanes = 2 * share
    width = PAIRS * lanes
    steps = steps_of(devices, points)
    early, late = early_steps(devices, points), late_steps(devices, points)
    split = len(early)
    early_rows, late_rows = split * points, len(late) * points
    back = [shaped((PAIRS, points, lanes))] * devices
    me = lax.axis_index("col").astype(jnp.int32).reshape(1)
    far = [
        pltpu.with_memory_space_constraint(array, pltpu.HBM)
        for array in (col_owner.reshape(1, columns), kept_modes, state_now, force_now, force_old)
    ]

    outs = call(
        functools.partial(first_kernel, devices),
        [shaped((8, columns), jnp.int32), shaped((8, lanes))] + [shaped((2, PAIRS, points, lanes))] * devices,
        [SCALAR] + [FAR] * 5,
        [LOCAL] * (2 + devices),
        1,
        [pltpu.VMEM((1, columns), jnp.int32), pltpu.VMEM((2, columns), jnp.int32)]
        + [pltpu.VMEM((comps, points, columns), F32)] * 3
        + [pltpu.SemaphoreType.DMA((2 + 3 * PAIRS,))],
    )(me, *far)
    info, wave = outs[:2]
    forward = exchange(outs[2:], steps)

    square = shaped((depth, depth), BF16)
    operators = call(
        operators_kernel,
        [square] * 4 + [shaped((depth, 3 * depth), BF16), shaped((depth, lanes))],
        [LOCAL] * 4,
        [LOCAL] * 6,
        HEAVY,
    )(second_deriv, eig_inverse, eig_basis, eig_values.reshape(1, depth))
    basis, values = operators[4:]

    begun = call(
        functools.partial(solve_early_kernel, early),
        shaped((depth, width)),
        [SCALAR] + [LOCAL] * (4 + split),
        LOCAL,
        HEAVY,
        [pltpu.VMEM((early_rows, width), F32)] * 2,
    )(me, *operators[:4], *forward[:split])
    outs = call(
        functools.partial(solve_late_kernel, late, steps),
        back + [shaped((PAIRS, depth, lanes))],
        [SCALAR] + [LOCAL] * (8 + len(late)),
        [LOCAL] * (devices + 1),
        1,
        [pltpu.VMEM((late_rows, width), F32)] * 2 + [pltpu.VMEM((depth, width), F32)],
    )(me, wave, values, basis, begun, *operators[:4], *forward[split:])
    solved = outs[devices]
    returned = exchange(outs[:devices], steps)

    begun, chosen = call(
        functools.partial(surplus_early_kernel, early),
        [shaped((comps * points, columns)), shaped((len(late) * share, columns), BF16)],
        [LOCAL] * (1 + split),
        [LOCAL] * 2,
        HEAVY,
    )(info, *returned[:split])
    outs = call(
        functools.partial(surplus_late_kernel, late, steps),
        back,
        [LOCAL] * (2 + len(late)),
        [LOCAL] * devices,
        1,
    )(begun, chosen, *returned[split:])
    extra = exchange(outs, steps)

    state_next, emf = call(
        functools.partial(state_kernel, steps),
        [shaped(state_now.shape), shaped((3, points))],
        [LOCAL] * (3 + devices) + [ANYWHERE],
        [FAR, LOCAL],
        HEAVY,
        [pltpu.VMEM(state_now.shape, F32), pltpu.SemaphoreType.DMA],
    )(info, kept_modes, velocity, *returned, extra[early.index(3)])
    terms = lax.all_gather(emf, "grp")

    owned = call(
        functools.partial(assemble_early_kernel, early),
        shaped((comps, depth, lanes)),
        [SCALAR] + [LOCAL] * (2 + split),
        FAR,
        HEAVY,
        [
            pltpu.VMEM((comps, early_rows, lanes), F32),
            pltpu.SemaphoreType.DMA((comps * early_rows // LANES,)),
        ],
    )(me, info, solved, *extra[:split])
    owned, mean_emf = call(
        functools.partial(assemble_late_kernel, late),
        [shaped((comps, depth, lanes)), shaped((3, points))],
        [SCALAR] + [LOCAL] * (3 + len(late)) + [FAR],
        [FAR, LOCAL],
        1,
        [pltpu.VMEM((comps, late_rows, lanes), F32), pltpu.SemaphoreType.DMA((comps,))],
        aliases={4 + len(late): 0},
    )(me, info, solved, *extra[split:], terms, owned)
    return (state_next, owned, mean_emf)


def solution(mesh):
    return jax.shard_map(
        on_device,
        mesh=mesh,
        in_specs=(
            P(None, "col", "grp"),
            P(None, "col", "grp"),
            P(None, "col", "grp"),
            P(None, "col", "grp"),
            P(),
            P(),
            P(),
            P(),
            P(None, "grp"),
            P("grp", None),
        ),
        out_specs=(P(None, "col", "grp"), P(None, None, ("grp", "col")), P(None, "col")),
        check_vma=False,
    )
```

```python
import functools

import jax
import jax.numpy as jnp
from jax import lax
from jax.experimental import pallas as pl
from jax.experimental.pallas import tpu as pltpu
from jax.sharding import PartitionSpec as P

KMAX = 2048
TIME_STEP = 2.0
RK_ALPHA = -3.0 / 40.0
RK_BETA = 5.0 / 24.0
RK_GAMMA = 5.0 / 12.0
RK_ZETA = -17.0 / 60.0
WAVE_SCALE = 8.0
VMEM_LIMIT = 24 * 1024 * 1024
PAIRS = 3
LANES = 128
HEAVY = 10

F32 = jnp.float32
BF16 = jnp.bfloat16


def call(body, out_shape, in_specs, out_specs, weight, scratch=(), aliases=None):
    return pl.pallas_call(
        body,
        out_shape=out_shape,
        in_specs=in_specs,
        out_specs=out_specs,
        scratch_shapes=list(scratch),
        input_output_aliases=aliases or {},
        cost_estimate=pl.CostEstimate(flops=weight * 10**9, bytes_accessed=weight * 10**6, transcendentals=0),
        compiler_params=pltpu.CompilerParams(vmem_limit_bytes=VMEM_LIMIT),
    )


LOCAL = pl.BlockSpec(memory_space=pltpu.VMEM)
SCALAR = pl.BlockSpec(memory_space=pltpu.SMEM)
FAR = pl.BlockSpec(memory_space=pltpu.HBM)
ANYWHERE = pl.BlockSpec(memory_space=pl.ANY)


def shaped(shape, dtype=F32):
    return jax.ShapeDtypeStruct(shape, dtype)


def three_parts(x):
    high = x.astype(BF16)
    rest = x - high.astype(F32)
    middle = rest.astype(BF16)
    low = (rest - middle.astype(F32)).astype(BF16)
    return jnp.concatenate([high, middle, low], axis=0)


def sum_parts(x):
    rows = x.shape[0] // 3
    return x[:rows] + x[rows : 2 * rows] + x[2 * rows :]


def two_parts(x):
    high = x.astype(BF16)
    low = (x - high.astype(F32)).astype(BF16)
    return high, low


def selector(places, rows):
    columns = places.shape[1]
    return (lax.broadcasted_iota(jnp.int32, (rows, columns), 0) == places).astype(F32).astype(BF16)


def wave_row(modes):
    wave_x = modes[0:1, :].astype(F32)
    wave_z = modes[1:2, :].astype(F32)
    return (wave_x * wave_x + wave_z * wave_z) * (WAVE_SCALE / (KMAX * KMAX))


NT = (((1,), (1,)), ((), ()))


def plan(devices, me, owner, modes):
    columns = owner.shape[1]
    share = columns // devices
    rows = -(-devices // 8) * 8
    owned = (lax.broadcasted_iota(jnp.int32, (rows, columns), 0) == owner).astype(F32)
    before = (
        lax.broadcasted_iota(jnp.int32, (LANES, LANES), 0) < lax.broadcasted_iota(jnp.int32, (LANES, LANES), 1)
    ).astype(F32)
    carry = jnp.zeros((rows, 1), F32)
    earlier = []
    for at in range(columns // LANES):
        block = owned[:, at * LANES : (at + 1) * LANES]
        earlier.append(jnp.dot(block, before, preferred_element_type=F32) + carry)
        carry = carry + jnp.sum(block, axis=1, keepdims=True)
    counts = carry
    rank = jnp.sum(owned * jnp.concatenate(earlier, axis=1), axis=0, keepdims=True)
    surplus = jnp.maximum(counts - share, 0.0)
    lower = (lax.broadcasted_iota(jnp.int32, (rows, columns), 0) < owner).astype(F32)
    number = jnp.sum(lower * surplus, axis=0, keepdims=True) + (rank - share)
    free = share - jnp.minimum(counts, share)
    start = jnp.zeros((1, 1), F32)
    solver = owner
    slot = rank
    beyond = rank >= share
    for device in range(devices):
        here = free[device : device + 1, :]
        inside = beyond & (number >= start) & (number < start + here)
        solver = jnp.where(inside, device, solver)
        slot = jnp.where(inside, share - here + number - start, slot)
        start = start + here
    place = (solver ^ me) * share + slot.astype(jnp.int32)
    extra = jnp.where(beyond, (owner ^ me) * share + rank.astype(jnp.int32) - share, -1)
    mine = jnp.sum((owner == me).astype(F32), axis=1, keepdims=True).astype(jnp.int32)
    info = jnp.concatenate(
        [place, extra, jnp.broadcast_to(mine, (1, columns)), jnp.zeros((5, columns), jnp.int32)], axis=0
    )
    wave = jnp.broadcast_to(wave_row(modes), (16, columns))
    picked = sum_parts(
        lax.dot_general(three_parts(wave), selector(place, share), NT, preferred_element_type=F32)
    )
    return info, jnp.concatenate([picked, picked], axis=1)[:8]


def pack(devices, wave, chosen, state, now, old, out_refs, pair):
    comps, points, columns = state.shape
    share = columns // devices
    wave = wave.reshape(1, 1, columns)
    forcing = RK_GAMMA * now + RK_ZETA * old
    local = state + TIME_STEP * (forcing - RK_ALPHA * (wave * state))
    rows = comps * points
    both = jnp.concatenate([state.reshape(rows, columns), local.reshape(rows, columns)], axis=0)
    placed = sum_parts(lax.dot_general(three_parts(both), chosen, NT, preferred_element_type=F32))
    for step, out in zip(steps_of(devices, points), out_refs):
        taken = placed[:, step * share : (step + 1) * share]
        for kind in range(2):
            real = 2 * kind * points
            imag = real + points
            out[kind, pair] = jnp.concatenate([taken[real : real + points], taken[imag : imag + points]], axis=1)


def first_kernel(
    devices, me_ref, owner_hbm, modes_hbm, state_hbm, now_hbm, old_hbm, info_ref, wave_ref, *refs
):
    out_refs, (owner_ref, modes_ref, state_ref, now_ref, old_ref, sems) = refs[:devices], refs[devices:]
    columns = owner_ref.shape[1]
    copies = [
        pltpu.make_async_copy(owner_hbm, owner_ref, sems.at[0]),
        pltpu.make_async_copy(modes_hbm, modes_ref, sems.at[1]),
    ]
    for pair in range(PAIRS):
        comps = slice(2 * pair, 2 * pair + 2)
        for at, (source, target) in enumerate(((state_hbm, state_ref), (now_hbm, now_ref), (old_hbm, old_ref))):
            copies.append(
                pltpu.make_async_copy(source.at[comps], target.at[comps], sems.at[2 + 3 * pair + at])
            )
    for copy in copies:
        copy.start()
    copies[0].wait()
    copies[1].wait()
    info, wave = plan(devices, me_ref[0], owner_ref[...], modes_ref[...])
    info_ref[...] = info
    wave_ref[...] = wave
    wave = wave_row(modes_ref[...])
    chosen = selector(info[0:1], columns)
    for pair in range(PAIRS):
        for copy in copies[2 + 3 * pair : 5 + 3 * pair]:
            copy.wait()
        comps = slice(2 * pair, 2 * pair + 2)
        pack(devices, wave, chosen, state_ref[comps], now_ref[comps], old_ref[comps], out_refs, pair)


def operators_kernel(
    deriv_ref, inverse_ref, basis_ref, values_ref, high_out, low_out, both_high_out, both_low_out, basis_out, values_out
):
    high, low = two_parts(inverse_ref[...])
    high_out[...] = high
    low_out[...] = low
    both = (TIME_STEP * RK_ALPHA) * apply(jnp.concatenate([high, high, low], axis=1), deriv_ref[...])
    high, low = two_parts(both)
    both_high_out[...] = high
    both_low_out[...] = low
    high, low = two_parts(basis_ref[...])
    basis_out[...] = jnp.concatenate([high, high, low], axis=1)
    lanes = values_out.shape[1]
    values_out[...] = jnp.transpose(jnp.broadcast_to(values_ref[...], (lanes, values_ref.shape[1])))


def apply(operator, x):
    high, low = two_parts(x)
    return jnp.dot(operator, jnp.concatenate([high, low, high], axis=0), preferred_element_type=F32)


def projected(me, operators, steps, blocks, state, local):
    _, pairs, points, lanes = blocks[0].shape
    fill = LANES // points
    for at, (step, block) in enumerate(zip(steps, blocks)):
        first = at // fill * LANES
        rows = pl.ds(pl.multiple_of(first + ((me ^ step) % fill) * points, points), points)
        for pair in range(pairs):
            state[rows, pair * lanes : (pair + 1) * lanes] = block[0, pair]
            local[rows, pair * lanes : (pair + 1) * lanes] = block[1, pair]
    high, low, both_high, both_low = operators
    matrix, values = [], []
    for first in range(0, len(steps), fill):
        depth = pl.ds(pl.multiple_of((me ^ steps[first]) // fill * LANES, LANES), LANES)
        rows = slice(first // fill * LANES, (first // fill + 1) * LANES)
        for upper, lower, x in ((high, low, local), (both_high, both_low, state)):
            x_high, x_low = two_parts(x[rows, :])
            matrix += [upper[:, depth], upper[:, depth], lower[:, depth]]
            values += [x_high, x_low, x_high]
    return jnp.dot(
        jnp.concatenate(matrix, axis=1), jnp.concatenate(values, axis=0), preferred_element_type=F32
    )


def solve_early_kernel(steps, me_ref, *refs):
    operators, in_refs, (out_ref, state, local) = refs[:4], refs[4:-3], refs[-3:]
    out_ref[...] = projected(me_ref[0], operators, steps, in_refs, state, local)


def solve_late_kernel(steps, order, me_ref, wave_ref, values_ref, basis_ref, early_ref, *refs):
    operators, refs = refs[:4], refs[4:]
    in_refs, refs = refs[: len(steps)], refs[len(steps) :]
    out_refs, (solved_ref, state, local, after) = refs[:-4], refs[-4:]
    me = me_ref[0]
    pairs, points, lanes = out_refs[0].shape
    project = early_ref[...] + projected(me, operators, steps, in_refs, state, local)
    damping = 1.0 + TIME_STEP * RK_BETA * (values_ref[...] + wave_ref[0:1, :])
    project = project / jnp.concatenate([damping] * pairs, axis=1)
    after[...] = apply(basis_ref[...], project)
    for pair in range(pairs):
        solved_ref[pair] = after[:, pair * lanes : (pair + 1) * lanes]
    for step, block in zip(order, out_refs):
        rows = pl.ds(pl.multiple_of((me ^ step) * points, points), points)
        for pair in range(pairs):
            block[pair] = after[rows, pair * lanes : (pair + 1) * lanes]


def side_by_side(steps, blocks):
    pairs, _, lanes = blocks[0].shape
    share = lanes // 2
    sorted_blocks = [blocks[steps.index(step)] for step in sorted(steps)]
    rows = []
    for pair in range(pairs):
        for half in range(2):
            rows.append(
                jnp.concatenate(
                    [block[pair][:, half * share : (half + 1) * share] for block in sorted_blocks], axis=1
                )
            )
    return jnp.concatenate(rows, axis=0)


def surplus_early_kernel(steps, info_ref, *refs):
    in_refs, (out_ref, late_ref) = refs[:-2], refs[-2:]
    columns = info_ref.shape[1]
    share = in_refs[0].shape[2] // 2
    chosen = lax.dot_general(
        selector(info_ref[0:1, :], columns), selector(info_ref[1:2, :], columns), NT, preferred_element_type=F32
    ).astype(BF16)
    devices = columns // share
    late = [step for step in range(devices) if step not in steps]
    first, last = late[0] * share, (late[-1] + 1) * share
    late_ref[...] = chosen[first:last]
    kept = jnp.concatenate([chosen[:first], chosen[last:]], axis=0)
    out_ref[...] = sum_parts(
        jnp.dot(three_parts(side_by_side(steps, in_refs)), kept, preferred_element_type=F32)
    )


def surplus_late_kernel(steps, order, early_ref, chosen_ref, *refs):
    in_refs, out_refs = refs[: len(steps)], refs[len(steps) :]
    pairs, points, lanes = in_refs[0].shape
    share = lanes // 2
    extra = early_ref[...] + sum_parts(
        jnp.dot(three_parts(side_by_side(steps, in_refs)), chosen_ref[...], preferred_element_type=F32)
    )
    for step, out in zip(order, out_refs):
        taken = extra[:, step * share : (step + 1) * share]
        for pair in range(pairs):
            real = 2 * pair * points
            imag = real + points
            out[pair] = jnp.concatenate([taken[real : real + points], taken[imag : imag + points]], axis=1)


def state_kernel(order, info_ref, modes_ref, velocity_ref, *refs):
    in_refs, (_, state_hbm, emf_ref, state_ref, sem) = refs[: len(order)], refs[len(order) :]
    comps, points, columns = state_ref.shape
    state = sum_parts(
        jnp.dot(
            three_parts(side_by_side(order, in_refs)),
            selector(info_ref[0:1, :], columns),
            preferred_element_type=F32,
        )
    )
    state_ref[...] = state.reshape(comps, points, columns)
    copy = pltpu.make_async_copy(state_ref, state_hbm, sem)
    copy.start()
    emf_ref[...] = emf_of(modes_ref[...], velocity_ref, state_ref)
    copy.wait()


def emf_of(modes, velocity_ref, state_ref):
    _, points, columns = state_ref.shape
    weight = jnp.where(modes[0:1, :] > 0, 2.0, 1.0).astype(F32)
    totals = [jnp.zeros((points, columns), F32)] * 3
    for field in range(3):
        real = weight * state_ref[2 * field]
        imag = weight * state_ref[2 * field + 1]
        for sign, i, j in ((1.0, (field + 1) % 3, (field + 2) % 3), (-1.0, (field + 2) % 3, (field + 1) % 3)):
            totals[i] = totals[i] + sign * (velocity_ref[2 * j] * real + velocity_ref[2 * j + 1] * imag)
    rows = []
    for total in totals:
        folded = total[:, :LANES]
        for at in range(1, columns // LANES):
            folded = folded + total[:, at * LANES : (at + 1) * LANES]
        rows.append(jnp.sum(jnp.transpose(folded), axis=0, keepdims=True))
    return jnp.concatenate(rows, axis=0)


def assemble(me, steps, used, solved_ref, in_refs, out_hbm, rows_ref, sems):
    pairs, points, lanes = in_refs[0].shape
    share = lanes // 2
    fill = LANES // points
    copies = []
    for first in range(0, len(steps), fill):
        depth = pl.ds(pl.multiple_of((me ^ steps[first]) // fill * LANES, LANES), LANES)
        rows = slice(first // fill * LANES, (first // fill + 1) * LANES)
        for pair in range(pairs):
            solved = solved_ref[pair, depth, :]
            for half in range(2):
                comp = 2 * pair + half
                kept = solved[:, half * share : (half + 1) * share]
                rows_ref[comp, rows, :share] = jnp.where(used < 0, 0.0, kept)
                for at in range(first, first + fill):
                    place = pl.ds(
                        pl.multiple_of(first // fill * LANES + ((me ^ steps[at]) % fill) * points, points), points
                    )
                    rows_ref[comp, place, share:] = in_refs[at][pair][:, half * share : (half + 1) * share]
                copies.append(
                    pltpu.make_async_copy(
                        rows_ref.at[comp, rows], out_hbm.at[comp, depth], sems.at[first // fill * 2 * pairs + comp]
                    )
                )
                copies[-1].start()
    for copy in copies:
        copy.wait()


def unused(info_ref, share):
    lane = lax.broadcasted_iota(jnp.int32, (LANES, share), 1)
    return jnp.where(lane < info_ref[2:3, :share], 0, -1)


def assemble_early_kernel(steps, me_ref, info_ref, solved_ref, *refs):
    in_refs, (out_hbm, rows_ref, sems) = refs[: len(steps)], refs[len(steps) :]
    share = in_refs[0].shape[2] // 2
    assemble(me_ref[0], steps, unused(info_ref, share), solved_ref, in_refs, out_hbm, rows_ref, sems)


def assemble_late_kernel(steps, terms, me_ref, info_ref, solved_ref, *refs):
    in_refs, refs = refs[: len(steps)], refs[len(steps) :]
    parts, (_, out_hbm, emf_ref, rows_ref, sems) = refs[:terms], refs[terms:]
    parts = [ref[...] for ref in parts]
    while len(parts) > 1:
        parts = [parts[at] + parts[at + 1] for at in range(0, len(parts), 2)]
    emf_ref[...] = parts[0]
    share = in_refs[0].shape[2] // 2
    assemble(me_ref[0], steps, unused(info_ref, share), solved_ref, in_refs, out_hbm, rows_ref, sems)


def near_first(steps, devices):
    return [step for step in steps if step < devices // 2] + [step for step in steps if step >= devices // 2]


def late_steps(devices, points):
    return list(range(devices // 2, devices // 2 + LANES // points))


def early_steps(devices, points):
    fill, half = LANES // points, devices // 2
    return list(range(fill)) + list(range(half + fill, devices)) + list(range(fill, half))


def steps_of(devices, points):
    return early_steps(devices, points) + late_steps(devices, points)


def exchange(blocks, steps):
    devices = len(blocks)
    return [
        block if step == 0 else lax.ppermute(block, "col", [(i, i ^ step) for i in range(devices)])
        for step, block in zip(steps, blocks)
    ]


def pair_sums(value, step):
    groups = lax.axis_size("grp")
    while 2 * step < groups:
        value = value + lax.ppermute(value, "grp", [(i, i ^ step) for i in range(groups)])
        step = 2 * step
    return [value, lax.ppermute(value, "grp", [(i, i ^ step) for i in range(groups)])]


def on_device(
    state_now,
    force_now,
    force_old,
    velocity,
    second_deriv,
    eig_basis,
    eig_inverse,
    eig_values,
    kept_modes,
    col_owner,
):
    comps, points, columns = state_now.shape
    devices = lax.axis_size("col")
    depth = devices * points
    share = columns // devices
    lanes = 2 * share
    width = PAIRS * lanes
    steps = steps_of(devices, points)
    early, late = early_steps(devices, points), late_steps(devices, points)
    split = len(early)
    early_rows, late_rows = split * points, len(late) * points
    back = [shaped((PAIRS, points, lanes))] * devices
    me = lax.axis_index("col").astype(jnp.int32).reshape(1)
    far = [
        pltpu.with_memory_space_constraint(array, pltpu.HBM)
        for array in (col_owner.reshape(1, columns), kept_modes, state_now, force_now, force_old)
    ]

    outs = call(
        functools.partial(first_kernel, devices),
        [shaped((8, columns), jnp.int32), shaped((8, lanes))] + [shaped((2, PAIRS, points, lanes))] * devices,
        [SCALAR] + [FAR] * 5,
        [LOCAL] * (2 + devices),
        1,
        [pltpu.VMEM((1, columns), jnp.int32), pltpu.VMEM((2, columns), jnp.int32)]
        + [pltpu.VMEM((comps, points, columns), F32)] * 3
        + [pltpu.SemaphoreType.DMA((2 + 3 * PAIRS,))],
    )(me, *far)
    info, wave = outs[:2]
    forward = exchange(outs[2:], steps)

    square = shaped((depth, depth), BF16)
    operators = call(
        operators_kernel,
        [square] * 4 + [shaped((depth, 3 * depth), BF16), shaped((depth, lanes))],
        [LOCAL] * 4,
        [LOCAL] * 6,
        HEAVY,
    )(second_deriv, eig_inverse, eig_basis, eig_values.reshape(1, depth))
    basis, values = operators[4:]

    begun = call(
        functools.partial(solve_early_kernel, early),
        shaped((depth, width)),
        [SCALAR] + [LOCAL] * (4 + split),
        LOCAL,
        HEAVY,
        [pltpu.VMEM((early_rows, width), F32)] * 2,
    )(me, *operators[:4], *forward[:split])
    outs = call(
        functools.partial(solve_late_kernel, late, steps),
        back + [shaped((PAIRS, depth, lanes))],
        [SCALAR] + [LOCAL] * (8 + len(late)),
        [LOCAL] * (devices + 1),
        1,
        [pltpu.VMEM((late_rows, width), F32)] * 2 + [pltpu.VMEM((depth, width), F32)],
    )(me, wave, values, basis, begun, *operators[:4], *forward[split:])
    solved = outs[devices]
    returned = exchange(outs[:devices], steps)

    early_back, steps_back = near_first(early, devices), near_first(early, devices) + late
    begun, chosen = call(
        functools.partial(surplus_early_kernel, early),
        [shaped((comps * points, columns)), shaped((len(late) * share, columns), BF16)],
        [LOCAL] * (1 + split),
        [LOCAL] * 2,
        HEAVY,
    )(info, *returned[:split])
    outs = call(
        functools.partial(surplus_late_kernel, late, steps_back),
        back,
        [LOCAL] * (2 + len(late)),
        [LOCAL] * devices,
        1,
    )(begun, chosen, *returned[split:])
    extra = exchange(outs, steps_back)

    state_next, emf = call(
        functools.partial(state_kernel, steps),
        [shaped(state_now.shape), shaped((3, points))],
        [LOCAL] * (3 + devices) + [ANYWHERE],
        [FAR, LOCAL],
        HEAVY,
        [pltpu.VMEM(state_now.shape, F32), pltpu.SemaphoreType.DMA],
    )(info, kept_modes, velocity, *returned, extra[early_back.index(3)])
    terms = pair_sums(emf, 1)

    owned = call(
        functools.partial(assemble_early_kernel, early_back),
        shaped((comps, depth, lanes)),
        [SCALAR] + [LOCAL] * (2 + split),
        FAR,
        HEAVY,
        [
            pltpu.VMEM((comps, early_rows, lanes), F32),
            pltpu.SemaphoreType.DMA((comps * early_rows // LANES,)),
        ],
    )(me, info, solved, *extra[:split])
    owned, mean_emf = call(
        functools.partial(assemble_late_kernel, late, len(terms)),
        [shaped((comps, depth, lanes)), shaped((3, points))],
        [SCALAR] + [LOCAL] * (2 + len(late) + len(terms)) + [FAR],
        [FAR, LOCAL],
        1,
        [pltpu.VMEM((comps, late_rows, lanes), F32), pltpu.SemaphoreType.DMA((comps,))],
        aliases={3 + len(late) + len(terms): 0},
    )(me, info, solved, *extra[split:], *terms, owned)
    return (state_next, owned, mean_emf)


def solution(mesh):
    return jax.shard_map(
        on_device,
        mesh=mesh,
        in_specs=(
            P(None, "col", "grp"),
            P(None, "col", "grp"),
            P(None, "col", "grp"),
            P(None, "col", "grp"),
            P(),
            P(),
            P(),
            P(),
            P(None, "grp"),
            P("grp", None),
        ),
        out_specs=(P(None, "col", "grp"), P(None, None, ("grp", "col")), P(None, "col")),
        check_vma=False,
    )
```

```python
import functools

import jax
import jax.numpy as jnp
from jax import lax
from jax.experimental import pallas as pl
from jax.experimental.pallas import tpu as pltpu
from jax.sharding import PartitionSpec as P

KMAX = 2048
TIME_STEP = 2.0
RK_ALPHA = -3.0 / 40.0
RK_BETA = 5.0 / 24.0
RK_GAMMA = 5.0 / 12.0
RK_ZETA = -17.0 / 60.0
WAVE_SCALE = 8.0
VMEM_LIMIT = 24 * 1024 * 1024
PAIRS = 3
LANES = 128
HEAVY = 10

F32 = jnp.float32
BF16 = jnp.bfloat16


def call(body, out_shape, in_specs, out_specs, weight, scratch=(), aliases=None):
    return pl.pallas_call(
        body,
        out_shape=out_shape,
        in_specs=in_specs,
        out_specs=out_specs,
        scratch_shapes=list(scratch),
        input_output_aliases=aliases or {},
        cost_estimate=pl.CostEstimate(flops=weight * 10**9, bytes_accessed=weight * 10**6, transcendentals=0),
        compiler_params=pltpu.CompilerParams(vmem_limit_bytes=VMEM_LIMIT),
    )


LOCAL = pl.BlockSpec(memory_space=pltpu.VMEM)
SCALAR = pl.BlockSpec(memory_space=pltpu.SMEM)
FAR = pl.BlockSpec(memory_space=pltpu.HBM)
ANYWHERE = pl.BlockSpec(memory_space=pl.ANY)


def shaped(shape, dtype=F32):
    return jax.ShapeDtypeStruct(shape, dtype)


def three_parts(x):
    high = x.astype(BF16)
    rest = x - high.astype(F32)
    middle = rest.astype(BF16)
    low = (rest - middle.astype(F32)).astype(BF16)
    return jnp.concatenate([high, middle, low], axis=0)


def sum_parts(x):
    rows = x.shape[0] // 3
    return x[:rows] + x[rows : 2 * rows] + x[2 * rows :]


def two_parts(x):
    high = x.astype(BF16)
    low = (x - high.astype(F32)).astype(BF16)
    return high, low


def arrived(refs):
    return [ref.at[at % 2] for at, ref in enumerate(refs)]


def halves(refs):
    return [ref.at[half] for ref in refs for half in range(2)]


def selector(places, rows):
    columns = places.shape[1]
    return (lax.broadcasted_iota(jnp.int32, (rows, columns), 0) == places).astype(F32).astype(BF16)


def wave_row(modes):
    wave_x = modes[0:1, :].astype(F32)
    wave_z = modes[1:2, :].astype(F32)
    return (wave_x * wave_x + wave_z * wave_z) * (WAVE_SCALE / (KMAX * KMAX))


NT = (((1,), (1,)), ((), ()))


def plan(devices, me, owner, modes):
    columns = owner.shape[1]
    share = columns // devices
    rows = -(-devices // 8) * 8
    owned = (lax.broadcasted_iota(jnp.int32, (rows, columns), 0) == owner).astype(F32)
    before = (
        lax.broadcasted_iota(jnp.int32, (LANES, LANES), 0) < lax.broadcasted_iota(jnp.int32, (LANES, LANES), 1)
    ).astype(F32)
    carry = jnp.zeros((rows, 1), F32)
    earlier = []
    for at in range(columns // LANES):
        block = owned[:, at * LANES : (at + 1) * LANES]
        earlier.append(jnp.dot(block, before, preferred_element_type=F32) + carry)
        carry = carry + jnp.sum(block, axis=1, keepdims=True)
    counts = carry
    rank = jnp.sum(owned * jnp.concatenate(earlier, axis=1), axis=0, keepdims=True)
    surplus = jnp.maximum(counts - share, 0.0)
    lower = (lax.broadcasted_iota(jnp.int32, (rows, columns), 0) < owner).astype(F32)
    number = jnp.sum(lower * surplus, axis=0, keepdims=True) + (rank - share)
    free = share - jnp.minimum(counts, share)
    start = jnp.zeros((1, 1), F32)
    solver = owner
    slot = rank
    beyond = rank >= share
    for device in range(devices):
        here = free[device : device + 1, :]
        inside = beyond & (number >= start) & (number < start + here)
        solver = jnp.where(inside, device, solver)
        slot = jnp.where(inside, share - here + number - start, slot)
        start = start + here
    place = (solver ^ me) * share + slot.astype(jnp.int32)
    extra = jnp.where(beyond, (owner ^ me) * share + rank.astype(jnp.int32) - share, -1)
    mine = jnp.sum((owner == me).astype(F32), axis=1, keepdims=True).astype(jnp.int32)
    info = jnp.concatenate(
        [place, extra, jnp.broadcast_to(mine, (1, columns)), jnp.zeros((5, columns), jnp.int32)], axis=0
    )
    wave = jnp.broadcast_to(wave_row(modes), (16, columns))
    picked = sum_parts(
        lax.dot_general(three_parts(wave), selector(place, share), NT, preferred_element_type=F32)
    )
    return info, jnp.concatenate([picked, picked], axis=1)[:8]


def pack(devices, wave, chosen, state, now, old, out_refs, pair):
    comps, points, columns = state.shape
    share = columns // devices
    wave = wave.reshape(1, 1, columns)
    forcing = RK_GAMMA * now + RK_ZETA * old
    local = state + TIME_STEP * (forcing - RK_ALPHA * (wave * state))
    rows = comps * points
    both = jnp.concatenate([state.reshape(rows, columns), local.reshape(rows, columns)], axis=0)
    placed = sum_parts(lax.dot_general(three_parts(both), chosen, NT, preferred_element_type=F32))
    for step, out in zip(steps_of(devices, points), halves(out_refs)):
        taken = placed[:, step * share : (step + 1) * share]
        for kind in range(2):
            real = 2 * kind * points
            imag = real + points
            out[kind, pair] = jnp.concatenate([taken[real : real + points], taken[imag : imag + points]], axis=1)


def first_kernel(
    devices, me_ref, owner_hbm, modes_hbm, state_hbm, now_hbm, old_hbm, info_ref, wave_ref, *refs
):
    out_refs, (owner_ref, modes_ref, state_ref, now_ref, old_ref, sems) = refs[:-6], refs[-6:]
    columns = owner_ref.shape[1]
    copies = [
        pltpu.make_async_copy(owner_hbm, owner_ref, sems.at[0]),
        pltpu.make_async_copy(modes_hbm, modes_ref, sems.at[1]),
    ]
    for pair in range(PAIRS):
        comps = slice(2 * pair, 2 * pair + 2)
        for at, (source, target) in enumerate(((state_hbm, state_ref), (now_hbm, now_ref), (old_hbm, old_ref))):
            copies.append(
                pltpu.make_async_copy(source.at[comps], target.at[comps], sems.at[2 + 3 * pair + at])
            )
    for copy in copies:
        copy.start()
    copies[0].wait()
    copies[1].wait()
    info, wave = plan(devices, me_ref[0], owner_ref[...], modes_ref[...])
    info_ref[...] = info
    wave_ref[...] = wave
    wave = wave_row(modes_ref[...])
    chosen = selector(info[0:1], columns)
    for pair in range(PAIRS):
        for copy in copies[2 + 3 * pair : 5 + 3 * pair]:
            copy.wait()
        comps = slice(2 * pair, 2 * pair + 2)
        pack(devices, wave, chosen, state_ref[comps], now_ref[comps], old_ref[comps], out_refs, pair)


def operators_kernel(
    deriv_ref, inverse_ref, basis_ref, values_ref, high_out, low_out, both_high_out, both_low_out, basis_out, values_out
):
    high, low = two_parts(inverse_ref[...])
    high_out[...] = high
    low_out[...] = low
    both = (TIME_STEP * RK_ALPHA) * apply(jnp.concatenate([high, high, low], axis=1), deriv_ref[...])
    high, low = two_parts(both)
    both_high_out[...] = high
    both_low_out[...] = low
    high, low = two_parts(basis_ref[...])
    basis_out[...] = jnp.concatenate([high, high, low], axis=1)
    lanes = values_out.shape[1]
    values_out[...] = jnp.transpose(jnp.broadcast_to(values_ref[...], (lanes, values_ref.shape[1])))


def apply(operator, x):
    high, low = two_parts(x)
    return jnp.dot(operator, jnp.concatenate([high, low, high], axis=0), preferred_element_type=F32)


def projected(me, operators, steps, blocks, state, local):
    _, pairs, points, lanes = blocks[0].shape
    fill = LANES // points
    for at, (step, block) in enumerate(zip(steps, blocks)):
        first = at // fill * LANES
        rows = pl.ds(pl.multiple_of(first + ((me ^ step) % fill) * points, points), points)
        for pair in range(pairs):
            state[rows, pair * lanes : (pair + 1) * lanes] = block[0, pair]
            local[rows, pair * lanes : (pair + 1) * lanes] = block[1, pair]
    high, low, both_high, both_low = operators
    matrix, values = [], []
    for first in range(0, len(steps), fill):
        depth = pl.ds(pl.multiple_of((me ^ steps[first]) // fill * LANES, LANES), LANES)
        rows = slice(first // fill * LANES, (first // fill + 1) * LANES)
        for upper, lower, x in ((high, low, local), (both_high, both_low, state)):
            x_high, x_low = two_parts(x[rows, :])
            matrix += [upper[:, depth], upper[:, depth], lower[:, depth]]
            values += [x_high, x_low, x_high]
    return jnp.dot(
        jnp.concatenate(matrix, axis=1), jnp.concatenate(values, axis=0), preferred_element_type=F32
    )


def solve_early_kernel(steps, me_ref, *refs):
    operators, in_refs, (out_ref, state, local) = refs[:4], arrived(refs[4:-3]), refs[-3:]
    out_ref[...] = projected(me_ref[0], operators, steps, in_refs, state, local)


def solve_late_kernel(steps, order, me_ref, wave_ref, values_ref, basis_ref, early_ref, *refs):
    operators, refs = refs[:4], refs[4:]
    in_refs, refs = arrived(refs[: len(steps)]), refs[len(steps) :]
    out_refs, (solved_ref, state, local, after) = halves(refs[:-4]), refs[-4:]
    me = me_ref[0]
    pairs, points, lanes = out_refs[0].shape
    project = early_ref[...] + projected(me, operators, steps, in_refs, state, local)
    damping = 1.0 + TIME_STEP * RK_BETA * (values_ref[...] + wave_ref[0:1, :])
    project = project / jnp.concatenate([damping] * pairs, axis=1)
    after[...] = apply(basis_ref[...], project)
    for pair in range(pairs):
        solved_ref[pair] = after[:, pair * lanes : (pair + 1) * lanes]
    for step, block in zip(order, out_refs):
        rows = pl.ds(pl.multiple_of((me ^ step) * points, points), points)
        for pair in range(pairs):
            block[pair] = after[rows, pair * lanes : (pair + 1) * lanes]


def side_by_side(steps, blocks):
    pairs, _, lanes = blocks[0].shape
    share = lanes // 2
    sorted_blocks = [blocks[steps.index(step)] for step in sorted(steps)]
    rows = []
    for pair in range(pairs):
        for half in range(2):
            rows.append(
                jnp.concatenate(
                    [block[pair][:, half * share : (half + 1) * share] for block in sorted_blocks], axis=1
                )
            )
    return jnp.concatenate(rows, axis=0)


def surplus_early_kernel(steps, info_ref, *refs):
    in_refs, (out_ref, late_ref) = arrived(refs[:-2]), refs[-2:]
    columns = info_ref.shape[1]
    share = in_refs[0].shape[2] // 2
    chosen = lax.dot_general(
        selector(info_ref[0:1, :], columns), selector(info_ref[1:2, :], columns), NT, preferred_element_type=F32
    ).astype(BF16)
    devices = columns // share
    late = [step for step in range(devices) if step not in steps]
    first, last = late[0] * share, (late[-1] + 1) * share
    late_ref[...] = chosen[first:last]
    kept = jnp.concatenate([chosen[:first], chosen[last:]], axis=0)
    out_ref[...] = sum_parts(
        jnp.dot(three_parts(side_by_side(steps, in_refs)), kept, preferred_element_type=F32)
    )


def surplus_late_kernel(steps, order, early_ref, chosen_ref, *refs):
    in_refs, out_refs = arrived(refs[: len(steps)]), halves(refs[len(steps) :])
    pairs, points, lanes = in_refs[0].shape
    share = lanes // 2
    extra = early_ref[...] + sum_parts(
        jnp.dot(three_parts(side_by_side(steps, in_refs)), chosen_ref[...], preferred_element_type=F32)
    )
    for step, out in zip(order, out_refs):
        taken = extra[:, step * share : (step + 1) * share]
        for pair in range(pairs):
            real = 2 * pair * points
            imag = real + points
            out[pair] = jnp.concatenate([taken[real : real + points], taken[imag : imag + points]], axis=1)


def state_kernel(order, info_ref, modes_ref, velocity_ref, *refs):
    in_refs, (_, state_hbm, emf_ref, state_ref, sem) = arrived(refs[: len(order)]), refs[len(order) :]
    comps, points, columns = state_ref.shape
    state = sum_parts(
        jnp.dot(
            three_parts(side_by_side(order, in_refs)),
            selector(info_ref[0:1, :], columns),
            preferred_element_type=F32,
        )
    )
    state_ref[...] = state.reshape(comps, points, columns)
    copy = pltpu.make_async_copy(state_ref, state_hbm, sem)
    copy.start()
    emf_ref[...] = emf_of(modes_ref[...], velocity_ref, state_ref)
    copy.wait()


def emf_of(modes, velocity_ref, state_ref):
    _, points, columns = state_ref.shape
    weight = jnp.where(modes[0:1, :] > 0, 2.0, 1.0).astype(F32)
    totals = [jnp.zeros((points, columns), F32)] * 3
    for field in range(3):
        real = weight * state_ref[2 * field]
        imag = weight * state_ref[2 * field + 1]
        for sign, i, j in ((1.0, (field + 1) % 3, (field + 2) % 3), (-1.0, (field + 2) % 3, (field + 1) % 3)):
            totals[i] = totals[i] + sign * (velocity_ref[2 * j] * real + velocity_ref[2 * j + 1] * imag)
    rows = []
    for total in totals:
        folded = total[:, :LANES]
        for at in range(1, columns // LANES):
            folded = folded + total[:, at * LANES : (at + 1) * LANES]
        rows.append(jnp.sum(jnp.transpose(folded), axis=0, keepdims=True))
    return jnp.concatenate(rows, axis=0)


def assemble(me, steps, used, solved_ref, in_refs, out_hbm, rows_ref, sems):
    pairs, points, lanes = in_refs[0].shape
    share = lanes // 2
    fill = LANES // points
    copies = []
    for first in range(0, len(steps), fill):
        depth = pl.ds(pl.multiple_of((me ^ steps[first]) // fill * LANES, LANES), LANES)
        rows = slice(first // fill * LANES, (first // fill + 1) * LANES)
        for pair in range(pairs):
            solved = solved_ref[pair, depth, :]
            for half in range(2):
                comp = 2 * pair + half
                kept = solved[:, half * share : (half + 1) * share]
                rows_ref[comp, rows, :share] = jnp.where(used < 0, 0.0, kept)
                for at in range(first, first + fill):
                    place = pl.ds(
                        pl.multiple_of(first // fill * LANES + ((me ^ steps[at]) % fill) * points, points), points
                    )
                    rows_ref[comp, place, share:] = in_refs[at][pair][:, half * share : (half + 1) * share]
                copies.append(
                    pltpu.make_async_copy(
                        rows_ref.at[comp, rows], out_hbm.at[comp, depth], sems.at[first // fill * 2 * pairs + comp]
                    )
                )
                copies[-1].start()
    for copy in copies:
        copy.wait()


def unused(info_ref, share):
    lane = lax.broadcasted_iota(jnp.int32, (LANES, share), 1)
    return jnp.where(lane < info_ref[2:3, :share], 0, -1)


def assemble_early_kernel(steps, me_ref, info_ref, solved_ref, *refs):
    in_refs, (out_hbm, rows_ref, sems) = arrived(refs[: len(steps)]), refs[len(steps) :]
    share = in_refs[0].shape[2] // 2
    assemble(me_ref[0], steps, unused(info_ref, share), solved_ref, in_refs, out_hbm, rows_ref, sems)


def assemble_late_kernel(steps, terms, me_ref, info_ref, solved_ref, *refs):
    in_refs, refs = arrived(refs[: len(steps)]), refs[len(steps) :]
    parts, (_, out_hbm, emf_ref, rows_ref, sems) = refs[:terms], refs[terms:]
    parts = [ref[...] for ref in parts]
    while len(parts) > 1:
        parts = [parts[at] + parts[at + 1] for at in range(0, len(parts), 2)]
    emf_ref[...] = parts[0]
    share = in_refs[0].shape[2] // 2
    assemble(me_ref[0], steps, unused(info_ref, share), solved_ref, in_refs, out_hbm, rows_ref, sems)


def late_steps(devices, points):
    return list(range(devices // 2, devices // 2 + LANES // points))


def early_steps(devices, points):
    fill, half = LANES // points, devices // 2
    return list(range(fill)) + list(range(half + fill, devices)) + list(range(fill, half))


def steps_of(devices, points):
    return early_steps(devices, points) + late_steps(devices, points)


def send(blocks, steps):
    devices = len(steps)
    return [
        lax.ppermute(block, "col", [(i, i ^ step) for i in range(devices)]) if step else block
        for step, block in zip(steps[::2], blocks)
    ]


def hand_over(block):
    devices = lax.axis_size("col")
    return lax.ppermute(block, "col", [(i, i ^ 1) for i in range(devices)])


def exchange(blocks, steps):
    return [array for block in send(blocks, steps) for array in (block, hand_over(block))]


def from_groups(value):
    groups = lax.axis_size("grp")
    return [value] + [
        lax.ppermute(value, "grp", [(i, i ^ step) for i in range(groups)]) for step in range(1, groups)
    ]


def on_device(
    state_now,
    force_now,
    force_old,
    velocity,
    second_deriv,
    eig_basis,
    eig_inverse,
    eig_values,
    kept_modes,
    col_owner,
):
    comps, points, columns = state_now.shape
    devices = lax.axis_size("col")
    depth = devices * points
    share = columns // devices
    lanes = 2 * share
    width = PAIRS * lanes
    steps = steps_of(devices, points)
    early, late = early_steps(devices, points), late_steps(devices, points)
    split = len(early)
    early_rows, late_rows = split * points, len(late) * points
    back = [shaped((2, PAIRS, points, lanes))] * (devices // 2)
    me = lax.axis_index("col").astype(jnp.int32).reshape(1)
    far = [
        pltpu.with_memory_space_constraint(array, pltpu.HBM)
        for array in (col_owner.reshape(1, columns), kept_modes, state_now, force_now, force_old)
    ]

    outs = call(
        functools.partial(first_kernel, devices),
        [shaped((8, columns), jnp.int32), shaped((8, lanes))] + [shaped((2, 2, PAIRS, points, lanes))] * (devices // 2),
        [SCALAR] + [FAR] * 5,
        [LOCAL] * (2 + devices // 2),
        1,
        [pltpu.VMEM((1, columns), jnp.int32), pltpu.VMEM((2, columns), jnp.int32)]
        + [pltpu.VMEM((comps, points, columns), F32)] * 3
        + [pltpu.SemaphoreType.DMA((2 + 3 * PAIRS,))],
    )(me, *far)
    info, wave = outs[:2]
    forward = exchange(outs[2:], steps)

    square = shaped((depth, depth), BF16)
    operators = call(
        operators_kernel,
        [square] * 4 + [shaped((depth, 3 * depth), BF16), shaped((depth, lanes))],
        [LOCAL] * 4,
        [LOCAL] * 6,
        HEAVY,
    )(second_deriv, eig_inverse, eig_basis, eig_values.reshape(1, depth))
    basis, values = operators[4:]

    begun = call(
        functools.partial(solve_early_kernel, early),
        shaped((depth, width)),
        [SCALAR] + [LOCAL] * (4 + split),
        LOCAL,
        HEAVY,
        [pltpu.VMEM((early_rows, width), F32)] * 2,
    )(me, *operators[:4], *forward[:split])
    outs = call(
        functools.partial(solve_late_kernel, late, steps),
        back + [shaped((PAIRS, depth, lanes))],
        [SCALAR] + [LOCAL] * (8 + len(late)),
        [LOCAL] * (devices // 2 + 1),
        1,
        [pltpu.VMEM((late_rows, width), F32)] * 2 + [pltpu.VMEM((depth, width), F32)],
    )(me, wave, values, basis, begun, *operators[:4], *forward[split:])
    solved = outs[-1]
    returned = exchange(outs[:-1], steps)

    begun, chosen = call(
        functools.partial(surplus_early_kernel, early),
        [shaped((comps * points, columns)), shaped((len(late) * share, columns), BF16)],
        [LOCAL] * (1 + split),
        [LOCAL] * 2,
        HEAVY,
    )(info, *returned[:split])
    outs = call(
        functools.partial(surplus_late_kernel, late, steps),
        back,
        [LOCAL] * (2 + len(late)),
        [LOCAL] * (devices // 2),
        1,
    )(begun, chosen, *returned[split:])
    sent = send(outs, steps)
    own = steps[::2].index(0)
    handed = hand_over(sent[own])

    state_next, emf = call(
        functools.partial(state_kernel, steps),
        [shaped(state_now.shape), shaped((3, points))],
        [LOCAL] * (3 + devices) + [ANYWHERE],
        [FAR, LOCAL],
        HEAVY,
        [pltpu.VMEM(state_now.shape, F32), pltpu.SemaphoreType.DMA],
    )(info, kept_modes, velocity, *returned, handed)
    terms = from_groups(emf)
    near = steps[::2].index(2)
    sent[near], _ = lax.optimization_barrier((sent[near], terms[-1]))
    extra = [
        array
        for at, block in enumerate(sent)
        for array in (block, handed if at == own else hand_over(block))
    ]

    owned = call(
        functools.partial(assemble_early_kernel, early),
        shaped((comps, depth, lanes)),
        [SCALAR] + [LOCAL] * (2 + split),
        FAR,
        HEAVY,
        [
            pltpu.VMEM((comps, early_rows, lanes), F32),
            pltpu.SemaphoreType.DMA((comps * early_rows // LANES,)),
        ],
    )(me, info, solved, *extra[:split])
    owned, mean_emf = call(
        functools.partial(assemble_late_kernel, late, len(terms)),
        [shaped((comps, depth, lanes)), shaped((3, points))],
        [SCALAR] + [LOCAL] * (2 + len(late) + len(terms)) + [FAR],
        [FAR, LOCAL],
        1,
        [pltpu.VMEM((comps, late_rows, lanes), F32), pltpu.SemaphoreType.DMA((comps,))],
        aliases={3 + len(late) + len(terms): 0},
    )(me, info, solved, *extra[split:], *terms, owned)
    return (state_next, owned, mean_emf)


def solution(mesh):
    return jax.shard_map(
        on_device,
        mesh=mesh,
        in_specs=(
            P(None, "col", "grp"),
            P(None, "col", "grp"),
            P(None, "col", "grp"),
            P(None, "col", "grp"),
            P(),
            P(),
            P(),
            P(),
            P(None, "grp"),
            P("grp", None),
        ),
        out_specs=(P(None, "col", "grp"), P(None, None, ("grp", "col")), P(None, "col")),
        check_vma=False,
    )
```

```python
import functools

import jax
import jax.numpy as jnp
from jax import lax
from jax.experimental import pallas as pl
from jax.experimental.pallas import tpu as pltpu
from jax.sharding import PartitionSpec as P

KMAX = 2048
TIME_STEP = 2.0
RK_ALPHA = -3.0 / 40.0
RK_BETA = 5.0 / 24.0
RK_GAMMA = 5.0 / 12.0
RK_ZETA = -17.0 / 60.0
WAVE_SCALE = 8.0
VMEM_LIMIT = 24 * 1024 * 1024
PAIRS = 3
LANES = 128
HEAVY = 10

F32 = jnp.float32
BF16 = jnp.bfloat16


def call(body, out_shape, in_specs, out_specs, weight, scratch=(), aliases=None):
    return pl.pallas_call(
        body,
        out_shape=out_shape,
        in_specs=in_specs,
        out_specs=out_specs,
        scratch_shapes=list(scratch),
        input_output_aliases=aliases or {},
        cost_estimate=pl.CostEstimate(flops=weight * 10**9, bytes_accessed=weight * 10**6, transcendentals=0),
        compiler_params=pltpu.CompilerParams(vmem_limit_bytes=VMEM_LIMIT),
    )


LOCAL = pl.BlockSpec(memory_space=pltpu.VMEM)
SCALAR = pl.BlockSpec(memory_space=pltpu.SMEM)
FAR = pl.BlockSpec(memory_space=pltpu.HBM)
ANYWHERE = pl.BlockSpec(memory_space=pl.ANY)


def shaped(shape, dtype=F32):
    return jax.ShapeDtypeStruct(shape, dtype)


def three_parts(x):
    high = x.astype(BF16)
    rest = x - high.astype(F32)
    middle = rest.astype(BF16)
    low = (rest - middle.astype(F32)).astype(BF16)
    return jnp.concatenate([high, middle, low], axis=0)


def sum_parts(x):
    rows = x.shape[0] // 3
    return x[:rows] + x[rows : 2 * rows] + x[2 * rows :]


def two_parts(x):
    high = x.astype(BF16)
    low = (x - high.astype(F32)).astype(BF16)
    return high, low


def selector(places, rows):
    columns = places.shape[1]
    return (lax.broadcasted_iota(jnp.int32, (rows, columns), 0) == places).astype(F32).astype(BF16)


def wave_row(modes):
    wave_x = modes[0:1, :].astype(F32)
    wave_z = modes[1:2, :].astype(F32)
    return (wave_x * wave_x + wave_z * wave_z) * (WAVE_SCALE / (KMAX * KMAX))


NT = (((1,), (1,)), ((), ()))


def plan(devices, me, owner, modes):
    columns = owner.shape[1]
    share = columns // devices
    rows = -(-devices // 8) * 8
    owned = (lax.broadcasted_iota(jnp.int32, (rows, columns), 0) == owner).astype(F32)
    before = (
        lax.broadcasted_iota(jnp.int32, (LANES, LANES), 0) < lax.broadcasted_iota(jnp.int32, (LANES, LANES), 1)
    ).astype(F32)
    carry = jnp.zeros((rows, 1), F32)
    earlier = []
    for at in range(columns // LANES):
        block = owned[:, at * LANES : (at + 1) * LANES]
        earlier.append(jnp.dot(block, before, preferred_element_type=F32) + carry)
        carry = carry + jnp.sum(block, axis=1, keepdims=True)
    counts = carry
    rank = jnp.sum(owned * jnp.concatenate(earlier, axis=1), axis=0, keepdims=True)
    surplus = jnp.maximum(counts - share, 0.0)
    lower = (lax.broadcasted_iota(jnp.int32, (rows, columns), 0) < owner).astype(F32)
    number = jnp.sum(lower * surplus, axis=0, keepdims=True) + (rank - share)
    free = share - jnp.minimum(counts, share)
    start = jnp.zeros((1, 1), F32)
    solver = owner
    slot = rank
    beyond = rank >= share
    for device in range(devices):
        here = free[device : device + 1, :]
        inside = beyond & (number >= start) & (number < start + here)
        solver = jnp.where(inside, device, solver)
        slot = jnp.where(inside, share - here + number - start, slot)
        start = start + here
    place = (solver ^ me) * share + slot.astype(jnp.int32)
    extra = jnp.where(beyond, (owner ^ me) * share + rank.astype(jnp.int32) - share, -1)
    mine = jnp.sum((owner == me).astype(F32), axis=1, keepdims=True).astype(jnp.int32)
    info = jnp.concatenate(
        [place, extra, jnp.broadcast_to(mine, (1, columns)), jnp.zeros((5, columns), jnp.int32)], axis=0
    )
    wave = jnp.broadcast_to(wave_row(modes), (16, columns))
    picked = sum_parts(
        lax.dot_general(three_parts(wave), selector(place, share), NT, preferred_element_type=F32)
    )
    return info, jnp.concatenate([picked, picked], axis=1)[:8]


def pack(devices, wave, chosen, state, now, old, out_refs, pair):
    comps, points, columns = state.shape
    share = columns // devices
    wave = wave.reshape(1, 1, columns)
    forcing = RK_GAMMA * now + RK_ZETA * old
    local = state + TIME_STEP * (forcing - RK_ALPHA * (wave * state))
    rows = comps * points
    both = jnp.concatenate([state.reshape(rows, columns), local.reshape(rows, columns)], axis=0)
    placed = sum_parts(lax.dot_general(three_parts(both), chosen, NT, preferred_element_type=F32))
    for step, out in zip(steps_of(devices, points), out_refs):
        taken = placed[:, step * share : (step + 1) * share]
        for kind in range(2):
            real = 2 * kind * points
            imag = real + points
            out[kind, pair] = jnp.concatenate([taken[real : real + points], taken[imag : imag + points]], axis=1)


def first_kernel(
    devices, me_ref, owner_hbm, modes_hbm, state_hbm, now_hbm, old_hbm, info_ref, wave_ref, *refs
):
    out_refs, (owner_ref, modes_ref, state_ref, now_ref, old_ref, sems) = refs[:devices], refs[devices:]
    columns = owner_ref.shape[1]
    copies = [
        pltpu.make_async_copy(owner_hbm, owner_ref, sems.at[0]),
        pltpu.make_async_copy(modes_hbm, modes_ref, sems.at[1]),
    ]
    for pair in range(PAIRS):
        comps = slice(2 * pair, 2 * pair + 2)
        for at, (source, target) in enumerate(((state_hbm, state_ref), (now_hbm, now_ref), (old_hbm, old_ref))):
            copies.append(
                pltpu.make_async_copy(source.at[comps], target.at[comps], sems.at[2 + 3 * pair + at])
            )
    for copy in copies:
        copy.start()
    copies[0].wait()
    copies[1].wait()
    info, wave = plan(devices, me_ref[0], owner_ref[...], modes_ref[...])
    info_ref[...] = info
    wave_ref[...] = wave
    wave = wave_row(modes_ref[...])
    chosen = selector(info[0:1], columns)
    for pair in range(PAIRS):
        for copy in copies[2 + 3 * pair : 5 + 3 * pair]:
            copy.wait()
        comps = slice(2 * pair, 2 * pair + 2)
        pack(devices, wave, chosen, state_ref[comps], now_ref[comps], old_ref[comps], out_refs, pair)


def operators_kernel(
    deriv_ref, inverse_ref, basis_ref, values_ref, high_out, low_out, both_high_out, both_low_out, basis_out, values_out
):
    high, low = two_parts(inverse_ref[...])
    high_out[...] = high
    low_out[...] = low
    both = (TIME_STEP * RK_ALPHA) * apply(jnp.concatenate([high, high, low], axis=1), deriv_ref[...])
    high, low = two_parts(both)
    both_high_out[...] = high
    both_low_out[...] = low
    high, low = two_parts(basis_ref[...])
    basis_out[...] = jnp.concatenate([high, high, low], axis=1)
    lanes = values_out.shape[1]
    values_out[...] = jnp.transpose(jnp.broadcast_to(values_ref[...], (lanes, values_ref.shape[1])))


def apply(operator, x):
    high, low = two_parts(x)
    return jnp.dot(operator, jnp.concatenate([high, low, high], axis=0), preferred_element_type=F32)


def projected(me, operators, steps, blocks, state, local):
    _, pairs, points, lanes = blocks[0].shape
    fill = LANES // points
    for at, (step, block) in enumerate(zip(steps, blocks)):
        first = at // fill * LANES
        rows = pl.ds(pl.multiple_of(first + ((me ^ step) % fill) * points, points), points)
        for pair in range(pairs):
            state[rows, pair * lanes : (pair + 1) * lanes] = block[0, pair]
            local[rows, pair * lanes : (pair + 1) * lanes] = block[1, pair]
    high, low, both_high, both_low = operators
    matrix, values = [], []
    for first in range(0, len(steps), fill):
        depth = pl.ds(pl.multiple_of((me ^ steps[first]) // fill * LANES, LANES), LANES)
        rows = slice(first // fill * LANES, (first // fill + 1) * LANES)
        for upper, lower, x in ((high, low, local), (both_high, both_low, state)):
            x_high, x_low = two_parts(x[rows, :])
            matrix += [upper[:, depth], upper[:, depth], lower[:, depth]]
            values += [x_high, x_low, x_high]
    return jnp.dot(
        jnp.concatenate(matrix, axis=1), jnp.concatenate(values, axis=0), preferred_element_type=F32
    )


def solve_early_kernel(steps, me_ref, *refs):
    operators, in_refs, (out_ref, state, local) = refs[:4], refs[4:-3], refs[-3:]
    out_ref[...] = projected(me_ref[0], operators, steps, in_refs, state, local)


def solve_late_kernel(steps, order, me_ref, wave_ref, values_ref, basis_ref, early_ref, *refs):
    operators, refs = refs[:4], refs[4:]
    in_refs, refs = refs[: len(steps)], refs[len(steps) :]
    out_refs, (solved_ref, state, local, after) = refs[:-4], refs[-4:]
    me = me_ref[0]
    pairs, points, lanes = out_refs[0].shape
    project = early_ref[...] + projected(me, operators, steps, in_refs, state, local)
    damping = 1.0 + TIME_STEP * RK_BETA * (values_ref[...] + wave_ref[0:1, :])
    project = project / jnp.concatenate([damping] * pairs, axis=1)
    after[...] = apply(basis_ref[...], project)
    for pair in range(pairs):
        solved_ref[pair] = after[:, pair * lanes : (pair + 1) * lanes]
    for step, block in zip(order, out_refs):
        rows = pl.ds(pl.multiple_of((me ^ step) * points, points), points)
        for pair in range(pairs):
            block[pair] = after[rows, pair * lanes : (pair + 1) * lanes]


def side_by_side(steps, blocks):
    pairs, _, lanes = blocks[0].shape
    share = lanes // 2
    sorted_blocks = [blocks[steps.index(step)] for step in sorted(steps)]
    rows = []
    for pair in range(pairs):
        for half in range(2):
            rows.append(
                jnp.concatenate(
                    [block[pair][:, half * share : (half + 1) * share] for block in sorted_blocks], axis=1
                )
            )
    return jnp.concatenate(rows, axis=0)


def surplus_early_kernel(steps, info_ref, *refs):
    in_refs, (out_ref, late_ref) = refs[:-2], refs[-2:]
    columns = info_ref.shape[1]
    share = in_refs[0].shape[2] // 2
    chosen = lax.dot_general(
        selector(info_ref[0:1, :], columns), selector(info_ref[1:2, :], columns), NT, preferred_element_type=F32
    ).astype(BF16)
    devices = columns // share
    late = [step for step in range(devices) if step not in steps]
    first, last = late[0] * share, (late[-1] + 1) * share
    late_ref[...] = chosen[first:last]
    kept = jnp.concatenate([chosen[:first], chosen[last:]], axis=0)
    out_ref[...] = sum_parts(
        jnp.dot(three_parts(side_by_side(steps, in_refs)), kept, preferred_element_type=F32)
    )


def surplus_late_kernel(steps, order, early_ref, chosen_ref, *refs):
    in_refs, out_refs = refs[: len(steps)], refs[len(steps) :]
    pairs, points, lanes = in_refs[0].shape
    share = lanes // 2
    extra = early_ref[...] + sum_parts(
        jnp.dot(three_parts(side_by_side(steps, in_refs)), chosen_ref[...], preferred_element_type=F32)
    )
    for step, out in zip(order, out_refs):
        taken = extra[:, step * share : (step + 1) * share]
        for pair in range(pairs):
            real = 2 * pair * points
            imag = real + points
            out[pair] = jnp.concatenate([taken[real : real + points], taken[imag : imag + points]], axis=1)


def state_kernel(order, info_ref, modes_ref, velocity_ref, *refs):
    in_refs, (_, state_hbm, emf_ref, state_ref, sem) = refs[: len(order)], refs[len(order) :]
    comps, points, columns = state_ref.shape
    state = sum_parts(
        jnp.dot(
            three_parts(side_by_side(order, in_refs)),
            selector(info_ref[0:1, :], columns),
            preferred_element_type=F32,
        )
    )
    state_ref[...] = state.reshape(comps, points, columns)
    copy = pltpu.make_async_copy(state_ref, state_hbm, sem)
    copy.start()
    emf_ref[...] = emf_of(modes_ref[...], velocity_ref, state_ref)
    copy.wait()


def emf_of(modes, velocity_ref, state_ref):
    _, points, columns = state_ref.shape
    weight = jnp.where(modes[0:1, :] > 0, 2.0, 1.0).astype(F32)
    totals = [jnp.zeros((points, columns), F32)] * 3
    for field in range(3):
        real = weight * state_ref[2 * field]
        imag = weight * state_ref[2 * field + 1]
        for sign, i, j in ((1.0, (field + 1) % 3, (field + 2) % 3), (-1.0, (field + 2) % 3, (field + 1) % 3)):
            totals[i] = totals[i] + sign * (velocity_ref[2 * j] * real + velocity_ref[2 * j + 1] * imag)
    rows = []
    for total in totals:
        folded = total[:, :LANES]
        for at in range(1, columns // LANES):
            folded = folded + total[:, at * LANES : (at + 1) * LANES]
        rows.append(jnp.sum(jnp.transpose(folded), axis=0, keepdims=True))
    return jnp.concatenate(rows, axis=0)


def assemble(me, steps, used, solved_ref, in_refs, out_hbm, rows_ref, sems):
    pairs, points, lanes = in_refs[0].shape
    share = lanes // 2
    fill = LANES // points
    copies = []
    for first in range(0, len(steps), fill):
        depth = pl.ds(pl.multiple_of((me ^ steps[first]) // fill * LANES, LANES), LANES)
        rows = slice(first // fill * LANES, (first // fill + 1) * LANES)
        for pair in range(pairs):
            solved = solved_ref[pair, depth, :]
            for half in range(2):
                comp = 2 * pair + half
                kept = solved[:, half * share : (half + 1) * share]
                rows_ref[comp, rows, :share] = jnp.where(used < 0, 0.0, kept)
                for at in range(first, first + fill):
                    place = pl.ds(
                        pl.multiple_of(first // fill * LANES + ((me ^ steps[at]) % fill) * points, points), points
                    )
                    rows_ref[comp, place, share:] = in_refs[at][pair][:, half * share : (half + 1) * share]
                copies.append(
                    pltpu.make_async_copy(
                        rows_ref.at[comp, rows], out_hbm.at[comp, depth], sems.at[first // fill * 2 * pairs + comp]
                    )
                )
                copies[-1].start()
    for copy in copies:
        copy.wait()


def unused(info_ref, share):
    lane = lax.broadcasted_iota(jnp.int32, (LANES, share), 1)
    return jnp.where(lane < info_ref[2:3, :share], 0, -1)


def assemble_early_kernel(steps, me_ref, info_ref, solved_ref, *refs):
    in_refs, (out_hbm, rows_ref, sems) = refs[: len(steps)], refs[len(steps) :]
    share = in_refs[0].shape[2] // 2
    assemble(me_ref[0], steps, unused(info_ref, share), solved_ref, in_refs, out_hbm, rows_ref, sems)


def assemble_late_kernel(steps, terms, me_ref, info_ref, solved_ref, *refs):
    in_refs, refs = refs[: len(steps)], refs[len(steps) :]
    parts, (_, out_hbm, emf_ref, rows_ref, sems) = refs[:terms], refs[terms:]
    parts = [ref[...] for ref in parts]
    while len(parts) > 1:
        parts = [parts[at] + parts[at + 1] for at in range(0, len(parts), 2)]
    emf_ref[...] = parts[0]
    share = in_refs[0].shape[2] // 2
    assemble(me_ref[0], steps, unused(info_ref, share), solved_ref, in_refs, out_hbm, rows_ref, sems)


def near_first(steps, devices):
    return [step for step in steps if step < devices // 2] + [step for step in steps if step >= devices // 2]


def late_steps(devices, points):
    return list(range(devices // 2, devices // 2 + LANES // points))


def early_steps(devices, points):
    fill, half = LANES // points, devices // 2
    return list(range(fill)) + list(range(half + fill, devices)) + list(range(fill, half))


def steps_of(devices, points):
    return early_steps(devices, points) + late_steps(devices, points)


def exchange(blocks, steps, held=None, until=None):
    devices = len(blocks)
    arrived = {}
    for step, block in sorted(zip(steps, blocks), key=lambda pair: pair[0] == held):
        if step == held:
            block, _ = lax.optimization_barrier((block, arrived[until]))
        arrived[step] = (
            block if step == 0 else lax.ppermute(block, "col", [(i, i ^ step) for i in range(devices)])
        )
    return [arrived[step] for step in steps]


def pair_sums(value, step):
    groups = lax.axis_size("grp")
    while 2 * step < groups:
        value = value + lax.ppermute(value, "grp", [(i, i ^ step) for i in range(groups)])
        step = 2 * step
    return [value, lax.ppermute(value, "grp", [(i, i ^ step) for i in range(groups)])]


def on_device(
    state_now,
    force_now,
    force_old,
    velocity,
    second_deriv,
    eig_basis,
    eig_inverse,
    eig_values,
    kept_modes,
    col_owner,
):
    comps, points, columns = state_now.shape
    devices = lax.axis_size("col")
    depth = devices * points
    share = columns // devices
    lanes = 2 * share
    width = PAIRS * lanes
    steps = steps_of(devices, points)
    early, late = early_steps(devices, points), late_steps(devices, points)
    split = len(early)
    early_rows, late_rows = split * points, len(late) * points
    back = [shaped((PAIRS, points, lanes))] * devices
    me = lax.axis_index("col").astype(jnp.int32).reshape(1)
    far = [
        pltpu.with_memory_space_constraint(array, pltpu.HBM)
        for array in (col_owner.reshape(1, columns), kept_modes, state_now, force_now, force_old)
    ]

    outs = call(
        functools.partial(first_kernel, devices),
        [shaped((8, columns), jnp.int32), shaped((8, lanes))] + [shaped((2, PAIRS, points, lanes))] * devices,
        [SCALAR] + [FAR] * 5,
        [LOCAL] * (2 + devices),
        1,
        [pltpu.VMEM((1, columns), jnp.int32), pltpu.VMEM((2, columns), jnp.int32)]
        + [pltpu.VMEM((comps, points, columns), F32)] * 3
        + [pltpu.SemaphoreType.DMA((2 + 3 * PAIRS,))],
    )(me, *far)
    info, wave = outs[:2]
    forward = exchange(outs[2:], steps)

    square = shaped((depth, depth), BF16)
    operators = call(
        operators_kernel,
        [square] * 4 + [shaped((depth, 3 * depth), BF16), shaped((depth, lanes))],
        [LOCAL] * 4,
        [LOCAL] * 6,
        HEAVY,
    )(second_deriv, eig_inverse, eig_basis, eig_values.reshape(1, depth))
    basis, values = operators[4:]

    begun = call(
        functools.partial(solve_early_kernel, early),
        shaped((depth, width)),
        [SCALAR] + [LOCAL] * (4 + split),
        LOCAL,
        HEAVY,
        [pltpu.VMEM((early_rows, width), F32)] * 2,
    )(me, *operators[:4], *forward[:split])
    outs = call(
        functools.partial(solve_late_kernel, late, steps),
        back + [shaped((PAIRS, depth, lanes))],
        [SCALAR] + [LOCAL] * (8 + len(late)),
        [LOCAL] * (devices + 1),
        1,
        [pltpu.VMEM((late_rows, width), F32)] * 2 + [pltpu.VMEM((depth, width), F32)],
    )(me, wave, values, basis, begun, *operators[:4], *forward[split:])
    solved = outs[devices]
    returned = exchange(outs[:devices], steps)

    begun, chosen = call(
        functools.partial(surplus_early_kernel, early),
        [shaped((comps * points, columns)), shaped((len(late) * share, columns), BF16)],
        [LOCAL] * (1 + split),
        [LOCAL] * 2,
        HEAVY,
    )(info, *returned[:split])
    outs = call(
        functools.partial(surplus_late_kernel, late, steps),
        back,
        [LOCAL] * (2 + len(late)),
        [LOCAL] * devices,
        1,
    )(begun, chosen, *returned[split:])
    extra = exchange(outs, steps, 2, 1)

    state_next, emf = call(
        functools.partial(state_kernel, steps),
        [shaped(state_now.shape), shaped((3, points))],
        [LOCAL] * (3 + devices) + [ANYWHERE],
        [FAR, LOCAL],
        HEAVY,
        [pltpu.VMEM(state_now.shape, F32), pltpu.SemaphoreType.DMA],
    )(info, kept_modes, velocity, *returned, extra[early.index(1)])
    terms = pair_sums(emf, 1)

    owned = call(
        functools.partial(assemble_early_kernel, early),
        shaped((comps, depth, lanes)),
        [SCALAR] + [LOCAL] * (2 + split),
        FAR,
        HEAVY,
        [
            pltpu.VMEM((comps, early_rows, lanes), F32),
            pltpu.SemaphoreType.DMA((comps * early_rows // LANES,)),
        ],
    )(me, info, solved, *extra[:split])
    owned, mean_emf = call(
        functools.partial(assemble_late_kernel, late, len(terms)),
        [shaped((comps, depth, lanes)), shaped((3, points))],
        [SCALAR] + [LOCAL] * (2 + len(late) + len(terms)) + [FAR],
        [FAR, LOCAL],
        1,
        [pltpu.VMEM((comps, late_rows, lanes), F32), pltpu.SemaphoreType.DMA((comps,))],
        aliases={3 + len(late) + len(terms): 0},
    )(me, info, solved, *extra[split:], *terms, owned)
    return (state_next, owned, mean_emf)


def solution(mesh):
    return jax.shard_map(
        on_device,
        mesh=mesh,
        in_specs=(
            P(None, "col", "grp"),
            P(None, "col", "grp"),
            P(None, "col", "grp"),
            P(None, "col", "grp"),
            P(),
            P(),
            P(),
            P(),
            P(None, "grp"),
            P("grp", None),
        ),
        out_specs=(P(None, "col", "grp"), P(None, None, ("grp", "col")), P(None, "col")),
        check_vma=False,
    )
```

```python
import functools

import jax
import jax.numpy as jnp
from jax import lax
from jax.experimental import pallas as pl
from jax.experimental.pallas import tpu as pltpu
from jax.sharding import PartitionSpec as P

KMAX = 2048
TIME_STEP = 2.0
RK_ALPHA = -3.0 / 40.0
RK_BETA = 5.0 / 24.0
RK_GAMMA = 5.0 / 12.0
RK_ZETA = -17.0 / 60.0
WAVE_SCALE = 8.0
VMEM_LIMIT = 24 * 1024 * 1024
PAIRS = 3
LANES = 128
HEAVY = 10

F32 = jnp.float32
BF16 = jnp.bfloat16


def call(body, out_shape, in_specs, out_specs, weight, scratch=(), aliases=None):
    return pl.pallas_call(
        body,
        out_shape=out_shape,
        in_specs=in_specs,
        out_specs=out_specs,
        scratch_shapes=list(scratch),
        input_output_aliases=aliases or {},
        cost_estimate=pl.CostEstimate(flops=weight * 10**9, bytes_accessed=weight * 10**6, transcendentals=0),
        compiler_params=pltpu.CompilerParams(vmem_limit_bytes=VMEM_LIMIT),
    )


LOCAL = pl.BlockSpec(memory_space=pltpu.VMEM)
SCALAR = pl.BlockSpec(memory_space=pltpu.SMEM)
FAR = pl.BlockSpec(memory_space=pltpu.HBM)
ANYWHERE = pl.BlockSpec(memory_space=pl.ANY)


def shaped(shape, dtype=F32):
    return jax.ShapeDtypeStruct(shape, dtype)


def three_parts(x):
    high = x.astype(BF16)
    rest = x - high.astype(F32)
    middle = rest.astype(BF16)
    low = (rest - middle.astype(F32)).astype(BF16)
    return jnp.concatenate([high, middle, low], axis=0)


def sum_parts(x):
    rows = x.shape[0] // 3
    return x[:rows] + x[rows : 2 * rows] + x[2 * rows :]


def two_parts(x):
    high = x.astype(BF16)
    low = (x - high.astype(F32)).astype(BF16)
    return high, low


def selector(places, rows):
    columns = places.shape[1]
    return (lax.broadcasted_iota(jnp.int32, (rows, columns), 0) == places).astype(F32).astype(BF16)


def wave_row(modes):
    wave_x = modes[0:1, :].astype(F32)
    wave_z = modes[1:2, :].astype(F32)
    return (wave_x * wave_x + wave_z * wave_z) * (WAVE_SCALE / (KMAX * KMAX))


NT = (((1,), (1,)), ((), ()))


def plan(devices, me, owner, modes):
    columns = owner.shape[1]
    share = columns // devices
    rows = -(-devices // 8) * 8
    owned = (lax.broadcasted_iota(jnp.int32, (rows, columns), 0) == owner).astype(F32)
    before = (
        lax.broadcasted_iota(jnp.int32, (LANES, LANES), 0) < lax.broadcasted_iota(jnp.int32, (LANES, LANES), 1)
    ).astype(F32)
    carry = jnp.zeros((rows, 1), F32)
    earlier = []
    for at in range(columns // LANES):
        block = owned[:, at * LANES : (at + 1) * LANES]
        earlier.append(jnp.dot(block, before, preferred_element_type=F32) + carry)
        carry = carry + jnp.sum(block, axis=1, keepdims=True)
    counts = carry
    rank = jnp.sum(owned * jnp.concatenate(earlier, axis=1), axis=0, keepdims=True)
    surplus = jnp.maximum(counts - share, 0.0)
    lower = (lax.broadcasted_iota(jnp.int32, (rows, columns), 0) < owner).astype(F32)
    number = jnp.sum(lower * surplus, axis=0, keepdims=True) + (rank - share)
    free = share - jnp.minimum(counts, share)
    start = jnp.zeros((1, 1), F32)
    solver = owner
    slot = rank
    beyond = rank >= share
    for device in range(devices):
        here = free[device : device + 1, :]
        inside = beyond & (number >= start) & (number < start + here)
        solver = jnp.where(inside, device, solver)
        slot = jnp.where(inside, share - here + number - start, slot)
        start = start + here
    place = (solver ^ me) * share + slot.astype(jnp.int32)
    extra = jnp.where(beyond, (owner ^ me) * share + rank.astype(jnp.int32) - share, -1)
    mine = jnp.sum((owner == me).astype(F32), axis=1, keepdims=True).astype(jnp.int32)
    info = jnp.concatenate(
        [place, extra, jnp.broadcast_to(mine, (1, columns)), jnp.zeros((5, columns), jnp.int32)], axis=0
    )
    wave = jnp.broadcast_to(wave_row(modes), (16, columns))
    picked = sum_parts(
        lax.dot_general(three_parts(wave), selector(place, share), NT, preferred_element_type=F32)
    )
    return info, jnp.concatenate([picked, picked], axis=1)[:8]


def pack(devices, wave, chosen, state, now, old, out_refs, pair):
    comps, points, columns = state.shape
    share = columns // devices
    wave = wave.reshape(1, 1, columns)
    forcing = RK_GAMMA * now + RK_ZETA * old
    local = state + TIME_STEP * (forcing - RK_ALPHA * (wave * state))
    rows = comps * points
    both = jnp.concatenate([state.reshape(rows, columns), local.reshape(rows, columns)], axis=0)
    placed = sum_parts(lax.dot_general(three_parts(both), chosen, NT, preferred_element_type=F32))
    for step, out in zip(steps_of(devices, points), out_refs):
        taken = placed[:, step * share : (step + 1) * share]
        for kind in range(2):
            real = 2 * kind * points
            imag = real + points
            out[kind, pair] = jnp.concatenate([taken[real : real + points], taken[imag : imag + points]], axis=1)


def first_kernel(
    devices, me_ref, owner_hbm, modes_hbm, state_hbm, now_hbm, old_hbm, info_ref, wave_ref, *refs
):
    out_refs, (owner_ref, modes_ref, state_ref, now_ref, old_ref, sems) = refs[:devices], refs[devices:]
    columns = owner_ref.shape[1]
    copies = [
        pltpu.make_async_copy(owner_hbm, owner_ref, sems.at[0]),
        pltpu.make_async_copy(modes_hbm, modes_ref, sems.at[1]),
    ]
    for pair in range(PAIRS):
        comps = slice(2 * pair, 2 * pair + 2)
        for at, (source, target) in enumerate(((state_hbm, state_ref), (now_hbm, now_ref), (old_hbm, old_ref))):
            copies.append(
                pltpu.make_async_copy(source.at[comps], target.at[comps], sems.at[2 + 3 * pair + at])
            )
    for copy in copies:
        copy.start()
    copies[0].wait()
    copies[1].wait()
    info, wave = plan(devices, me_ref[0], owner_ref[...], modes_ref[...])
    info_ref[...] = info
    wave_ref[...] = wave
    wave = wave_row(modes_ref[...])
    chosen = selector(info[0:1], columns)
    for pair in range(PAIRS):
        for copy in copies[2 + 3 * pair : 5 + 3 * pair]:
            copy.wait()
        comps = slice(2 * pair, 2 * pair + 2)
        pack(devices, wave, chosen, state_ref[comps], now_ref[comps], old_ref[comps], out_refs, pair)


def operators_kernel(
    deriv_ref, inverse_ref, basis_ref, values_ref, high_out, low_out, both_high_out, both_low_out, basis_out, values_out
):
    high, low = two_parts(inverse_ref[...])
    high_out[...] = high
    low_out[...] = low
    both = (TIME_STEP * RK_ALPHA) * apply(jnp.concatenate([high, high, low], axis=1), deriv_ref[...])
    high, low = two_parts(both)
    both_high_out[...] = high
    both_low_out[...] = low
    high, low = two_parts(basis_ref[...])
    basis_out[...] = jnp.concatenate([high, high, low], axis=1)
    lanes = values_out.shape[1]
    values_out[...] = jnp.transpose(jnp.broadcast_to(values_ref[...], (lanes, values_ref.shape[1])))


def apply(operator, x):
    high, low = two_parts(x)
    return jnp.dot(operator, jnp.concatenate([high, low, high], axis=0), preferred_element_type=F32)


def projected(me, operators, steps, blocks, state, local):
    _, pairs, points, lanes = blocks[0].shape
    fill = LANES // points
    for at, (step, block) in enumerate(zip(steps, blocks)):
        first = at // fill * LANES
        rows = pl.ds(pl.multiple_of(first + ((me ^ step) % fill) * points, points), points)
        for pair in range(pairs):
            state[rows, pair * lanes : (pair + 1) * lanes] = block[0, pair]
            local[rows, pair * lanes : (pair + 1) * lanes] = block[1, pair]
    high, low, both_high, both_low = operators
    matrix, values = [], []
    for first in range(0, len(steps), fill):
        depth = pl.ds(pl.multiple_of((me ^ steps[first]) // fill * LANES, LANES), LANES)
        rows = slice(first // fill * LANES, (first // fill + 1) * LANES)
        for upper, lower, x in ((high, low, local), (both_high, both_low, state)):
            x_high, x_low = two_parts(x[rows, :])
            matrix += [upper[:, depth], upper[:, depth], lower[:, depth]]
            values += [x_high, x_low, x_high]
    return jnp.dot(
        jnp.concatenate(matrix, axis=1), jnp.concatenate(values, axis=0), preferred_element_type=F32
    )


def solve_early_kernel(steps, me_ref, *refs):
    operators, in_refs, (out_ref, state, local) = refs[:4], refs[4:-3], refs[-3:]
    out_ref[...] = projected(me_ref[0], operators, steps, in_refs, state, local)


def solve_late_kernel(steps, order, me_ref, wave_ref, values_ref, basis_ref, early_ref, *refs):
    operators, refs = refs[:4], refs[4:]
    in_refs, refs = refs[: len(steps)], refs[len(steps) :]
    out_refs, (solved_ref, state, local, after) = refs[:-4], refs[-4:]
    me = me_ref[0]
    pairs, points, lanes = out_refs[0].shape
    project = early_ref[...] + projected(me, operators, steps, in_refs, state, local)
    damping = 1.0 + TIME_STEP * RK_BETA * (values_ref[...] + wave_ref[0:1, :])
    project = project / jnp.concatenate([damping] * pairs, axis=1)
    after[...] = apply(basis_ref[...], project)
    for pair in range(pairs):
        solved_ref[pair] = after[:, pair * lanes : (pair + 1) * lanes]
    for step, block in zip(order, out_refs):
        rows = pl.ds(pl.multiple_of((me ^ step) * points, points), points)
        for pair in range(pairs):
            block[pair] = after[rows, pair * lanes : (pair + 1) * lanes]


def side_by_side(steps, blocks):
    pairs, _, lanes = blocks[0].shape
    share = lanes // 2
    sorted_blocks = [blocks[steps.index(step)] for step in sorted(steps)]
    rows = []
    for pair in range(pairs):
        for half in range(2):
            rows.append(
                jnp.concatenate(
                    [block[pair][:, half * share : (half + 1) * share] for block in sorted_blocks], axis=1
                )
            )
    return jnp.concatenate(rows, axis=0)


def surplus_early_kernel(steps, info_ref, *refs):
    in_refs, (out_ref, late_ref) = refs[:-2], refs[-2:]
    columns = info_ref.shape[1]
    share = in_refs[0].shape[2] // 2
    chosen = lax.dot_general(
        selector(info_ref[0:1, :], columns), selector(info_ref[1:2, :], columns), NT, preferred_element_type=F32
    ).astype(BF16)
    devices = columns // share
    late = [step for step in range(devices) if step not in steps]
    first, last = late[0] * share, (late[-1] + 1) * share
    late_ref[...] = chosen[first:last]
    kept = jnp.concatenate([chosen[:first], chosen[last:]], axis=0)
    out_ref[...] = sum_parts(
        jnp.dot(three_parts(side_by_side(steps, in_refs)), kept, preferred_element_type=F32)
    )


def surplus_late_kernel(steps, order, early_ref, chosen_ref, *refs):
    in_refs, out_refs = refs[: len(steps)], refs[len(steps) :]
    pairs, points, lanes = in_refs[0].shape
    share = lanes // 2
    extra = early_ref[...] + sum_parts(
        jnp.dot(three_parts(side_by_side(steps, in_refs)), chosen_ref[...], preferred_element_type=F32)
    )
    for step, out in zip(order, out_refs):
        taken = extra[:, step * share : (step + 1) * share]
        for pair in range(pairs):
            real = 2 * pair * points
            imag = real + points
            out[pair] = jnp.concatenate([taken[real : real + points], taken[imag : imag + points]], axis=1)


def state_kernel(order, info_ref, modes_ref, velocity_ref, *refs):
    in_refs, (_, state_hbm, emf_ref, state_ref, sem) = refs[: len(order)], refs[len(order) :]
    comps, points, columns = state_ref.shape
    state = sum_parts(
        jnp.dot(
            three_parts(side_by_side(order, in_refs)),
            selector(info_ref[0:1, :], columns),
            preferred_element_type=F32,
        )
    )
    state_ref[...] = state.reshape(comps, points, columns)
    copy = pltpu.make_async_copy(state_ref, state_hbm, sem)
    copy.start()
    emf_ref[...] = emf_of(modes_ref[...], velocity_ref, state_ref)
    copy.wait()


def emf_of(modes, velocity_ref, state_ref):
    _, points, columns = state_ref.shape
    weight = jnp.where(modes[0:1, :] > 0, 2.0, 1.0).astype(F32)
    totals = [jnp.zeros((points, columns), F32)] * 3
    for field in range(3):
        real = weight * state_ref[2 * field]
        imag = weight * state_ref[2 * field + 1]
        for sign, i, j in ((1.0, (field + 1) % 3, (field + 2) % 3), (-1.0, (field + 2) % 3, (field + 1) % 3)):
            totals[i] = totals[i] + sign * (velocity_ref[2 * j] * real + velocity_ref[2 * j + 1] * imag)
    rows = []
    for total in totals:
        folded = total[:, :LANES]
        for at in range(1, columns // LANES):
            folded = folded + total[:, at * LANES : (at + 1) * LANES]
        rows.append(jnp.sum(jnp.transpose(folded), axis=0, keepdims=True))
    return jnp.concatenate(rows, axis=0)


def assemble(me, steps, used, solved_ref, in_refs, out_hbm, rows_ref, sems):
    pairs, points, lanes = in_refs[0].shape
    share = lanes // 2
    fill = LANES // points
    copies = []
    for first in range(0, len(steps), fill):
        depth = pl.ds(pl.multiple_of((me ^ steps[first]) // fill * LANES, LANES), LANES)
        rows = slice(first // fill * LANES, (first // fill + 1) * LANES)
        for pair in range(pairs):
            solved = solved_ref[pair, depth, :]
            for half in range(2):
                comp = 2 * pair + half
                kept = solved[:, half * share : (half + 1) * share]
                rows_ref[comp, rows, :share] = jnp.where(used < 0, 0.0, kept)
                for at in range(first, first + fill):
                    place = pl.ds(
                        pl.multiple_of(first // fill * LANES + ((me ^ steps[at]) % fill) * points, points), points
                    )
                    rows_ref[comp, place, share:] = in_refs[at][pair][:, half * share : (half + 1) * share]
                copies.append(
                    pltpu.make_async_copy(
                        rows_ref.at[comp, rows], out_hbm.at[comp, depth], sems.at[first // fill * 2 * pairs + comp]
                    )
                )
                copies[-1].start()
    for copy in copies:
        copy.wait()


def unused(info_ref, share):
    lane = lax.broadcasted_iota(jnp.int32, (LANES, share), 1)
    return jnp.where(lane < info_ref[2:3, :share], 0, -1)


def assemble_early_kernel(steps, me_ref, info_ref, solved_ref, *refs):
    in_refs, (out_hbm, rows_ref, sems) = refs[: len(steps)], refs[len(steps) :]
    share = in_refs[0].shape[2] // 2
    assemble(me_ref[0], steps, unused(info_ref, share), solved_ref, in_refs, out_hbm, rows_ref, sems)


def assemble_late_kernel(steps, terms, me_ref, info_ref, solved_ref, *refs):
    in_refs, refs = refs[: len(steps)], refs[len(steps) :]
    parts, (_, out_hbm, emf_ref, rows_ref, sems) = refs[:terms], refs[terms:]
    parts = [ref[...] for ref in parts]
    while len(parts) > 1:
        parts = [parts[at] + parts[at + 1] for at in range(0, len(parts), 2)]
    emf_ref[...] = parts[0]
    share = in_refs[0].shape[2] // 2
    assemble(me_ref[0], steps, unused(info_ref, share), solved_ref, in_refs, out_hbm, rows_ref, sems)


def near_first(steps, devices):
    return [step for step in steps if step < devices // 2] + [step for step in steps if step >= devices // 2]


def late_steps(devices, points):
    return list(range(devices // 2, devices // 2 + LANES // points))


def early_steps(devices, points):
    fill, half = LANES // points, devices // 2
    return list(range(fill)) + list(range(half + fill, devices)) + list(range(fill, half))


def steps_of(devices, points):
    return early_steps(devices, points) + late_steps(devices, points)


def exchange(blocks, steps, held=None, until=None):
    devices = len(blocks)
    arrived = {}
    for step, block in sorted(zip(steps, blocks), key=lambda pair: pair[0] == held):
        if step == held:
            block, _ = lax.optimization_barrier((block, arrived[until]))
        arrived[step] = (
            block if step == 0 else lax.ppermute(block, "col", [(i, i ^ step) for i in range(devices)])
        )
    return [arrived[step] for step in steps]


def from_groups(value):
    groups = lax.axis_size("grp")
    return [value] + [
        lax.ppermute(value, "grp", [(i, i ^ step) for i in range(groups)]) for step in range(1, groups)
    ]


def on_device(
    state_now,
    force_now,
    force_old,
    velocity,
    second_deriv,
    eig_basis,
    eig_inverse,
    eig_values,
    kept_modes,
    col_owner,
):
    comps, points, columns = state_now.shape
    devices = lax.axis_size("col")
    depth = devices * points
    share = columns // devices
    lanes = 2 * share
    width = PAIRS * lanes
    steps = steps_of(devices, points)
    early, late = early_steps(devices, points), late_steps(devices, points)
    split = len(early)
    early_rows, late_rows = split * points, len(late) * points
    back = [shaped((PAIRS, points, lanes))] * devices
    me = lax.axis_index("col").astype(jnp.int32).reshape(1)
    far = [
        pltpu.with_memory_space_constraint(array, pltpu.HBM)
        for array in (col_owner.reshape(1, columns), kept_modes, state_now, force_now, force_old)
    ]

    outs = call(
        functools.partial(first_kernel, devices),
        [shaped((8, columns), jnp.int32), shaped((8, lanes))] + [shaped((2, PAIRS, points, lanes))] * devices,
        [SCALAR] + [FAR] * 5,
        [LOCAL] * (2 + devices),
        1,
        [pltpu.VMEM((1, columns), jnp.int32), pltpu.VMEM((2, columns), jnp.int32)]
        + [pltpu.VMEM((comps, points, columns), F32)] * 3
        + [pltpu.SemaphoreType.DMA((2 + 3 * PAIRS,))],
    )(me, *far)
    info, wave = outs[:2]
    forward = exchange(outs[2:], steps)

    square = shaped((depth, depth), BF16)
    operators = call(
        operators_kernel,
        [square] * 4 + [shaped((depth, 3 * depth), BF16), shaped((depth, lanes))],
        [LOCAL] * 4,
        [LOCAL] * 6,
        HEAVY,
    )(second_deriv, eig_inverse, eig_basis, eig_values.reshape(1, depth))
    basis, values = operators[4:]

    begun = call(
        functools.partial(solve_early_kernel, early),
        shaped((depth, width)),
        [SCALAR] + [LOCAL] * (4 + split),
        LOCAL,
        HEAVY,
        [pltpu.VMEM((early_rows, width), F32)] * 2,
    )(me, *operators[:4], *forward[:split])
    outs = call(
        functools.partial(solve_late_kernel, late, steps),
        back + [shaped((PAIRS, depth, lanes))],
        [SCALAR] + [LOCAL] * (8 + len(late)),
        [LOCAL] * (devices + 1),
        1,
        [pltpu.VMEM((late_rows, width), F32)] * 2 + [pltpu.VMEM((depth, width), F32)],
    )(me, wave, values, basis, begun, *operators[:4], *forward[split:])
    solved = outs[devices]
    returned = exchange(outs[:devices], steps)

    begun, chosen = call(
        functools.partial(surplus_early_kernel, early),
        [shaped((comps * points, columns)), shaped((len(late) * share, columns), BF16)],
        [LOCAL] * (1 + split),
        [LOCAL] * 2,
        HEAVY,
    )(info, *returned[:split])
    outs = call(
        functools.partial(surplus_late_kernel, late, steps),
        back,
        [LOCAL] * (2 + len(late)),
        [LOCAL] * devices,
        1,
    )(begun, chosen, *returned[split:])
    extra = exchange(outs, steps, 2, 1)

    state_next, emf = call(
        functools.partial(state_kernel, steps),
        [shaped(state_now.shape), shaped((3, points))],
        [LOCAL] * (3 + devices) + [ANYWHERE],
        [FAR, LOCAL],
        HEAVY,
        [pltpu.VMEM(state_now.shape, F32), pltpu.SemaphoreType.DMA],
    )(info, kept_modes, velocity, *returned, extra[early.index(1)])
    terms = from_groups(emf)

    owned = call(
        functools.partial(assemble_early_kernel, early),
        shaped((comps, depth, lanes)),
        [SCALAR] + [LOCAL] * (2 + split),
        FAR,
        HEAVY,
        [
            pltpu.VMEM((comps, early_rows, lanes), F32),
            pltpu.SemaphoreType.DMA((comps * early_rows // LANES,)),
        ],
    )(me, info, solved, *extra[:split])
    owned, mean_emf = call(
        functools.partial(assemble_late_kernel, late, len(terms)),
        [shaped((comps, depth, lanes)), shaped((3, points))],
        [SCALAR] + [LOCAL] * (2 + len(late) + len(terms)) + [FAR],
        [FAR, LOCAL],
        1,
        [pltpu.VMEM((comps, late_rows, lanes), F32), pltpu.SemaphoreType.DMA((comps,))],
        aliases={3 + len(late) + len(terms): 0},
    )(me, info, solved, *extra[split:], *terms, owned)
    return (state_next, owned, mean_emf)


def solution(mesh):
    return jax.shard_map(
        on_device,
        mesh=mesh,
        in_specs=(
            P(None, "col", "grp"),
            P(None, "col", "grp"),
            P(None, "col", "grp"),
            P(None, "col", "grp"),
            P(),
            P(),
            P(),
            P(),
            P(None, "grp"),
            P("grp", None),
        ),
        out_specs=(P(None, "col", "grp"), P(None, None, ("grp", "col")), P(None, "col")),
        check_vma=False,
    )
```

```python
import functools

import jax
import jax.numpy as jnp
from jax import lax
from jax.experimental import pallas as pl
from jax.experimental.pallas import tpu as pltpu
from jax.sharding import PartitionSpec as P

KMAX = 2048
TIME_STEP = 2.0
RK_ALPHA = -3.0 / 40.0
RK_BETA = 5.0 / 24.0
RK_GAMMA = 5.0 / 12.0
RK_ZETA = -17.0 / 60.0
WAVE_SCALE = 8.0
VMEM_LIMIT = 24 * 1024 * 1024
PAIRS = 3
LANES = 128
HEAVY = 10

F32 = jnp.float32
BF16 = jnp.bfloat16


def call(body, out_shape, in_specs, out_specs, weight, scratch=(), aliases=None):
    return pl.pallas_call(
        body,
        out_shape=out_shape,
        in_specs=in_specs,
        out_specs=out_specs,
        scratch_shapes=list(scratch),
        input_output_aliases=aliases or {},
        cost_estimate=pl.CostEstimate(flops=weight * 10**9, bytes_accessed=weight * 10**6, transcendentals=0),
        compiler_params=pltpu.CompilerParams(vmem_limit_bytes=VMEM_LIMIT),
    )


LOCAL = pl.BlockSpec(memory_space=pltpu.VMEM)
SCALAR = pl.BlockSpec(memory_space=pltpu.SMEM)
FAR = pl.BlockSpec(memory_space=pltpu.HBM)
ANYWHERE = pl.BlockSpec(memory_space=pl.ANY)


def shaped(shape, dtype=F32):
    return jax.ShapeDtypeStruct(shape, dtype)


def three_parts(x):
    high = x.astype(BF16)
    rest = x - high.astype(F32)
    middle = rest.astype(BF16)
    low = (rest - middle.astype(F32)).astype(BF16)
    return jnp.concatenate([high, middle, low], axis=0)


def sum_parts(x):
    rows = x.shape[0] // 3
    return x[:rows] + x[rows : 2 * rows] + x[2 * rows :]


def two_parts(x):
    high = x.astype(BF16)
    low = (x - high.astype(F32)).astype(BF16)
    return high, low


def selector(places, rows):
    columns = places.shape[1]
    return (lax.broadcasted_iota(jnp.int32, (rows, columns), 0) == places).astype(F32).astype(BF16)


def wave_row(modes):
    wave_x = modes[0:1, :].astype(F32)
    wave_z = modes[1:2, :].astype(F32)
    return (wave_x * wave_x + wave_z * wave_z) * (WAVE_SCALE / (KMAX * KMAX))


NT = (((1,), (1,)), ((), ()))


def plan(devices, me, owner, modes):
    columns = owner.shape[1]
    share = columns // devices
    rows = -(-devices // 8) * 8
    owned = (lax.broadcasted_iota(jnp.int32, (rows, columns), 0) == owner).astype(F32)
    before = (
        lax.broadcasted_iota(jnp.int32, (LANES, LANES), 0) < lax.broadcasted_iota(jnp.int32, (LANES, LANES), 1)
    ).astype(F32)
    carry = jnp.zeros((rows, 1), F32)
    earlier = []
    for at in range(columns // LANES):
        block = owned[:, at * LANES : (at + 1) * LANES]
        earlier.append(jnp.dot(block, before, preferred_element_type=F32) + carry)
        carry = carry + jnp.sum(block, axis=1, keepdims=True)
    counts = carry
    rank = jnp.sum(owned * jnp.concatenate(earlier, axis=1), axis=0, keepdims=True)
    surplus = jnp.maximum(counts - share, 0.0)
    lower = (lax.broadcasted_iota(jnp.int32, (rows, columns), 0) < owner).astype(F32)
    number = jnp.sum(lower * surplus, axis=0, keepdims=True) + (rank - share)
    free = share - jnp.minimum(counts, share)
    start = jnp.zeros((1, 1), F32)
    solver = owner
    slot = rank
    beyond = rank >= share
    for device in range(devices):
        here = free[device : device + 1, :]
        inside = beyond & (number >= start) & (number < start + here)
        solver = jnp.where(inside, device, solver)
        slot = jnp.where(inside, share - here + number - start, slot)
        start = start + here
    place = (solver ^ me) * share + slot.astype(jnp.int32)
    extra = jnp.where(beyond, (owner ^ me) * share + rank.astype(jnp.int32) - share, -1)
    mine = jnp.sum((owner == me).astype(F32), axis=1, keepdims=True).astype(jnp.int32)
    info = jnp.concatenate(
        [place, extra, jnp.broadcast_to(mine, (1, columns)), jnp.zeros((5, columns), jnp.int32)], axis=0
    )
    wave = jnp.broadcast_to(wave_row(modes), (16, columns))
    picked = sum_parts(
        lax.dot_general(three_parts(wave), selector(place, share), NT, preferred_element_type=F32)
    )
    return info, jnp.concatenate([picked, picked], axis=1)[:8]


def pack(devices, wave, chosen, state, now, old, out_refs, pair):
    comps, points, columns = state.shape
    share = columns // devices
    wave = wave.reshape(1, 1, columns)
    forcing = RK_GAMMA * now + RK_ZETA * old
    local = state + TIME_STEP * (forcing - RK_ALPHA * (wave * state))
    rows = comps * points
    both = jnp.concatenate([state.reshape(rows, columns), local.reshape(rows, columns)], axis=0)
    high, low = two_parts(both)
    placed = lax.dot_general(jnp.concatenate([high, low], axis=0), chosen, NT, preferred_element_type=F32)
    placed = placed[: 2 * rows] + placed[2 * rows :]
    for step, out in zip(steps_of(devices, points), out_refs):
        taken = placed[:, step * share : (step + 1) * share]
        for kind in range(2):
            real = 2 * kind * points
            imag = real + points
            out[kind, pair] = jnp.concatenate([taken[real : real + points], taken[imag : imag + points]], axis=1)


def first_kernel(
    devices, me_ref, owner_hbm, modes_hbm, state_hbm, now_hbm, old_hbm, info_ref, wave_ref, *refs
):
    out_refs, (owner_ref, modes_ref, state_ref, now_ref, old_ref, sems) = refs[:devices], refs[devices:]
    columns = owner_ref.shape[1]
    copies = [
        pltpu.make_async_copy(owner_hbm, owner_ref, sems.at[0]),
        pltpu.make_async_copy(modes_hbm, modes_ref, sems.at[1]),
    ]
    for pair in range(PAIRS):
        comps = slice(2 * pair, 2 * pair + 2)
        for at, (source, target) in enumerate(((state_hbm, state_ref), (now_hbm, now_ref), (old_hbm, old_ref))):
            copies.append(
                pltpu.make_async_copy(source.at[comps], target.at[comps], sems.at[2 + 3 * pair + at])
            )
    for copy in copies:
        copy.start()
    copies[0].wait()
    copies[1].wait()
    info, wave = plan(devices, me_ref[0], owner_ref[...], modes_ref[...])
    info_ref[...] = info
    wave_ref[...] = wave
    wave = wave_row(modes_ref[...])
    chosen = selector(info[0:1], columns)
    for pair in range(PAIRS):
        for copy in copies[2 + 3 * pair : 5 + 3 * pair]:
            copy.wait()
        comps = slice(2 * pair, 2 * pair + 2)
        pack(devices, wave, chosen, state_ref[comps], now_ref[comps], old_ref[comps], out_refs, pair)


def operators_kernel(
    deriv_ref, inverse_ref, basis_ref, values_ref, high_out, low_out, both_high_out, both_low_out, basis_out, values_out
):
    high, low = two_parts(inverse_ref[...])
    high_out[...] = high
    low_out[...] = low
    both = (TIME_STEP * RK_ALPHA) * apply(jnp.concatenate([high, high, low], axis=1), deriv_ref[...])
    high, low = two_parts(both)
    both_high_out[...] = high
    both_low_out[...] = low
    high, low = two_parts(basis_ref[...])
    basis_out[...] = jnp.concatenate([high, high, low], axis=1)
    lanes = values_out.shape[1]
    values_out[...] = jnp.transpose(jnp.broadcast_to(values_ref[...], (lanes, values_ref.shape[1])))


def apply(operator, x):
    high, low = two_parts(x)
    return jnp.dot(operator, jnp.concatenate([high, low, high], axis=0), preferred_element_type=F32)


def projected(me, operators, steps, blocks, state, local):
    _, pairs, points, lanes = blocks[0].shape
    fill = LANES // points
    for at, (step, block) in enumerate(zip(steps, blocks)):
        first = at // fill * LANES
        rows = pl.ds(pl.multiple_of(first + ((me ^ step) % fill) * points, points), points)
        for pair in range(pairs):
            state[rows, pair * lanes : (pair + 1) * lanes] = block[0, pair]
            local[rows, pair * lanes : (pair + 1) * lanes] = block[1, pair]
    high, low, both_high, both_low = operators
    matrix, values = [], []
    for first in range(0, len(steps), fill):
        depth = pl.ds(pl.multiple_of((me ^ steps[first]) // fill * LANES, LANES), LANES)
        rows = slice(first // fill * LANES, (first // fill + 1) * LANES)
        for upper, lower, x in ((high, low, local), (both_high, both_low, state)):
            x_high, x_low = two_parts(x[rows, :])
            matrix += [upper[:, depth], upper[:, depth], lower[:, depth]]
            values += [x_high, x_low, x_high]
    return jnp.dot(
        jnp.concatenate(matrix, axis=1), jnp.concatenate(values, axis=0), preferred_element_type=F32
    )


def solve_early_kernel(steps, me_ref, *refs):
    operators, in_refs, (out_ref, state, local) = refs[:4], refs[4:-3], refs[-3:]
    out_ref[...] = projected(me_ref[0], operators, steps, in_refs, state, local)


def solve_late_kernel(steps, order, me_ref, wave_ref, values_ref, basis_ref, early_ref, *refs):
    operators, refs = refs[:4], refs[4:]
    in_refs, refs = refs[: len(steps)], refs[len(steps) :]
    out_refs, (solved_ref, state, local, after) = refs[:-4], refs[-4:]
    me = me_ref[0]
    pairs, points, lanes = out_refs[0].shape
    project = early_ref[...] + projected(me, operators, steps, in_refs, state, local)
    damping = 1.0 + TIME_STEP * RK_BETA * (values_ref[...] + wave_ref[0:1, :])
    project = project / jnp.concatenate([damping] * pairs, axis=1)
    after[...] = apply(basis_ref[...], project)
    for pair in range(pairs):
        solved_ref[pair] = after[:, pair * lanes : (pair + 1) * lanes]
    for step, block in zip(order, out_refs):
        rows = pl.ds(pl.multiple_of((me ^ step) * points, points), points)
        for pair in range(pairs):
            block[pair] = after[rows, pair * lanes : (pair + 1) * lanes]


def side_by_side(steps, blocks):
    pairs, _, lanes = blocks[0].shape
    share = lanes // 2
    sorted_blocks = [blocks[steps.index(step)] for step in sorted(steps)]
    rows = []
    for pair in range(pairs):
        for half in range(2):
            rows.append(
                jnp.concatenate(
                    [block[pair][:, half * share : (half + 1) * share] for block in sorted_blocks], axis=1
                )
            )
    return jnp.concatenate(rows, axis=0)


def surplus_early_kernel(steps, info_ref, *refs):
    in_refs, (out_ref, late_ref) = refs[:-2], refs[-2:]
    columns = info_ref.shape[1]
    share = in_refs[0].shape[2] // 2
    chosen = lax.dot_general(
        selector(info_ref[0:1, :], columns), selector(info_ref[1:2, :], columns), NT, preferred_element_type=F32
    ).astype(BF16)
    devices = columns // share
    late = [step for step in range(devices) if step not in steps]
    first, last = late[0] * share, (late[-1] + 1) * share
    late_ref[...] = chosen[first:last]
    kept = jnp.concatenate([chosen[:first], chosen[last:]], axis=0)
    out_ref[...] = sum_parts(
        jnp.dot(three_parts(side_by_side(steps, in_refs)), kept, preferred_element_type=F32)
    )


def surplus_late_kernel(steps, order, early_ref, chosen_ref, *refs):
    in_refs, out_refs = refs[: len(steps)], refs[len(steps) :]
    pairs, points, lanes = in_refs[0].shape
    share = lanes // 2
    extra = early_ref[...] + sum_parts(
        jnp.dot(three_parts(side_by_side(steps, in_refs)), chosen_ref[...], preferred_element_type=F32)
    )
    for step, out in zip(order, out_refs):
        taken = extra[:, step * share : (step + 1) * share]
        for pair in range(pairs):
            real = 2 * pair * points
            imag = real + points
            out[pair] = jnp.concatenate([taken[real : real + points], taken[imag : imag + points]], axis=1)


def state_kernel(order, info_ref, modes_ref, velocity_ref, *refs):
    in_refs, (_, state_hbm, emf_ref, state_ref, sem) = refs[: len(order)], refs[len(order) :]
    comps, points, columns = state_ref.shape
    state = sum_parts(
        jnp.dot(
            three_parts(side_by_side(order, in_refs)),
            selector(info_ref[0:1, :], columns),
            preferred_element_type=F32,
        )
    )
    state_ref[...] = state.reshape(comps, points, columns)
    copy = pltpu.make_async_copy(state_ref, state_hbm, sem)
    copy.start()
    emf_ref[...] = emf_of(modes_ref[...], velocity_ref, state_ref)
    copy.wait()


def emf_of(modes, velocity_ref, state_ref):
    _, points, columns = state_ref.shape
    weight = jnp.where(modes[0:1, :] > 0, 2.0, 1.0).astype(F32)
    totals = [jnp.zeros((points, columns), F32)] * 3
    for field in range(3):
        real = weight * state_ref[2 * field]
        imag = weight * state_ref[2 * field + 1]
        for sign, i, j in ((1.0, (field + 1) % 3, (field + 2) % 3), (-1.0, (field + 2) % 3, (field + 1) % 3)):
            totals[i] = totals[i] + sign * (velocity_ref[2 * j] * real + velocity_ref[2 * j + 1] * imag)
    rows = []
    for total in totals:
        folded = total[:, :LANES]
        for at in range(1, columns // LANES):
            folded = folded + total[:, at * LANES : (at + 1) * LANES]
        rows.append(jnp.sum(jnp.transpose(folded), axis=0, keepdims=True))
    return jnp.concatenate(rows, axis=0)


def assemble(me, steps, used, solved_ref, in_refs, out_hbm, rows_ref, sems):
    pairs, points, lanes = in_refs[0].shape
    share = lanes // 2
    fill = LANES // points
    copies = []
    for first in range(0, len(steps), fill):
        depth = pl.ds(pl.multiple_of((me ^ steps[first]) // fill * LANES, LANES), LANES)
        rows = slice(first // fill * LANES, (first // fill + 1) * LANES)
        for pair in range(pairs):
            solved = solved_ref[pair, depth, :]
            for half in range(2):
                comp = 2 * pair + half
                kept = solved[:, half * share : (half + 1) * share]
                rows_ref[comp, rows, :share] = jnp.where(used < 0, 0.0, kept)
                for at in range(first, first + fill):
                    place = pl.ds(
                        pl.multiple_of(first // fill * LANES + ((me ^ steps[at]) % fill) * points, points), points
                    )
                    rows_ref[comp, place, share:] = in_refs[at][pair][:, half * share : (half + 1) * share]
                copies.append(
                    pltpu.make_async_copy(
                        rows_ref.at[comp, rows], out_hbm.at[comp, depth], sems.at[first // fill * 2 * pairs + comp]
                    )
                )
                copies[-1].start()
    for copy in copies:
        copy.wait()


def unused(info_ref, share):
    lane = lax.broadcasted_iota(jnp.int32, (LANES, share), 1)
    return jnp.where(lane < info_ref[2:3, :share], 0, -1)


def assemble_early_kernel(steps, me_ref, info_ref, solved_ref, *refs):
    in_refs, (out_hbm, rows_ref, sems) = refs[: len(steps)], refs[len(steps) :]
    share = in_refs[0].shape[2] // 2
    assemble(me_ref[0], steps, unused(info_ref, share), solved_ref, in_refs, out_hbm, rows_ref, sems)


def assemble_late_kernel(steps, me_ref, info_ref, solved_ref, *refs):
    in_refs, (_, out_hbm, rows_ref, sems) = refs[: len(steps)], refs[len(steps) :]
    share = in_refs[0].shape[2] // 2
    assemble(me_ref[0], steps, unused(info_ref, share), solved_ref, in_refs, out_hbm, rows_ref, sems)


def near_first(steps, devices):
    return [step for step in steps if step < devices // 2] + [step for step in steps if step >= devices // 2]


def late_steps(devices, points):
    return list(range(devices // 2, devices // 2 + LANES // points))


def early_steps(devices, points):
    fill, half = LANES // points, devices // 2
    return list(range(fill)) + list(range(half + fill, devices)) + list(range(fill, half))


def steps_of(devices, points):
    return early_steps(devices, points) + late_steps(devices, points)


def exchange(blocks, steps, held=None, until=None):
    devices = len(blocks)
    arrived = {}
    for step, block in sorted(zip(steps, blocks), key=lambda pair: pair[0] == held):
        if step == held:
            block, _ = lax.optimization_barrier((block, arrived[until]))
        arrived[step] = (
            block if step == 0 else lax.ppermute(block, "col", [(i, i ^ step) for i in range(devices)])
        )
    return [arrived[step] for step in steps]


def from_groups(value):
    groups = lax.axis_size("grp")
    return [value] + [
        lax.ppermute(value, "grp", [(i, i ^ step) for i in range(groups)]) for step in range(1, groups)
    ]


def on_device(
    state_now,
    force_now,
    force_old,
    velocity,
    second_deriv,
    eig_basis,
    eig_inverse,
    eig_values,
    kept_modes,
    col_owner,
):
    comps, points, columns = state_now.shape
    devices = lax.axis_size("col")
    depth = devices * points
    share = columns // devices
    lanes = 2 * share
    width = PAIRS * lanes
    steps = steps_of(devices, points)
    early, late = early_steps(devices, points), late_steps(devices, points)
    split = len(early)
    early_rows, late_rows = split * points, len(late) * points
    back = [shaped((PAIRS, points, lanes))] * devices
    me = lax.axis_index("col").astype(jnp.int32).reshape(1)
    far = [
        pltpu.with_memory_space_constraint(array, pltpu.HBM)
        for array in (col_owner.reshape(1, columns), kept_modes, state_now, force_now, force_old)
    ]

    outs = call(
        functools.partial(first_kernel, devices),
        [shaped((8, columns), jnp.int32), shaped((8, lanes))] + [shaped((2, PAIRS, points, lanes))] * devices,
        [SCALAR] + [FAR] * 5,
        [LOCAL] * (2 + devices),
        1,
        [pltpu.VMEM((1, columns), jnp.int32), pltpu.VMEM((2, columns), jnp.int32)]
        + [pltpu.VMEM((comps, points, columns), F32)] * 3
        + [pltpu.SemaphoreType.DMA((2 + 3 * PAIRS,))],
    )(me, *far)
    info, wave = outs[:2]
    forward = exchange(outs[2:], steps)

    square = shaped((depth, depth), BF16)
    operators = call(
        operators_kernel,
        [square] * 4 + [shaped((depth, 3 * depth), BF16), shaped((depth, lanes))],
        [LOCAL] * 4,
        [LOCAL] * 6,
        HEAVY,
    )(second_deriv, eig_inverse, eig_basis, eig_values.reshape(1, depth))
    basis, values = operators[4:]

    begun = call(
        functools.partial(solve_early_kernel, early),
        shaped((depth, width)),
        [SCALAR] + [LOCAL] * (4 + split),
        LOCAL,
        HEAVY,
        [pltpu.VMEM((early_rows, width), F32)] * 2,
    )(me, *operators[:4], *forward[:split])
    outs = call(
        functools.partial(solve_late_kernel, late, steps),
        back + [shaped((PAIRS, depth, lanes))],
        [SCALAR] + [LOCAL] * (8 + len(late)),
        [LOCAL] * (devices + 1),
        1,
        [pltpu.VMEM((late_rows, width), F32)] * 2 + [pltpu.VMEM((depth, width), F32)],
    )(me, wave, values, basis, begun, *operators[:4], *forward[split:])
    solved = outs[devices]
    returned = exchange(outs[:devices], steps)

    begun, chosen = call(
        functools.partial(surplus_early_kernel, early),
        [shaped((comps * points, columns)), shaped((len(late) * share, columns), BF16)],
        [LOCAL] * (1 + split),
        [LOCAL] * 2,
        HEAVY,
    )(info, *returned[:split])
    outs = call(
        functools.partial(surplus_late_kernel, late, steps),
        back,
        [LOCAL] * (2 + len(late)),
        [LOCAL] * devices,
        1,
    )(begun, chosen, *returned[split:])
    extra = exchange(outs, steps, 2, 1)

    state_next, emf = call(
        functools.partial(state_kernel, steps),
        [shaped(state_now.shape), shaped((3, points))],
        [LOCAL] * (3 + devices) + [ANYWHERE],
        [FAR, LOCAL],
        HEAVY,
        [pltpu.VMEM(state_now.shape, F32), pltpu.SemaphoreType.DMA],
    )(info, kept_modes, velocity, *returned, extra[early.index(1)])
    terms = from_groups(emf)

    owned = call(
        functools.partial(assemble_early_kernel, early),
        shaped((comps, depth, lanes)),
        [SCALAR] + [LOCAL] * (2 + split),
        FAR,
        HEAVY,
        [
            pltpu.VMEM((comps, early_rows, lanes), F32),
            pltpu.SemaphoreType.DMA((comps * early_rows // LANES,)),
        ],
    )(me, info, solved, *extra[:split])
    owned = call(
        functools.partial(assemble_late_kernel, late),
        shaped((comps, depth, lanes)),
        [SCALAR] + [LOCAL] * (2 + len(late)) + [FAR],
        FAR,
        1,
        [pltpu.VMEM((comps, late_rows, lanes), F32), pltpu.SemaphoreType.DMA((comps,))],
        aliases={3 + len(late): 0},
    )(me, info, solved, *extra[split:], owned)
    while len(terms) > 1:
        terms = [terms[at] + terms[at + 1] for at in range(0, len(terms), 2)]
    mean_emf = terms[0]
    return (state_next, owned, mean_emf)


def solution(mesh):
    return jax.shard_map(
        on_device,
        mesh=mesh,
        in_specs=(
            P(None, "col", "grp"),
            P(None, "col", "grp"),
            P(None, "col", "grp"),
            P(None, "col", "grp"),
            P(),
            P(),
            P(),
            P(),
            P(None, "grp"),
            P("grp", None),
        ),
        out_specs=(P(None, "col", "grp"), P(None, None, ("grp", "col")), P(None, "col")),
        check_vma=False,
    )
```

```python
import functools

import jax
import jax.numpy as jnp
from jax import lax
from jax.experimental import pallas as pl
from jax.experimental.pallas import tpu as pltpu
from jax.sharding import PartitionSpec as P

KMAX = 2048
TIME_STEP = 2.0
RK_ALPHA = -3.0 / 40.0
RK_BETA = 5.0 / 24.0
RK_GAMMA = 5.0 / 12.0
RK_ZETA = -17.0 / 60.0
WAVE_SCALE = 8.0
VMEM_LIMIT = 24 * 1024 * 1024
PAIRS = 3
LANES = 128
HEAVY = 10

F32 = jnp.float32
BF16 = jnp.bfloat16


def call(body, out_shape, in_specs, out_specs, weight, scratch=(), aliases=None):
    return pl.pallas_call(
        body,
        out_shape=out_shape,
        in_specs=in_specs,
        out_specs=out_specs,
        scratch_shapes=list(scratch),
        input_output_aliases=aliases or {},
        cost_estimate=pl.CostEstimate(flops=weight * 10**9, bytes_accessed=weight * 10**6, transcendentals=0),
        compiler_params=pltpu.CompilerParams(vmem_limit_bytes=VMEM_LIMIT),
    )


LOCAL = pl.BlockSpec(memory_space=pltpu.VMEM)
SCALAR = pl.BlockSpec(memory_space=pltpu.SMEM)
FAR = pl.BlockSpec(memory_space=pltpu.HBM)
ANYWHERE = pl.BlockSpec(memory_space=pl.ANY)


def shaped(shape, dtype=F32):
    return jax.ShapeDtypeStruct(shape, dtype)


def three_parts(x):
    high = x.astype(BF16)
    rest = x - high.astype(F32)
    middle = rest.astype(BF16)
    low = (rest - middle.astype(F32)).astype(BF16)
    return jnp.concatenate([high, middle, low], axis=0)


def sum_parts(x):
    rows = x.shape[0] // 3
    return x[:rows] + x[rows : 2 * rows] + x[2 * rows :]


def two_parts(x):
    high = x.astype(BF16)
    low = (x - high.astype(F32)).astype(BF16)
    return high, low


def selector(places, rows):
    columns = places.shape[1]
    return (lax.broadcasted_iota(jnp.int32, (rows, columns), 0) == places).astype(F32).astype(BF16)


def wave_row(modes):
    wave_x = modes[0:1, :].astype(F32)
    wave_z = modes[1:2, :].astype(F32)
    return (wave_x * wave_x + wave_z * wave_z) * (WAVE_SCALE / (KMAX * KMAX))


NT = (((1,), (1,)), ((), ()))


def plan(devices, me, owner, modes):
    columns = owner.shape[1]
    share = columns // devices
    rows = -(-devices // 8) * 8
    owned = (lax.broadcasted_iota(jnp.int32, (rows, columns), 0) == owner).astype(F32)
    before = (
        lax.broadcasted_iota(jnp.int32, (LANES, LANES), 0) < lax.broadcasted_iota(jnp.int32, (LANES, LANES), 1)
    ).astype(F32)
    carry = jnp.zeros((rows, 1), F32)
    earlier = []
    for at in range(columns // LANES):
        block = owned[:, at * LANES : (at + 1) * LANES]
        earlier.append(jnp.dot(block, before, preferred_element_type=F32) + carry)
        carry = carry + jnp.sum(block, axis=1, keepdims=True)
    counts = carry
    rank = jnp.sum(owned * jnp.concatenate(earlier, axis=1), axis=0, keepdims=True)
    surplus = jnp.maximum(counts - share, 0.0)
    lower = (lax.broadcasted_iota(jnp.int32, (rows, columns), 0) < owner).astype(F32)
    number = jnp.sum(lower * surplus, axis=0, keepdims=True) + (rank - share)
    free = share - jnp.minimum(counts, share)
    start = jnp.zeros((1, 1), F32)
    solver = owner
    slot = rank
    beyond = rank >= share
    for device in range(devices):
        here = free[device : device + 1, :]
        inside = beyond & (number >= start) & (number < start + here)
        solver = jnp.where(inside, device, solver)
        slot = jnp.where(inside, share - here + number - start, slot)
        start = start + here
    place = (solver ^ me) * share + slot.astype(jnp.int32)
    extra = jnp.where(beyond, (owner ^ me) * share + rank.astype(jnp.int32) - share, -1)
    mine = jnp.sum((owner == me).astype(F32), axis=1, keepdims=True).astype(jnp.int32)
    info = jnp.concatenate(
        [place, extra, jnp.broadcast_to(mine, (1, columns)), jnp.zeros((5, columns), jnp.int32)], axis=0
    )
    wave = jnp.broadcast_to(wave_row(modes), (16, columns))
    picked = sum_parts(
        lax.dot_general(three_parts(wave), selector(place, share), NT, preferred_element_type=F32)
    )
    return info, jnp.concatenate([picked, picked], axis=1)[:8]


def pack(devices, wave, chosen, state, now, old, out_refs, pair):
    comps, points, columns = state.shape
    share = columns // devices
    wave = wave.reshape(1, 1, columns)
    forcing = RK_GAMMA * now + RK_ZETA * old
    local = state + TIME_STEP * (forcing - RK_ALPHA * (wave * state))
    rows = comps * points
    both = jnp.concatenate([state.reshape(rows, columns), local.reshape(rows, columns)], axis=0)
    high, low = two_parts(both)
    placed = lax.dot_general(jnp.concatenate([high, low], axis=0), chosen, NT, preferred_element_type=F32)
    placed = placed[: 2 * rows] + placed[2 * rows :]
    for step, out in zip(steps_of(devices, points), out_refs):
        taken = placed[:, step * share : (step + 1) * share]
        for kind in range(2):
            real = 2 * kind * points
            imag = real + points
            out[kind, pair] = jnp.concatenate([taken[real : real + points], taken[imag : imag + points]], axis=1)


def first_kernel(
    devices, me_ref, owner_hbm, modes_hbm, state_hbm, now_hbm, old_hbm, info_ref, wave_ref, *refs
):
    out_refs, (owner_ref, modes_ref, state_ref, now_ref, old_ref, sems) = refs[:devices], refs[devices:]
    columns = owner_ref.shape[1]
    copies = [
        pltpu.make_async_copy(owner_hbm, owner_ref, sems.at[0]),
        pltpu.make_async_copy(modes_hbm, modes_ref, sems.at[1]),
    ]
    for pair in range(PAIRS):
        comps = slice(2 * pair, 2 * pair + 2)
        for at, (source, target) in enumerate(((state_hbm, state_ref), (now_hbm, now_ref), (old_hbm, old_ref))):
            copies.append(
                pltpu.make_async_copy(source.at[comps], target.at[comps], sems.at[2 + 3 * pair + at])
            )
    for copy in copies:
        copy.start()
    copies[0].wait()
    copies[1].wait()
    info, wave = plan(devices, me_ref[0], owner_ref[...], modes_ref[...])
    info_ref[...] = info
    wave_ref[...] = wave
    wave = wave_row(modes_ref[...])
    chosen = selector(info[0:1], columns)
    for pair in range(PAIRS):
        for copy in copies[2 + 3 * pair : 5 + 3 * pair]:
            copy.wait()
        comps = slice(2 * pair, 2 * pair + 2)
        pack(devices, wave, chosen, state_ref[comps], now_ref[comps], old_ref[comps], out_refs, pair)


def operators_kernel(
    deriv_ref, inverse_ref, basis_ref, values_ref, high_out, low_out, both_high_out, both_low_out, basis_out, values_out
):
    high, low = two_parts(inverse_ref[...])
    high_out[...] = high
    low_out[...] = low
    both = (TIME_STEP * RK_ALPHA) * apply(jnp.concatenate([high, high, low], axis=1), deriv_ref[...])
    high, low = two_parts(both)
    both_high_out[...] = high
    both_low_out[...] = low
    high, low = two_parts(basis_ref[...])
    basis_out[...] = jnp.concatenate([high, high, low], axis=1)
    lanes = values_out.shape[1]
    values_out[...] = jnp.transpose(jnp.broadcast_to(values_ref[...], (lanes, values_ref.shape[1])))


def apply(operator, x):
    high, low = two_parts(x)
    return jnp.dot(operator, jnp.concatenate([high, low, high], axis=0), preferred_element_type=F32)


def projected(me, operators, steps, blocks, state, local):
    _, pairs, points, lanes = blocks[0].shape
    fill = LANES // points
    for at, (step, block) in enumerate(zip(steps, blocks)):
        first = at // fill * LANES
        rows = pl.ds(pl.multiple_of(first + ((me ^ step) % fill) * points, points), points)
        for pair in range(pairs):
            state[rows, pair * lanes : (pair + 1) * lanes] = block[0, pair]
            local[rows, pair * lanes : (pair + 1) * lanes] = block[1, pair]
    high, low, both_high, both_low = operators
    matrix, values = [], []
    for first in range(0, len(steps), fill):
        depth = pl.ds(pl.multiple_of((me ^ steps[first]) // fill * LANES, LANES), LANES)
        rows = slice(first // fill * LANES, (first // fill + 1) * LANES)
        for upper, lower, x in ((high, low, local), (both_high, both_low, state)):
            x_high, x_low = two_parts(x[rows, :])
            matrix += [upper[:, depth], upper[:, depth], lower[:, depth]]
            values += [x_high, x_low, x_high]
    return jnp.dot(
        jnp.concatenate(matrix, axis=1), jnp.concatenate(values, axis=0), preferred_element_type=F32
    )


def solve_early_kernel(steps, me_ref, *refs):
    operators, in_refs, (out_ref, state, local) = refs[:4], refs[4:-3], refs[-3:]
    out_ref[...] = projected(me_ref[0], operators, steps, in_refs, state, local)


def solve_late_kernel(steps, order, me_ref, wave_ref, values_ref, basis_ref, early_ref, *refs):
    operators, refs = refs[:4], refs[4:]
    in_refs, refs = refs[: len(steps)], refs[len(steps) :]
    out_refs, (solved_ref, state, local, after) = refs[:-4], refs[-4:]
    me = me_ref[0]
    pairs, points, lanes = out_refs[0].shape
    project = early_ref[...] + projected(me, operators, steps, in_refs, state, local)
    damping = 1.0 + TIME_STEP * RK_BETA * (values_ref[...] + wave_ref[0:1, :])
    project = project / jnp.concatenate([damping] * pairs, axis=1)
    after[...] = apply(basis_ref[...], project)
    for pair in range(pairs):
        solved_ref[pair] = after[:, pair * lanes : (pair + 1) * lanes]
    for step, block in zip(order, out_refs):
        rows = pl.ds(pl.multiple_of((me ^ step) * points, points), points)
        for pair in range(pairs):
            block[pair] = after[rows, pair * lanes : (pair + 1) * lanes]


def side_by_side(steps, blocks):
    pairs, _, lanes = blocks[0].shape
    share = lanes // 2
    sorted_blocks = [blocks[steps.index(step)] for step in sorted(steps)]
    rows = []
    for pair in range(pairs):
        for half in range(2):
            rows.append(
                jnp.concatenate(
                    [block[pair][:, half * share : (half + 1) * share] for block in sorted_blocks], axis=1
                )
            )
    return jnp.concatenate(rows, axis=0)


def surplus_early_kernel(steps, info_ref, *refs):
    in_refs, (out_ref, late_ref) = refs[:-2], refs[-2:]
    columns = info_ref.shape[1]
    share = in_refs[0].shape[2] // 2
    chosen = lax.dot_general(
        selector(info_ref[0:1, :], columns), selector(info_ref[1:2, :], columns), NT, preferred_element_type=F32
    ).astype(BF16)
    devices = columns // share
    late = [step for step in range(devices) if step not in steps]
    first, last = late[0] * share, (late[-1] + 1) * share
    late_ref[...] = chosen[first:last]
    kept = jnp.concatenate([chosen[:first], chosen[last:]], axis=0)
    out_ref[...] = sum_parts(
        jnp.dot(three_parts(side_by_side(steps, in_refs)), kept, preferred_element_type=F32)
    )


def surplus_late_kernel(steps, order, early_ref, chosen_ref, *refs):
    in_refs, out_refs = refs[: len(steps)], refs[len(steps) :]
    pairs, points, lanes = in_refs[0].shape
    share = lanes // 2
    extra = early_ref[...] + sum_parts(
        jnp.dot(three_parts(side_by_side(steps, in_refs)), chosen_ref[...], preferred_element_type=F32)
    )
    for step, out in zip(order, out_refs):
        taken = extra[:, step * share : (step + 1) * share]
        for pair in range(pairs):
            real = 2 * pair * points
            imag = real + points
            out[pair] = jnp.concatenate([taken[real : real + points], taken[imag : imag + points]], axis=1)


def state_kernel(order, info_ref, modes_ref, velocity_ref, *refs):
    in_refs, (_, state_hbm, emf_ref, state_ref, sem) = refs[: len(order)], refs[len(order) :]
    comps, points, columns = state_ref.shape
    state = sum_parts(
        jnp.dot(
            three_parts(side_by_side(order, in_refs)),
            selector(info_ref[0:1, :], columns),
            preferred_element_type=F32,
        )
    )
    state_ref[...] = state.reshape(comps, points, columns)
    copy = pltpu.make_async_copy(state_ref, state_hbm, sem)
    copy.start()
    emf_ref[...] = emf_of(modes_ref[...], velocity_ref, state_ref)
    copy.wait()


def emf_of(modes, velocity_ref, state_ref):
    _, points, columns = state_ref.shape
    weight = jnp.where(modes[0:1, :] > 0, 2.0, 1.0).astype(F32)
    totals = [jnp.zeros((points, columns), F32)] * 3
    for field in range(3):
        real = weight * state_ref[2 * field]
        imag = weight * state_ref[2 * field + 1]
        for sign, i, j in ((1.0, (field + 1) % 3, (field + 2) % 3), (-1.0, (field + 2) % 3, (field + 1) % 3)):
            totals[i] = totals[i] + sign * (velocity_ref[2 * j] * real + velocity_ref[2 * j + 1] * imag)
    rows = []
    for total in totals:
        folded = total[:, :LANES]
        for at in range(1, columns // LANES):
            folded = folded + total[:, at * LANES : (at + 1) * LANES]
        rows.append(jnp.sum(jnp.transpose(folded), axis=0, keepdims=True))
    return jnp.concatenate(rows, axis=0)


def assemble(me, steps, used, solved_ref, in_refs, out_hbm, rows_ref, sems):
    pairs, points, lanes = in_refs[0].shape
    share = lanes // 2
    fill = LANES // points
    copies = []
    for first in range(0, len(steps), fill):
        depth = pl.ds(pl.multiple_of((me ^ steps[first]) // fill * LANES, LANES), LANES)
        rows = slice(first // fill * LANES, (first // fill + 1) * LANES)
        for pair in range(pairs):
            solved = solved_ref[pair, depth, :]
            for half in range(2):
                comp = 2 * pair + half
                kept = solved[:, half * share : (half + 1) * share]
                rows_ref[comp, rows, :share] = jnp.where(used < 0, 0.0, kept)
                for at in range(first, first + fill):
                    place = pl.ds(
                        pl.multiple_of(first // fill * LANES + ((me ^ steps[at]) % fill) * points, points), points
                    )
                    rows_ref[comp, place, share:] = in_refs[at][pair][:, half * share : (half + 1) * share]
                copies.append(
                    pltpu.make_async_copy(
                        rows_ref.at[comp, rows], out_hbm.at[comp, depth], sems.at[first // fill * 2 * pairs + comp]
                    )
                )
                copies[-1].start()
    for copy in copies:
        copy.wait()


def unused(info_ref, share):
    lane = lax.broadcasted_iota(jnp.int32, (LANES, share), 1)
    return jnp.where(lane < info_ref[2:3, :share], 0, -1)


def assemble_early_kernel(steps, me_ref, info_ref, solved_ref, *refs):
    in_refs, (out_hbm, rows_ref, sems) = refs[: len(steps)], refs[len(steps) :]
    share = in_refs[0].shape[2] // 2
    assemble(me_ref[0], steps, unused(info_ref, share), solved_ref, in_refs, out_hbm, rows_ref, sems)


def assemble_late_kernel(steps, terms, me_ref, info_ref, solved_ref, *refs):
    in_refs, refs = refs[: len(steps)], refs[len(steps) :]
    parts, (_, out_hbm, emf_ref, rows_ref, sems) = refs[:terms], refs[terms:]
    parts = [ref[...] for ref in parts]
    while len(parts) > 1:
        parts = [parts[at] + parts[at + 1] for at in range(0, len(parts), 2)]
    emf_ref[...] = parts[0]
    share = in_refs[0].shape[2] // 2
    assemble(me_ref[0], steps, unused(info_ref, share), solved_ref, in_refs, out_hbm, rows_ref, sems)


def near_first(steps, devices):
    return [step for step in steps if step < devices // 2] + [step for step in steps if step >= devices // 2]


def late_steps(devices, points):
    return list(range(devices // 2, devices // 2 + LANES // points))


def early_steps(devices, points):
    fill, half = LANES // points, devices // 2
    return list(range(fill)) + list(range(half + fill, devices)) + list(range(fill, half))


def steps_of(devices, points):
    return early_steps(devices, points) + late_steps(devices, points)


def exchange(blocks, steps, held=None, until=None):
    devices = len(blocks)
    arrived = {}
    for step, block in sorted(zip(steps, blocks), key=lambda pair: pair[0] == held):
        if step == held:
            block, _ = lax.optimization_barrier((block, arrived[until]))
        arrived[step] = (
            block if step == 0 else lax.ppermute(block, "col", [(i, i ^ step) for i in range(devices)])
        )
    return [arrived[step] for step in steps]


def from_groups(value):
    groups = lax.axis_size("grp")
    return [value] + [
        lax.ppermute(value, "grp", [(i, i ^ step) for i in range(groups)]) for step in range(1, groups)
    ]


def on_device(
    state_now,
    force_now,
    force_old,
    velocity,
    second_deriv,
    eig_basis,
    eig_inverse,
    eig_values,
    kept_modes,
    col_owner,
):
    comps, points, columns = state_now.shape
    devices = lax.axis_size("col")
    depth = devices * points
    share = columns // devices
    lanes = 2 * share
    width = PAIRS * lanes
    steps = steps_of(devices, points)
    early, late = early_steps(devices, points), late_steps(devices, points)
    split = len(early)
    early_rows, late_rows = split * points, len(late) * points
    back = [shaped((PAIRS, points, lanes))] * devices
    me = lax.axis_index("col").astype(jnp.int32).reshape(1)
    far = [
        pltpu.with_memory_space_constraint(array, pltpu.HBM)
        for array in (col_owner.reshape(1, columns), kept_modes, state_now, force_now, force_old)
    ]

    outs = call(
        functools.partial(first_kernel, devices),
        [shaped((8, columns), jnp.int32), shaped((8, lanes))] + [shaped((2, PAIRS, points, lanes))] * devices,
        [SCALAR] + [FAR] * 5,
        [LOCAL] * (2 + devices),
        1,
        [pltpu.VMEM((1, columns), jnp.int32), pltpu.VMEM((2, columns), jnp.int32)]
        + [pltpu.VMEM((comps, points, columns), F32)] * 3
        + [pltpu.SemaphoreType.DMA((2 + 3 * PAIRS,))],
    )(me, *far)
    info, wave = outs[:2]
    forward = exchange(outs[2:], steps)

    square = shaped((depth, depth), BF16)
    operators = call(
        operators_kernel,
        [square] * 4 + [shaped((depth, 3 * depth), BF16), shaped((depth, lanes))],
        [LOCAL] * 4,
        [LOCAL] * 6,
        HEAVY,
    )(second_deriv, eig_inverse, eig_basis, eig_values.reshape(1, depth))
    basis, values = operators[4:]

    begun = call(
        functools.partial(solve_early_kernel, early),
        shaped((depth, width)),
        [SCALAR] + [LOCAL] * (4 + split),
        LOCAL,
        HEAVY,
        [pltpu.VMEM((early_rows, width), F32)] * 2,
    )(me, *operators[:4], *forward[:split])
    outs = call(
        functools.partial(solve_late_kernel, late, steps),
        back + [shaped((PAIRS, depth, lanes))],
        [SCALAR] + [LOCAL] * (8 + len(late)),
        [LOCAL] * (devices + 1),
        1,
        [pltpu.VMEM((late_rows, width), F32)] * 2 + [pltpu.VMEM((depth, width), F32)],
    )(me, wave, values, basis, begun, *operators[:4], *forward[split:])
    solved = outs[devices]
    returned = exchange(outs[:devices], steps)

    begun, chosen = call(
        functools.partial(surplus_early_kernel, early),
        [shaped((comps * points, columns)), shaped((len(late) * share, columns), BF16)],
        [LOCAL] * (1 + split),
        [LOCAL] * 2,
        HEAVY,
    )(info, *returned[:split])
    outs = call(
        functools.partial(surplus_late_kernel, late, steps),
        back,
        [LOCAL] * (2 + len(late)),
        [LOCAL] * devices,
        1,
    )(begun, chosen, *returned[split:])
    extra = exchange(outs, steps, 2, 1)

    state_next, emf = call(
        functools.partial(state_kernel, steps),
        [shaped(state_now.shape), shaped((3, points))],
        [LOCAL] * (3 + devices) + [ANYWHERE],
        [FAR, LOCAL],
        HEAVY,
        [pltpu.VMEM(state_now.shape, F32), pltpu.SemaphoreType.DMA],
    )(info, kept_modes, velocity, *returned, extra[early.index(1)])
    terms = from_groups(emf)

    owned = call(
        functools.partial(assemble_early_kernel, early),
        shaped((comps, depth, lanes)),
        [SCALAR] + [LOCAL] * (2 + split),
        FAR,
        HEAVY,
        [
            pltpu.VMEM((comps, early_rows, lanes), F32),
            pltpu.SemaphoreType.DMA((comps * early_rows // LANES,)),
        ],
    )(me, info, solved, *extra[:split])
    owned, mean_emf = call(
        functools.partial(assemble_late_kernel, late, len(terms)),
        [shaped((comps, depth, lanes)), shaped((3, points))],
        [SCALAR] + [LOCAL] * (2 + len(late) + len(terms)) + [FAR],
        [FAR, LOCAL],
        1,
        [pltpu.VMEM((comps, late_rows, lanes), F32), pltpu.SemaphoreType.DMA((comps,))],
        aliases={3 + len(late) + len(terms): 0},
    )(me, info, solved, *extra[split:], *terms, owned)
    return (state_next, owned, mean_emf)


def solution(mesh):
    return jax.shard_map(
        on_device,
        mesh=mesh,
        in_specs=(
            P(None, "col", "grp"),
            P(None, "col", "grp"),
            P(None, "col", "grp"),
            P(None, "col", "grp"),
            P(),
            P(),
            P(),
            P(),
            P(None, "grp"),
            P("grp", None),
        ),
        out_specs=(P(None, "col", "grp"), P(None, None, ("grp", "col")), P(None, "col")),
        check_vma=False,
    )
```

```python
import functools

import jax
import jax.numpy as jnp
from jax import lax
from jax.experimental import pallas as pl
from jax.experimental.pallas import tpu as pltpu
from jax.sharding import PartitionSpec as P

KMAX = 2048
TIME_STEP = 2.0
RK_ALPHA = -3.0 / 40.0
RK_BETA = 5.0 / 24.0
RK_GAMMA = 5.0 / 12.0
RK_ZETA = -17.0 / 60.0
WAVE_SCALE = 8.0
VMEM_LIMIT = 24 * 1024 * 1024
PAIRS = 3
LANES = 128
HEAVY = 10

F32 = jnp.float32
BF16 = jnp.bfloat16


def call(body, out_shape, in_specs, out_specs, weight, scratch=(), aliases=None):
    return pl.pallas_call(
        body,
        out_shape=out_shape,
        in_specs=in_specs,
        out_specs=out_specs,
        scratch_shapes=list(scratch),
        input_output_aliases=aliases or {},
        cost_estimate=pl.CostEstimate(flops=weight * 10**9, bytes_accessed=weight * 10**6, transcendentals=0),
        compiler_params=pltpu.CompilerParams(vmem_limit_bytes=VMEM_LIMIT),
    )


LOCAL = pl.BlockSpec(memory_space=pltpu.VMEM)
SCALAR = pl.BlockSpec(memory_space=pltpu.SMEM)
FAR = pl.BlockSpec(memory_space=pltpu.HBM)
ANYWHERE = pl.BlockSpec(memory_space=pl.ANY)


def shaped(shape, dtype=F32):
    return jax.ShapeDtypeStruct(shape, dtype)


def three_parts(x):
    high = x.astype(BF16)
    rest = x - high.astype(F32)
    middle = rest.astype(BF16)
    low = (rest - middle.astype(F32)).astype(BF16)
    return jnp.concatenate([high, middle, low], axis=0)


def sum_parts(x):
    rows = x.shape[0] // 3
    return x[:rows] + x[rows : 2 * rows] + x[2 * rows :]


def two_parts(x):
    high = x.astype(BF16)
    low = (x - high.astype(F32)).astype(BF16)
    return high, low


def selector(places, rows):
    columns = places.shape[1]
    return (lax.broadcasted_iota(jnp.int32, (rows, columns), 0) == places).astype(F32).astype(BF16)


def wave_row(modes):
    wave_x = modes[0:1, :].astype(F32)
    wave_z = modes[1:2, :].astype(F32)
    return (wave_x * wave_x + wave_z * wave_z) * (WAVE_SCALE / (KMAX * KMAX))


NT = (((1,), (1,)), ((), ()))


def plan(devices, me, owner, modes):
    columns = owner.shape[1]
    share = columns // devices
    rows = -(-devices // 8) * 8
    owned = (lax.broadcasted_iota(jnp.int32, (rows, columns), 0) == owner).astype(F32)
    before = (
        lax.broadcasted_iota(jnp.int32, (LANES, LANES), 0) < lax.broadcasted_iota(jnp.int32, (LANES, LANES), 1)
    ).astype(F32)
    carry = jnp.zeros((rows, 1), F32)
    earlier = []
    for at in range(columns // LANES):
        block = owned[:, at * LANES : (at + 1) * LANES]
        earlier.append(jnp.dot(block, before, preferred_element_type=F32) + carry)
        carry = carry + jnp.sum(block, axis=1, keepdims=True)
    counts = carry
    rank = jnp.sum(owned * jnp.concatenate(earlier, axis=1), axis=0, keepdims=True)
    surplus = jnp.maximum(counts - share, 0.0)
    lower = (lax.broadcasted_iota(jnp.int32, (rows, columns), 0) < owner).astype(F32)
    number = jnp.sum(lower * surplus, axis=0, keepdims=True) + (rank - share)
    free = share - jnp.minimum(counts, share)
    start = jnp.zeros((1, 1), F32)
    solver = owner
    slot = rank
    beyond = rank >= share
    for device in range(devices):
        here = free[device : device + 1, :]
        inside = beyond & (number >= start) & (number < start + here)
        solver = jnp.where(inside, device, solver)
        slot = jnp.where(inside, share - here + number - start, slot)
        start = start + here
    place = (solver ^ me) * share + slot.astype(jnp.int32)
    extra = jnp.where(beyond, (owner ^ me) * share + rank.astype(jnp.int32) - share, -1)
    mine = jnp.sum((owner == me).astype(F32), axis=1, keepdims=True).astype(jnp.int32)
    info = jnp.concatenate(
        [place, extra, jnp.broadcast_to(mine, (1, columns)), jnp.zeros((5, columns), jnp.int32)], axis=0
    )
    wave = jnp.broadcast_to(wave_row(modes), (16, columns))
    picked = sum_parts(
        lax.dot_general(three_parts(wave), selector(place, share), NT, preferred_element_type=F32)
    )
    return info, jnp.concatenate([picked, picked], axis=1)[:8]


def pack(devices, wave, chosen, state, now, old, out_refs, pair):
    comps, points, columns = state.shape
    share = columns // devices
    wave = wave.reshape(1, 1, columns)
    forcing = RK_GAMMA * now + RK_ZETA * old
    local = state + TIME_STEP * (forcing - RK_ALPHA * (wave * state))
    rows = comps * points
    both = jnp.concatenate([state.reshape(rows, columns), local.reshape(rows, columns)], axis=0)
    high, low = two_parts(both)
    placed = lax.dot_general(jnp.concatenate([high, low], axis=0), chosen, NT, preferred_element_type=F32)
    placed = placed[: 2 * rows] + placed[2 * rows :]
    for step, out in zip(steps_of(devices, points), out_refs):
        taken = placed[:, step * share : (step + 1) * share]
        for kind in range(2):
            real = 2 * kind * points
            imag = real + points
            out[kind, pair] = jnp.concatenate([taken[real : real + points], taken[imag : imag + points]], axis=1)


def first_kernel(
    devices, me_ref, owner_hbm, modes_hbm, state_hbm, now_hbm, old_hbm, info_ref, wave_ref, *refs
):
    out_refs, (owner_ref, modes_ref, state_ref, now_ref, old_ref, sems) = refs[:devices], refs[devices:]
    columns = owner_ref.shape[1]
    copies = [
        pltpu.make_async_copy(owner_hbm, owner_ref, sems.at[0]),
        pltpu.make_async_copy(modes_hbm, modes_ref, sems.at[1]),
    ]
    for pair in range(PAIRS):
        comps = slice(2 * pair, 2 * pair + 2)
        for at, (source, target) in enumerate(((state_hbm, state_ref), (now_hbm, now_ref), (old_hbm, old_ref))):
            copies.append(
                pltpu.make_async_copy(source.at[comps], target.at[comps], sems.at[2 + 3 * pair + at])
            )
    for copy in copies:
        copy.start()
    copies[0].wait()
    copies[1].wait()
    info, wave = plan(devices, me_ref[0], owner_ref[...], modes_ref[...])
    info_ref[...] = info
    wave_ref[...] = wave
    wave = wave_row(modes_ref[...])
    chosen = selector(info[0:1], columns)
    for pair in range(PAIRS):
        for copy in copies[2 + 3 * pair : 5 + 3 * pair]:
            copy.wait()
        comps = slice(2 * pair, 2 * pair + 2)
        pack(devices, wave, chosen, state_ref[comps], now_ref[comps], old_ref[comps], out_refs, pair)


def operators_kernel(
    deriv_ref, inverse_ref, basis_ref, values_ref, high_out, low_out, both_high_out, both_low_out, basis_out, values_out
):
    high, low = two_parts(inverse_ref[...])
    high_out[...] = high
    low_out[...] = low
    both = (TIME_STEP * RK_ALPHA) * apply(jnp.concatenate([high, high, low], axis=1), deriv_ref[...])
    high, low = two_parts(both)
    both_high_out[...] = high
    both_low_out[...] = low
    high, low = two_parts(basis_ref[...])
    basis_out[...] = jnp.concatenate([high, high, low], axis=1)
    lanes = values_out.shape[1]
    values_out[...] = jnp.transpose(jnp.broadcast_to(values_ref[...], (lanes, values_ref.shape[1])))


def apply(operator, x):
    high, low = two_parts(x)
    return jnp.dot(operator, jnp.concatenate([high, low, high], axis=0), preferred_element_type=F32)


def projected(me, operators, steps, blocks, state, local):
    _, pairs, points, lanes = blocks[0].shape
    fill = LANES // points
    for at, (step, block) in enumerate(zip(steps, blocks)):
        first = at // fill * LANES
        rows = pl.ds(pl.multiple_of(first + ((me ^ step) % fill) * points, points), points)
        for pair in range(pairs):
            state[rows, pair * lanes : (pair + 1) * lanes] = block[0, pair]
            local[rows, pair * lanes : (pair + 1) * lanes] = block[1, pair]
    high, low, both_high, both_low = operators
    matrix, values = [], []
    for first in range(0, len(steps), fill):
        depth = pl.ds(pl.multiple_of((me ^ steps[first]) // fill * LANES, LANES), LANES)
        rows = slice(first // fill * LANES, (first // fill + 1) * LANES)
        for upper, lower, x in ((high, low, local), (both_high, both_low, state)):
            x_high, x_low = two_parts(x[rows, :])
            matrix += [upper[:, depth], upper[:, depth], lower[:, depth]]
            values += [x_high, x_low, x_high]
    return jnp.dot(
        jnp.concatenate(matrix, axis=1), jnp.concatenate(values, axis=0), preferred_element_type=F32
    )


def solve_early_kernel(steps, me_ref, *refs):
    operators, in_refs, (out_ref, state, local) = refs[:4], refs[4:-3], refs[-3:]
    out_ref[...] = projected(me_ref[0], operators, steps, in_refs, state, local)


def solve_late_kernel(steps, order, me_ref, wave_ref, values_ref, basis_ref, early_ref, *refs):
    operators, refs = refs[:4], refs[4:]
    in_refs, refs = refs[: len(steps)], refs[len(steps) :]
    out_refs, (solved_ref, state, local, after) = refs[:-4], refs[-4:]
    me = me_ref[0]
    pairs, points, lanes = out_refs[0].shape
    project = early_ref[...] + projected(me, operators, steps, in_refs, state, local)
    damping = 1.0 + TIME_STEP * RK_BETA * (values_ref[...] + wave_ref[0:1, :])
    project = project / jnp.concatenate([damping] * pairs, axis=1)
    after[...] = apply(basis_ref[...], project)
    for pair in range(pairs):
        solved_ref[pair] = after[:, pair * lanes : (pair + 1) * lanes]
    for step, block in zip(order, out_refs):
        rows = pl.ds(pl.multiple_of((me ^ step) * points, points), points)
        for pair in range(pairs):
            block[pair] = after[rows, pair * lanes : (pair + 1) * lanes]


def side_by_side(steps, blocks):
    pairs, _, lanes = blocks[0].shape
    share = lanes // 2
    sorted_blocks = [blocks[steps.index(step)] for step in sorted(steps)]
    rows = []
    for pair in range(pairs):
        for half in range(2):
            rows.append(
                jnp.concatenate(
                    [block[pair][:, half * share : (half + 1) * share] for block in sorted_blocks], axis=1
                )
            )
    return jnp.concatenate(rows, axis=0)


def sum_halves(x):
    rows = x.shape[0] // 2
    return x[:rows] + x[rows:]


def surplus_early_kernel(steps, info_ref, *refs):
    in_refs, (out_ref, late_ref) = refs[:-2], refs[-2:]
    columns = info_ref.shape[1]
    share = in_refs[0].shape[2] // 2
    chosen = lax.dot_general(
        selector(info_ref[0:1, :], columns), selector(info_ref[1:2, :], columns), NT, preferred_element_type=F32
    ).astype(BF16)
    devices = columns // share
    late = [step for step in range(devices) if step not in steps]
    first, last = late[0] * share, (late[-1] + 1) * share
    late_ref[...] = chosen[first:last]
    kept = jnp.concatenate([chosen[:first], chosen[last:]], axis=0)
    out_ref[...] = sum_halves(
        jnp.dot(jnp.concatenate(two_parts(side_by_side(steps, in_refs)), axis=0), kept, preferred_element_type=F32)
    )


def surplus_late_kernel(steps, order, early_ref, chosen_ref, *refs):
    in_refs, out_refs = refs[: len(steps)], refs[len(steps) :]
    pairs, points, lanes = in_refs[0].shape
    share = lanes // 2
    extra = early_ref[...] + sum_halves(
        jnp.dot(jnp.concatenate(two_parts(side_by_side(steps, in_refs)), axis=0), chosen_ref[...], preferred_element_type=F32)
    )
    for step, out in zip(order, out_refs):
        taken = extra[:, step * share : (step + 1) * share]
        for pair in range(pairs):
            real = 2 * pair * points
            imag = real + points
            out[pair] = jnp.concatenate([taken[real : real + points], taken[imag : imag + points]], axis=1)


def state_kernel(order, info_ref, modes_ref, velocity_ref, *refs):
    in_refs, (_, state_hbm, emf_ref, state_ref, sem) = refs[: len(order)], refs[len(order) :]
    comps, points, columns = state_ref.shape
    state = sum_parts(
        jnp.dot(
            three_parts(side_by_side(order, in_refs)),
            selector(info_ref[0:1, :], columns),
            preferred_element_type=F32,
        )
    )
    state_ref[...] = state.reshape(comps, points, columns)
    copy = pltpu.make_async_copy(state_ref, state_hbm, sem)
    copy.start()
    emf_ref[...] = emf_of(modes_ref[...], velocity_ref, state_ref)
    copy.wait()


def emf_of(modes, velocity_ref, state_ref):
    _, points, columns = state_ref.shape
    weight = jnp.where(modes[0:1, :] > 0, 2.0, 1.0).astype(F32)
    totals = [jnp.zeros((points, columns), F32)] * 3
    for field in range(3):
        real = weight * state_ref[2 * field]
        imag = weight * state_ref[2 * field + 1]
        for sign, i, j in ((1.0, (field + 1) % 3, (field + 2) % 3), (-1.0, (field + 2) % 3, (field + 1) % 3)):
            totals[i] = totals[i] + sign * (velocity_ref[2 * j] * real + velocity_ref[2 * j + 1] * imag)
    rows = []
    for total in totals:
        folded = total[:, :LANES]
        for at in range(1, columns // LANES):
            folded = folded + total[:, at * LANES : (at + 1) * LANES]
        rows.append(jnp.sum(jnp.transpose(folded), axis=0, keepdims=True))
    return jnp.concatenate(rows, axis=0)


def assemble(me, steps, used, solved_ref, in_refs, out_hbm, rows_ref, sems):
    pairs, points, lanes = in_refs[0].shape
    share = lanes // 2
    fill = LANES // points
    copies = []
    for first in range(0, len(steps), fill):
        depth = pl.ds(pl.multiple_of((me ^ steps[first]) // fill * LANES, LANES), LANES)
        rows = slice(first // fill * LANES, (first // fill + 1) * LANES)
        for pair in range(pairs):
            solved = solved_ref[pair, depth, :]
            for half in range(2):
                comp = 2 * pair + half
                kept = solved[:, half * share : (half + 1) * share]
                rows_ref[comp, rows, :share] = jnp.where(used < 0, 0.0, kept)
                for at in range(first, first + fill):
                    place = pl.ds(
                        pl.multiple_of(first // fill * LANES + ((me ^ steps[at]) % fill) * points, points), points
                    )
                    rows_ref[comp, place, share:] = in_refs[at][pair][:, half * share : (half + 1) * share]
                copies.append(
                    pltpu.make_async_copy(
                        rows_ref.at[comp, rows], out_hbm.at[comp, depth], sems.at[first // fill * 2 * pairs + comp]
                    )
                )
                copies[-1].start()
    for copy in copies:
        copy.wait()


def unused(info_ref, share):
    lane = lax.broadcasted_iota(jnp.int32, (LANES, share), 1)
    return jnp.where(lane < info_ref[2:3, :share], 0, -1)


def assemble_early_kernel(steps, me_ref, info_ref, solved_ref, *refs):
    in_refs, (out_hbm, rows_ref, sems) = refs[: len(steps)], refs[len(steps) :]
    share = in_refs[0].shape[2] // 2
    assemble(me_ref[0], steps, unused(info_ref, share), solved_ref, in_refs, out_hbm, rows_ref, sems)


def assemble_late_kernel(steps, terms, me_ref, info_ref, solved_ref, *refs):
    in_refs, refs = refs[: len(steps)], refs[len(steps) :]
    parts, (_, out_hbm, emf_ref, rows_ref, sems) = refs[:terms], refs[terms:]
    parts = [ref[...] for ref in parts]
    while len(parts) > 1:
        parts = [parts[at] + parts[at + 1] for at in range(0, len(parts), 2)]
    emf_ref[...] = parts[0]
    share = in_refs[0].shape[2] // 2
    assemble(me_ref[0], steps, unused(info_ref, share), solved_ref, in_refs, out_hbm, rows_ref, sems)


def near_first(steps, devices):
    return [step for step in steps if step < devices // 2] + [step for step in steps if step >= devices // 2]


def late_steps(devices, points):
    return list(range(devices // 2, devices // 2 + LANES // points))


def early_steps(devices, points):
    fill, half = LANES // points, devices // 2
    return list(range(fill)) + list(range(half + fill, devices)) + list(range(fill, half))


def steps_of(devices, points):
    return early_steps(devices, points) + late_steps(devices, points)


def exchange(blocks, steps, held=None, until=None):
    devices = len(blocks)
    arrived = {}
    for step, block in sorted(zip(steps, blocks), key=lambda pair: pair[0] == held):
        if step == held:
            block, _ = lax.optimization_barrier((block, arrived[until]))
        arrived[step] = (
            block if step == 0 else lax.ppermute(block, "col", [(i, i ^ step) for i in range(devices)])
        )
    return [arrived[step] for step in steps]


def from_groups(value):
    groups = lax.axis_size("grp")
    return [value] + [
        lax.ppermute(value, "grp", [(i, i ^ step) for i in range(groups)]) for step in range(1, groups)
    ]


def on_device(
    state_now,
    force_now,
    force_old,
    velocity,
    second_deriv,
    eig_basis,
    eig_inverse,
    eig_values,
    kept_modes,
    col_owner,
):
    comps, points, columns = state_now.shape
    devices = lax.axis_size("col")
    depth = devices * points
    share = columns // devices
    lanes = 2 * share
    width = PAIRS * lanes
    steps = steps_of(devices, points)
    early, late = early_steps(devices, points), late_steps(devices, points)
    split = len(early)
    early_rows, late_rows = split * points, len(late) * points
    back = [shaped((PAIRS, points, lanes))] * devices
    me = lax.axis_index("col").astype(jnp.int32).reshape(1)
    far = [
        pltpu.with_memory_space_constraint(array, pltpu.HBM)
        for array in (col_owner.reshape(1, columns), kept_modes, state_now, force_now, force_old)
    ]

    outs = call(
        functools.partial(first_kernel, devices),
        [shaped((8, columns), jnp.int32), shaped((8, lanes))] + [shaped((2, PAIRS, points, lanes))] * devices,
        [SCALAR] + [FAR] * 5,
        [LOCAL] * (2 + devices),
        1,
        [pltpu.VMEM((1, columns), jnp.int32), pltpu.VMEM((2, columns), jnp.int32)]
        + [pltpu.VMEM((comps, points, columns), F32)] * 3
        + [pltpu.SemaphoreType.DMA((2 + 3 * PAIRS,))],
    )(me, *far)
    info, wave = outs[:2]
    forward = exchange(outs[2:], steps)

    square = shaped((depth, depth), BF16)
    operators = call(
        operators_kernel,
        [square] * 4 + [shaped((depth, 3 * depth), BF16), shaped((depth, lanes))],
        [LOCAL] * 4,
        [LOCAL] * 6,
        HEAVY,
    )(second_deriv, eig_inverse, eig_basis, eig_values.reshape(1, depth))
    basis, values = operators[4:]

    begun = call(
        functools.partial(solve_early_kernel, early),
        shaped((depth, width)),
        [SCALAR] + [LOCAL] * (4 + split),
        LOCAL,
        HEAVY,
        [pltpu.VMEM((early_rows, width), F32)] * 2,
    )(me, *operators[:4], *forward[:split])
    outs = call(
        functools.partial(solve_late_kernel, late, steps),
        back + [shaped((PAIRS, depth, lanes))],
        [SCALAR] + [LOCAL] * (8 + len(late)),
        [LOCAL] * (devices + 1),
        1,
        [pltpu.VMEM((late_rows, width), F32)] * 2 + [pltpu.VMEM((depth, width), F32)],
    )(me, wave, values, basis, begun, *operators[:4], *forward[split:])
    solved = outs[devices]
    returned = exchange(outs[:devices], steps)

    begun, chosen = call(
        functools.partial(surplus_early_kernel, early),
        [shaped((comps * points, columns)), shaped((len(late) * share, columns), BF16)],
        [LOCAL] * (1 + split),
        [LOCAL] * 2,
        HEAVY,
    )(info, *returned[:split])
    outs = call(
        functools.partial(surplus_late_kernel, late, steps),
        back,
        [LOCAL] * (2 + len(late)),
        [LOCAL] * devices,
        1,
    )(begun, chosen, *returned[split:])
    extra = exchange(outs, steps, 2, 1)

    state_next, emf = call(
        functools.partial(state_kernel, steps),
        [shaped(state_now.shape), shaped((3, points))],
        [LOCAL] * (3 + devices) + [ANYWHERE],
        [FAR, LOCAL],
        HEAVY,
        [pltpu.VMEM(state_now.shape, F32), pltpu.SemaphoreType.DMA],
    )(info, kept_modes, velocity, *returned, extra[early.index(1)])
    terms = from_groups(emf)

    owned = call(
        functools.partial(assemble_early_kernel, early),
        shaped((comps, depth, lanes)),
        [SCALAR] + [LOCAL] * (2 + split),
        FAR,
        HEAVY,
        [
            pltpu.VMEM((comps, early_rows, lanes), F32),
            pltpu.SemaphoreType.DMA((comps * early_rows // LANES,)),
        ],
    )(me, info, solved, *extra[:split])
    owned, mean_emf = call(
        functools.partial(assemble_late_kernel, late, len(terms)),
        [shaped((comps, depth, lanes)), shaped((3, points))],
        [SCALAR] + [LOCAL] * (2 + len(late) + len(terms)) + [FAR],
        [FAR, LOCAL],
        1,
        [pltpu.VMEM((comps, late_rows, lanes), F32), pltpu.SemaphoreType.DMA((comps,))],
        aliases={3 + len(late) + len(terms): 0},
    )(me, info, solved, *extra[split:], *terms, owned)
    return (state_next, owned, mean_emf)


def solution(mesh):
    return jax.shard_map(
        on_device,
        mesh=mesh,
        in_specs=(
            P(None, "col", "grp"),
            P(None, "col", "grp"),
            P(None, "col", "grp"),
            P(None, "col", "grp"),
            P(),
            P(),
            P(),
            P(),
            P(None, "grp"),
            P("grp", None),
        ),
        out_specs=(P(None, "col", "grp"), P(None, None, ("grp", "col")), P(None, "col")),
        check_vma=False,
    )
```
